32 devices in a mesh: dp: 4 (over x, core), table: 8 (over z, y).
Axes of the slice: x: 2, y: 2, z: 4, core: 2. Of those that a mesh axis runs over, the one named last changes fastest.
Arguments:
- features: bfloat16 [4096, 2048], P(('dp', 'table')), may hold values from -6 to 6
- w_first: bfloat16 [2048, 1024], replicated, may hold values from -0.125 to 0.125
- b_first: float32 [1024], replicated, may hold values from -4 to 4
- grad_out: bfloat16 [4096, 1024], P(('dp', 'table')), may hold values from -6 to 6
- admit: int32 [4096, 16], P(('dp', 'table')), may hold values from 0 to 1, as said below
- owner: int32 [4096, 16, 1], P(('dp', 'table')), may hold values from 0 to 3, as said below
- adm_row: int32 [4096, 16], P(('dp', 'table')), may hold values from 0 to 1023
- q_shard: int32 [4096, 16, 1], P(('dp', 'table')), may hold values from 0 to 31, as said below
- q_local: int32 [4096, 16], P(('dp', 'table')), may hold values from 0 to 4095
- r_shard: int32 [4096, 16, 1], P(('dp', 'table')), may hold values from 0 to 31, as said below
- r_local: int32 [4096, 16], P(('dp', 'table')), may hold values from 0 to 4095
Outputs:
- w_grad: float32 [2048, 1024], replicated
- b_grad: float32 [1024], replicated
- adm_grad: float32 [4096, 128], P(('dp', 'table'))
- q_grad: float32 [131072, 128], P(('dp', 'table'))
- r_grad: float32 [131072, 128], P(('dp', 'table'))
The draws below stay inside these ranges and needn't reach their ends.
Inputs may be any that keep to these rules, and one draw needn't show every extreme that they name: `admit`: on some device every lookup is admitted, and on another device none is. Among the 2048 lookups of one device no owner is named more than 768 times, and on every device some owner exactly 768 times. `q_shard`: among the 2048 lookups of one device no block is named more than 96 times, and on every device some block exactly 96 times. `r_shard`: among the 2048 lookups of one device no block is named more than 96 times, and on every device some block exactly 96 times.
All inputs are finite; a program needn't handle non-finite values.
Results may differ from the reference program's by a relative error of at most 0.0055.
Values may be sent and summed in bfloat16 or wider, within the bound.
No kernel may reach another device: no remote copies, remote signals or barrier semaphores. Data moves between devices by JAX's collectives and lax.ppermute only.
A program may use at most 128 MiB of HBM per device.

```python
import jax
import jax.numpy as jnp
from jax import lax

F = 16
E = 128
H = 1024
B_DEV = 128
QROWS_DEV = 4096
SAMPLES = 4096
ADM_ROWS = 4096
ADM_OWN = 1024
QROWS = 131072
CAP = 768
QCAP = 96
N_DP = 4
DEVICES = 32


def routed_labels(key, n_dest, most):
    count = B_DEV * F
    spare = count - most
    others = max(n_dest - 1, 1)
    base = spare // others
    reach = max(0, min((most - (spare + others - 1) // others) // 2, base // 2))

    def one_device(dev_key):
        key_one, key_two, key_cut, key_perm = jax.random.split(dev_key, 4)
        first = jax.random.randint(key_one, (), 0, n_dest)
        second = jax.random.randint(key_two, (), 0, n_dest)
        hottest = jnp.minimum(first, second).astype(jnp.int32)
        inner = jnp.arange(1, others, dtype=jnp.int32)
        jitter = jax.random.randint(key_cut, (others - 1,), -reach, reach + 1)
        cuts = (inner * spare // others + jitter).astype(jnp.int32)
        places = jnp.arange(count, dtype=jnp.int32)
        offset = places - most
        region = jnp.sum((offset[:, None] >= cuts[None, :]).astype(jnp.int32), axis=1)
        labels = jnp.where(places < most, hottest, (hottest + 1 + region) % n_dest).astype(jnp.int32)
        order = jax.random.permutation(key_perm, count)
        return labels[order]
    device_keys = jax.random.split(key, DEVICES)
    result = lax.map(one_device, device_keys)
    return result.reshape(SAMPLES, F, 1).astype(jnp.int32)


def draw_owner(key, part):
    return routed_labels(jax.random.fold_in(key, 11), N_DP, CAP)


def draw_q_shard(key, part):
    return routed_labels(jax.random.fold_in(key, 12), DEVICES, QCAP)


def draw_r_shard(key, part):
    return routed_labels(jax.random.fold_in(key, 13), DEVICES, QCAP)


def draw_admit(key, part):
    base_key = jax.random.fold_in(key, 14)
    key_full, key_empty, key_coin = jax.random.split(base_key, 3)
    full_dev = jax.random.randint(key_full, (), 0, DEVICES)
    empty_dev = (full_dev + 1 + jax.random.randint(key_empty, (), 0, DEVICES - 1)) % DEVICES
    coins = jax.random.randint(key_coin, (DEVICES, B_DEV * F), 0, 2)
    device_ids = jnp.arange(DEVICES, dtype=jnp.int32)[:, None]
    marks = jnp.where(device_ids == full_dev, 1, jnp.where(device_ids == empty_dev, 0, coins))
    return marks.reshape(SAMPLES, F).astype(jnp.int32)


def with_ends(entries, stream_key, low, top_value):
    index_at = [jax.random.randint(jax.random.fold_in(stream_key, axis), (), 0, length) for axis, length in enumerate(entries.shape)]
    widest = entries.shape.index(max(entries.shape))
    beside = index_at[:widest] + [(index_at[widest] + 1) % entries.shape[widest]] + index_at[widest + 1:]
    return entries.at[tuple(index_at)].set(low).at[tuple(beside)].set(top_value)


def levels(key, extent, shards, low, top_value):
    level, own = 1.0, jax.random.fold_in(key, 6)
    for dim, blocks in shards:
        steps = jnp.exp(jax.random.uniform(jax.random.fold_in(own, dim), (blocks,), jnp.float32, low / len(shards), top_value / len(shards)))
        level = level * jnp.repeat(steps, extent[dim] // blocks).reshape([-1 if axis == dim else 1 for axis in range(len(extent))])
    return level


def noise(key, shape, deviation, most, cuts=(), held_as=jnp.bfloat16):
    values = jax.random.normal(key, shape, jnp.float32) * deviation
    if len(cuts) > 0:
        values = levels(key, shape, cuts, -0.22, 0.18) * values
    return jnp.clip(values, min=-most, max=most).astype(held_as)


def setup_inputs(seed: int = 0) -> dict:
    streams_of = jax.random.split(jax.random.key(seed), 12)
    features = noise(streams_of[0], (SAMPLES, F * E), 1.0, 6.0, ((0, 32),))
    w_first = noise(streams_of[1], (F * E, H), (F * E) ** -0.5, 0.125)
    b_first = noise(streams_of[2], (H,), 1.0, 4.0, (), jnp.float32)
    grad_out = noise(streams_of[3], (SAMPLES, H), 1.0, 6.0, ((0, 32),))
    admit = draw_admit(jax.random.fold_in(streams_of[11], 71), 0)
    owner = draw_owner(jax.random.fold_in(streams_of[11], 71), 0)
    adm_row = with_ends(jax.random.randint(streams_of[6], (SAMPLES, F), 0, ADM_OWN), jax.random.fold_in(streams_of[6], 1), 0, ADM_OWN - 1).astype(jnp.int32)
    q_shard = draw_q_shard(jax.random.fold_in(streams_of[11], 71), 0)
    q_local = with_ends(jax.random.randint(streams_of[8], (SAMPLES, F), 0, QROWS_DEV), jax.random.fold_in(streams_of[8], 1), 0, QROWS_DEV - 1).astype(jnp.int32)
    r_shard = draw_r_shard(jax.random.fold_in(streams_of[11], 71), 0)
    r_local = with_ends(jax.random.randint(streams_of[10], (SAMPLES, F), 0, QROWS_DEV), jax.random.fold_in(streams_of[10], 1), 0, QROWS_DEV - 1).astype(jnp.int32)
    return {"features": features, "w_first": w_first, "b_first": b_first, "grad_out": grad_out, "admit": admit, "owner": owner, "adm_row": adm_row, "q_shard": q_shard, "q_local": q_local, "r_shard": r_shard, "r_local": r_local}


def reference(features, w_first, b_first, grad_out, admit, owner, adm_row, q_shard, q_local, r_shard, r_local):
    pre = jnp.dot(features, w_first, preferred_element_type=jnp.float32) + b_first
    sig = jax.nn.sigmoid(pre)
    dpre = (grad_out.astype(jnp.float32) * sig * (1.0 + pre * (1.0 - sig))).astype(jnp.bfloat16)
    w_grad = jnp.dot(features.T, dpre, preferred_element_type=jnp.float32)
    b_grad = jnp.sum(dpre.astype(jnp.float32), axis=0)
    lookup = lax.dot_general(dpre, w_first, (((1,), (1,)), ((), ())), preferred_element_type=jnp.float32).astype(jnp.bfloat16)
    values = lookup.reshape(-1, E).astype(jnp.float32)
    flag = admit.reshape(-1)
    rows = (owner.reshape(-1) * ADM_OWN + adm_row.reshape(-1)).astype(jnp.int32)
    rows = jnp.where(flag == 1, rows, ADM_ROWS).astype(jnp.int32)
    adm_grad = jax.ops.segment_sum(values, rows, ADM_ROWS + 1)[:ADM_ROWS]
    qrows = (q_shard.reshape(-1) * QROWS_DEV + q_local.reshape(-1)).astype(jnp.int32)
    rrows = (r_shard.reshape(-1) * QROWS_DEV + r_local.reshape(-1)).astype(jnp.int32)
    qrows = jnp.where(flag == 0, qrows, QROWS).astype(jnp.int32)
    rrows = jnp.where(flag == 0, rrows, QROWS).astype(jnp.int32)
    q_grad = jax.ops.segment_sum(values, qrows, QROWS + 1)[:QROWS]
    r_grad = jax.ops.segment_sum(values, rrows, QROWS + 1)[:QROWS]
    return (w_grad, b_grad, adm_grad, q_grad, r_grad)
```

```python
import functools

import jax
import jax.numpy as jnp
from jax import lax
from jax.experimental import pallas as pl
from jax.experimental.pallas import tpu as pltpu
from jax.sharding import Mesh, PartitionSpec as P

E = 128
ADM_DEV = 128
QROWS_DEV = 4096
N_Z = 4
GROUPS = 4
VMEM_LIMIT = 48 * 1024 * 1024
BF = jnp.bfloat16
F32 = jnp.float32


def iota(shape, dim):
    return lax.broadcasted_iota(jnp.int32, shape, dim)


def dot(a, b, dims=((1,), (0,))):
    return lax.dot_general(a, b, (dims, ((), ())), preferred_element_type=F32)


def slots_kernel(n_dest, cap, dq_ref, lq_ref, dr_ref, lr_ref, row_ref, slot_ref, labels_ref):
    n_rows, n_feat = dq_ref.shape
    n_s = n_rows // N_Z
    sample = iota((n_s, n_s), 0)
    earlier = (sample < iota((n_s, n_s), 1)).astype(F32).astype(BF)
    ones = jnp.ones((n_s, n_s), BF)
    count = n_dest * n_feat
    at_row, at_col = iota((count, count), 0), iota((count, count), 1)
    before = ((at_row // n_feat == at_col // n_feat) & (at_col < at_row)).astype(F32).astype(BF)
    for table, ref in enumerate((dq_ref, dr_ref)):
        across = ref[...].astype(F32).T
        for z in range(N_Z):
            dest = across[:, z * n_s : (z + 1) * n_s]
            hits = jnp.concatenate([jnp.where(dest == d, 1.0, 0.0) for d in range(n_dest)], axis=0)
            hits_bf = hits.astype(BF)
            rank = dot(hits_bf, earlier) + dot(before, dot(hits_bf, ones).astype(BF))
            rank = rank * hits
            total = rank[0:n_feat, :]
            for d in range(1, n_dest):
                total = total + rank[d * n_feat : (d + 1) * n_feat, :]
            slot = jnp.where(dest >= 0, dest * cap + total, -1.0)
            slot_ref[table, z, :, :] = slot.astype(jnp.int32)
    across = row_ref[...].astype(F32).T.astype(jnp.int32)
    for z in range(N_Z):
        slot_ref[2, z, :, :] = across[:, z * n_s : (z + 1) * n_s]
    lane = iota((n_s, E), 1) % 4
    for z in range(N_Z):
        lq, lr = lq_ref[z * n_s : (z + 1) * n_s, :], lr_ref[z * n_s : (z + 1) * n_s, :]
        for f in range(n_feat):
            q, r = lq[:, f : f + 1], lr[:, f : f + 1]
            one = jnp.where(lane < 2, q, r)
            one = jnp.where(lane % 2 == 0, one >> 8, one & 255)
            labels_ref[z, f * n_s : (f + 1) * n_s, :] = one.astype(F32).astype(BF)


def bucket_kernel(
    n_dest, cap, d_ref, w_ref, slot_ref, labels_ref, out_ref, v_ref, mark_ref
):
    n_rows, depth = d_ref.shape
    n_s = n_rows // N_Z
    n_feat = w_ref.shape[0] // E
    look = n_feat * n_s
    seg = N_Z * cap
    n_mark = -(-seg // E)

    def lookups(step, carry):
        wide = 2 * E
        start = pl.multiple_of(step * wide, wide)
        res = dot(d_ref[...], w_ref[pl.ds(start, wide), :], ((1,), (1,))).astype(BF)
        for z in range(N_Z):
            for h in range(2):
                row = pl.multiple_of((step * 2 + h) * n_s, n_s)
                v_ref[z, pl.ds(row, n_s), 0:E] = res[z * n_s : (z + 1) * n_s, h * E : (h + 1) * E]
        return carry

    lax.fori_loop(0, n_feat // 2, lookups, 0)
    for z in range(N_Z):
        v_ref[z, :, E : 2 * E] = labels_ref[z]

    def picked(which, z, base, n):
        wanted = iota((n, n_s), 0) + base
        parts = [
            jnp.where(wanted == slot_ref[which, z, f : f + 1, :], 1.0, 0.0).astype(BF)
            for f in range(n_feat)
        ]
        return jnp.concatenate(parts, axis=1)

    per = 4
    for which in range(2):
        for z in range(N_Z):

            def fill(block, carry):
                o = dot(picked(which, z, block * (per * cap), per * cap), v_ref[z])
                for g in range(per):
                    d = block * per + g
                    rows = o[g * cap : (g + 1) * cap, :]
                    out_ref[d, which * seg + z * cap : which * seg + (z + 1) * cap, :] = rows[:, 0:E].astype(BF)
                    mark_ref[which, d, z * cap : (z + 1) * cap, :] = rows[:, E : 2 * E]
                return carry

            lax.fori_loop(0, n_dest // per, fill, 0)

    def admitted(block, carry):
        o = jnp.zeros((per * ADM_DEV, E), F32)
        for z in range(N_Z):
            o = o + dot(picked(2, z, block * (per * ADM_DEV), per * ADM_DEV), v_ref[z, :, 0:E])
        for g in range(per):
            out_ref[block * per + g, 2 * seg : 2 * seg + ADM_DEV, :] = o[
                g * ADM_DEV : (g + 1) * ADM_DEV, :
            ].astype(BF)
        return carry

    lax.fori_loop(0, n_dest // per, admitted, 0)

    bias = jnp.sum(d_ref[...].astype(F32), axis=0, keepdims=True)
    high = bias.astype(BF)
    low = (bias - high.astype(F32)).astype(BF)
    n_bias = depth // E
    bias_rows = jnp.concatenate(
        [part[:, i * E : (i + 1) * E].astype(F32) for part in (high, low) for i in range(n_bias)], axis=0
    ).astype(BF)
    at_mark = 2 * seg + ADM_DEV

    def finish(d, carry):
        lane = iota((seg, E), 1) % 4
        mixed = jnp.where(lane < 2, mark_ref[0, d], mark_ref[1, d])
        if seg % E:
            mixed = jnp.concatenate([mixed, jnp.zeros((n_mark * E - seg, E), F32)], axis=0)
        rows = iota((16, E), 0) // 4
        marks = jnp.zeros((16, E), F32)
        for j in range(n_mark):
            across = mixed[j * E : (j + 1) * E, :].T
            marks = jnp.where(rows == j, across[0:16, :], marks)
        out_ref[d, at_mark : at_mark + 16, :] = marks.astype(BF)
        out_ref[d, at_mark + 16 : at_mark + 16 + 2 * n_bias, :] = bias_rows
        return carry

    lax.fori_loop(0, n_dest, finish, 0)


def sums_kernel(n_src, seg, n_bias, in_ref, bias_ref, adm_ref, q_ref, r_ref, v_ref, row_ref):
    n_mark = -(-seg // E)
    at_mark = 2 * seg + ADM_DEV
    adm = jnp.zeros((ADM_DEV, E), F32)
    bias = jnp.zeros((2 * n_bias, E), F32)
    for s in range(n_src):
        adm = adm + in_ref[s, 2 * seg : at_mark, :].astype(F32)
        bias = bias + in_ref[s, at_mark + 16 : at_mark + 16 + 2 * n_bias, :].astype(F32)
    adm_ref[...] = adm
    bias_ref[...] = bias[0:n_bias, :] + bias[n_bias:, :]

    per_group = QROWS_DEV // GROUPS
    tall = n_mark * E
    for table, out in enumerate((q_ref, r_ref)):
        for s in range(n_src):
            marks = in_ref[s, at_mark : at_mark + 16, :].astype(F32)
            down = jnp.concatenate([marks, jnp.zeros((E - 16, E), F32)], axis=0).T
            for j in range(n_mark):
                at = j * 4 + table * 2
                label = marks[at : at + 1, :] * 256.0 + marks[at + 1 : at + 2, :]
                label = label.astype(jnp.int32) % per_group
                if (j + 1) * E > seg:
                    label = jnp.where(iota((1, E), 1) + j * E < seg, label, -1)
                k = s * n_mark + j
                row_ref[k : k + 1, :] = label
                group = (down[:, at : at + 1] * 256.0 + down[:, at + 1 : at + 2]).astype(jnp.int32) // per_group
                rows = in_ref[s, table * seg + j * E : table * seg + (j + 1) * E, :]
                for g in range(GROUPS):
                    v_ref[k * E : (k + 1) * E, g * E : (g + 1) * E] = jnp.where(
                        group == g, rows.astype(F32), 0.0
                    ).astype(BF)
        block = 256

        def add_up(b, carry):
            wanted = iota((block, E), 0) + b * block
            hits = jnp.concatenate(
                [
                    jnp.where(wanted == row_ref[k : k + 1, :], 1.0, 0.0).astype(BF)
                    for k in range(n_src * n_mark)
                ],
                axis=1,
            )
            o = dot(hits, v_ref[...])
            for g in range(GROUPS):
                start = pl.multiple_of(g * per_group + b * block, block)
                out[pl.ds(start, block), :] = o[:, g * E : (g + 1) * E]
            return carry

        lax.fori_loop(0, per_group // block, add_up, 0)


def local(
    features, w_first, b_first, grad_out, admit, owner, adm_row, q_shard, q_local, r_shard, r_local
):
    n_dp = lax.axis_size("dp")
    n_y = lax.axis_size("ty")
    n_table = N_Z * n_y
    n_dev = n_dp * n_table
    n_plane = n_dp * n_y
    n_s, width = features.shape
    hidden = w_first.shape[1]
    n_feat = width // E
    count = n_s * n_feat
    cap = max(2, 3 * count // (2 * n_dev))
    seg = N_Z * cap
    n_bias = hidden // E
    my_z = lax.axis_index("tz")

    plain = admit == 0
    codes = jnp.stack(
        [
            jnp.where(plain, q_shard[:, :, 0] * QROWS_DEV + q_local, -1),
            jnp.where(plain, r_shard[:, :, 0] * QROWS_DEV + r_local, -1),
            jnp.where(admit == 1, owner[:, :, 0] * (ADM_DEV * n_table) + adm_row, -1),
        ]
    )
    codes = lax.all_to_all(
        jnp.broadcast_to(codes[None], (N_Z,) + codes.shape), "tz", split_axis=0, concat_axis=0, tiled=True
    )
    share = width // n_dev * n_y
    cut = features.reshape(n_s, n_dp, N_Z, share).transpose(2, 0, 1, 3).reshape(N_Z, n_s, n_dp * share)
    feat_in = lax.all_to_all(cut, "tz", split_axis=0, concat_axis=0, tiled=True)
    feat_in = feat_in.reshape(N_Z * n_s, n_dp * share)

    pre = jnp.dot(features, w_first, preferred_element_type=F32) + b_first
    sig = jax.nn.sigmoid(pre)
    dpre = (grad_out.astype(F32) * sig * (1.0 + pre * (1.0 - sig))).astype(BF)
    dpre = lax.all_to_all(
        jnp.broadcast_to(dpre[None], (N_Z,) + dpre.shape), "tz", split_axis=0, concat_axis=0, tiled=True
    ).reshape(N_Z * n_s, hidden)

    def in_plane(code, block):
        dev = code // block
        table = dev % n_table
        here = (code >= 0) & (table // n_y == my_z)
        return jnp.where(here, dev // n_table * n_y + table % n_y, -1), code % block

    rows = [codes[:, i].reshape(N_Z * n_s, n_feat) for i in range(3)]
    dq, lq = in_plane(rows[0], QROWS_DEV)
    dr, lr = in_plane(rows[1], QROWS_DEV)
    da, la = in_plane(rows[2], ADM_DEV)
    arow = jnp.where(da >= 0, da * ADM_DEV + la, -1)
    slots, labels = pl.pallas_call(
        functools.partial(slots_kernel, n_plane, cap),
        out_shape=(
            jax.ShapeDtypeStruct((3, N_Z, n_feat, n_s), jnp.int32),
            jax.ShapeDtypeStruct((N_Z, count, E), BF),
        ),
        compiler_params=pltpu.CompilerParams(vmem_limit_bytes=VMEM_LIMIT),
        cost_estimate=pl.CostEstimate(flops=10**9, bytes_accessed=3 * 10**6, transcendentals=0),
        name="slots",
    )(dq, lq, dr, lr, arow)

    w_part = lax.dot_general(feat_in, dpre, (((0,), (0,)), ((), ())), preferred_element_type=F32).astype(BF)
    w_part = lax.all_to_all(
        w_part.reshape(n_plane, width // n_dev, hidden), ("dp", "ty"), split_axis=0, concat_axis=0, tiled=True
    )

    n_rows = 2 * seg + ADM_DEV + 16 + 2 * n_bias
    chunks = pl.pallas_call(
        functools.partial(bucket_kernel, n_plane, cap),
        out_shape=jax.ShapeDtypeStruct((n_plane, n_rows, E), BF),
        scratch_shapes=[
            pltpu.VMEM((N_Z, count, 2 * E), BF),
            pltpu.VMEM((2, n_plane, seg, E), F32),
        ],
        compiler_params=pltpu.CompilerParams(vmem_limit_bytes=VMEM_LIMIT),
        cost_estimate=pl.CostEstimate(flops=13 * 10**9, bytes_accessed=10**7, transcendentals=0),
        name="buckets",
    )(dpre, w_first, slots, labels)
    chunks = lax.all_to_all(chunks, ("dp", "ty"), split_axis=0, concat_axis=0, tiled=True)

    w_own = jnp.sum(w_part.astype(F32), axis=0).astype(BF)
    w_all = lax.all_gather(w_own, ("dp", "tz", "ty"), axis=0, tiled=True)

    n_tall = n_plane * -(-seg // E)
    b_grad, adm_grad, q_grad, r_grad = pl.pallas_call(
        functools.partial(sums_kernel, n_plane, seg, n_bias),
        out_shape=(
            jax.ShapeDtypeStruct((n_bias, E), F32),
            jax.ShapeDtypeStruct((ADM_DEV, E), F32),
            jax.ShapeDtypeStruct((QROWS_DEV, E), F32),
            jax.ShapeDtypeStruct((QROWS_DEV, E), F32),
        ),
        scratch_shapes=[
            pltpu.VMEM((n_tall * E, GROUPS * E), BF),
            pltpu.VMEM((-(-n_tall // 8) * 8, E), jnp.int32),
        ],
        compiler_params=pltpu.CompilerParams(vmem_limit_bytes=VMEM_LIMIT),
        cost_estimate=pl.CostEstimate(flops=7 * 10**9, bytes_accessed=7 * 10**6, transcendentals=0),
        name="sums",
    )(chunks)
    return (w_all.astype(F32), b_grad.reshape(hidden), adm_grad, q_grad, r_grad)


def solution(mesh):
    n_dp, n_table = mesh.devices.shape
    fine = Mesh(mesh.devices.reshape(n_dp, N_Z, n_table // N_Z), ("dp", "tz", "ty"))
    every = ("dp", "tz", "ty")
    two, three = P(every, None), P(every, None, None)
    in_specs = (two, P(), P(), two, two, three, two, three, two, three, two)
    out_specs = (P(), P(), two, two, two)
    return jax.shard_map(local, mesh=fine, in_specs=in_specs, out_specs=out_specs, check_vma=False)
```

```python
import functools

import jax
import jax.numpy as jnp
from jax import lax
from jax.experimental import pallas as pl
from jax.experimental.pallas import tpu as pltpu
from jax.sharding import Mesh, PartitionSpec as P

E = 128
ADM_DEV = 128
QROWS_DEV = 4096
N_Z = 4
GROUPS = 4
VMEM_LIMIT = 48 * 1024 * 1024
BF = jnp.bfloat16
F32 = jnp.float32


def iota(shape, dim):
    return lax.broadcasted_iota(jnp.int32, shape, dim)


def dot(a, b, dims=((1,), (0,))):
    return lax.dot_general(a, b, (dims, ((), ())), preferred_element_type=F32)


def slots_kernel(n_dest, cap, dq_ref, lq_ref, dr_ref, lr_ref, row_ref, slot_ref, labels_ref):
    n_rows, n_feat = dq_ref.shape
    n_s = n_rows // N_Z
    sample = iota((n_s, n_s), 0)
    earlier = (sample < iota((n_s, n_s), 1)).astype(F32).astype(BF)
    ones = jnp.ones((n_s, n_s), BF)
    count = n_dest * n_feat
    at_row, at_col = iota((count, count), 0), iota((count, count), 1)
    before = ((at_row // n_feat == at_col // n_feat) & (at_col < at_row)).astype(F32).astype(BF)
    for table, ref in enumerate((dq_ref, dr_ref)):
        across = ref[...].astype(F32).T
        for z in range(N_Z):
            dest = across[:, z * n_s : (z + 1) * n_s]
            hits = jnp.concatenate([jnp.where(dest == d, 1.0, 0.0) for d in range(n_dest)], axis=0)
            hits_bf = hits.astype(BF)
            rank = dot(hits_bf, earlier) + dot(before, dot(hits_bf, ones).astype(BF))
            rank = rank * hits
            total = rank[0:n_feat, :]
            for d in range(1, n_dest):
                total = total + rank[d * n_feat : (d + 1) * n_feat, :]
            slot = jnp.where(dest >= 0, dest * cap + total, -1.0)
            slot_ref[table, z, :, :] = slot.astype(jnp.int32)
    across = row_ref[...].astype(F32).T.astype(jnp.int32)
    for z in range(N_Z):
        slot_ref[2, z, :, :] = across[:, z * n_s : (z + 1) * n_s]
    lane = iota((n_s, E), 1) % 4
    for z in range(N_Z):
        lq, lr = lq_ref[z * n_s : (z + 1) * n_s, :], lr_ref[z * n_s : (z + 1) * n_s, :]
        for f in range(n_feat):
            q, r = lq[:, f : f + 1], lr[:, f : f + 1]
            one = jnp.where(lane < 2, q, r)
            one = jnp.where(lane % 2 == 0, one >> 8, one & 255)
            labels_ref[z, f * n_s : (f + 1) * n_s, :] = one.astype(F32).astype(BF)


def bucket_kernel(
    n_dest, cap, d_ref, w_ref, slot_ref, labels_ref, out_ref, v_ref, mark_ref
):
    n_rows, depth = d_ref.shape
    n_s = n_rows // N_Z
    n_feat = w_ref.shape[0] // E
    look = n_feat * n_s
    seg = N_Z * cap
    n_mark = -(-seg // E)

    def lookups(step, carry):
        wide = 2 * E
        start = pl.multiple_of(step * wide, wide)
        res = dot(d_ref[...], w_ref[pl.ds(start, wide), :], ((1,), (1,))).astype(BF)
        for z in range(N_Z):
            for h in range(2):
                row = pl.multiple_of((step * 2 + h) * n_s, n_s)
                v_ref[z, pl.ds(row, n_s), 0:E] = res[z * n_s : (z + 1) * n_s, h * E : (h + 1) * E]
        return carry

    lax.fori_loop(0, n_feat // 2, lookups, 0)
    for z in range(N_Z):
        v_ref[z, :, E : 2 * E] = labels_ref[z]

    def picked(which, z, base, n):
        wanted = iota((n, n_s), 0) + base
        parts = [
            jnp.where(wanted == slot_ref[which, z, f : f + 1, :], 1.0, 0.0).astype(BF)
            for f in range(n_feat)
        ]
        return jnp.concatenate(parts, axis=1)

    per = 4
    for which in range(2):
        for z in range(N_Z):

            def fill(block, carry):
                o = dot(picked(which, z, block * (per * cap), per * cap), v_ref[z])
                for g in range(per):
                    d = block * per + g
                    rows = o[g * cap : (g + 1) * cap, :]
                    out_ref[d, which * seg + z * cap : which * seg + (z + 1) * cap, :] = rows[:, 0:E].astype(BF)
                    mark_ref[which, d, z * cap : (z + 1) * cap, :] = rows[:, E : 2 * E]
                return carry

            lax.fori_loop(0, n_dest // per, fill, 0)

    def admitted(block, carry):
        o = jnp.zeros((per * ADM_DEV, E), F32)
        for z in range(N_Z):
            o = o + dot(picked(2, z, block * (per * ADM_DEV), per * ADM_DEV), v_ref[z, :, 0:E])
        for g in range(per):
            out_ref[block * per + g, 2 * seg : 2 * seg + ADM_DEV, :] = o[
                g * ADM_DEV : (g + 1) * ADM_DEV, :
            ].astype(BF)
        return carry

    lax.fori_loop(0, n_dest // per, admitted, 0)

    bias = jnp.sum(d_ref[...].astype(F32), axis=0, keepdims=True)
    high = bias.astype(BF)
    low = (bias - high.astype(F32)).astype(BF)
    n_bias = depth // E
    bias_rows = jnp.concatenate(
        [part[:, i * E : (i + 1) * E].astype(F32) for part in (high, low) for i in range(n_bias)], axis=0
    ).astype(BF)
    at_mark = 2 * seg + ADM_DEV

    def finish(d, carry):
        lane = iota((seg, E), 1) % 4
        mixed = jnp.where(lane < 2, mark_ref[0, d], mark_ref[1, d])
        if seg % E:
            mixed = jnp.concatenate([mixed, jnp.zeros((n_mark * E - seg, E), F32)], axis=0)
        rows = iota((16, E), 0) // 4
        marks = jnp.zeros((16, E), F32)
        for j in range(n_mark):
            across = mixed[j * E : (j + 1) * E, :].T
            marks = jnp.where(rows == j, across[0:16, :], marks)
        out_ref[d, at_mark : at_mark + 16, :] = marks.astype(BF)
        out_ref[d, at_mark + 16 : at_mark + 16 + 2 * n_bias, :] = bias_rows
        return carry

    lax.fori_loop(0, n_dest, finish, 0)


def sums_kernel(n_src, seg, n_bias, in_ref, bias_ref, adm_ref, q_ref, r_ref, v_ref, row_ref):
    n_mark = -(-seg // E)
    at_mark = 2 * seg + ADM_DEV
    adm = jnp.zeros((ADM_DEV, E), F32)
    bias = jnp.zeros((2 * n_bias, E), F32)
    for s in range(n_src):
        adm = adm + in_ref[s, 2 * seg : at_mark, :].astype(F32)
        bias = bias + in_ref[s, at_mark + 16 : at_mark + 16 + 2 * n_bias, :].astype(F32)
    adm_ref[...] = adm
    bias_ref[...] = bias[0:n_bias, :] + bias[n_bias:, :]

    per_group = QROWS_DEV // GROUPS
    tall = n_mark * E
    for table, out in enumerate((q_ref, r_ref)):
        for s in range(n_src):
            marks = in_ref[s, at_mark : at_mark + 16, :].astype(F32)
            down = jnp.concatenate([marks, jnp.zeros((E - 16, E), F32)], axis=0).T
            for j in range(n_mark):
                at = j * 4 + table * 2
                label = marks[at : at + 1, :] * 256.0 + marks[at + 1 : at + 2, :]
                label = label.astype(jnp.int32) % per_group
                if (j + 1) * E > seg:
                    label = jnp.where(iota((1, E), 1) + j * E < seg, label, -1)
                k = s * n_mark + j
                row_ref[k : k + 1, :] = label
                group = (down[:, at : at + 1] * 256.0 + down[:, at + 1 : at + 2]).astype(jnp.int32) // per_group
                rows = in_ref[s, table * seg + j * E : table * seg + (j + 1) * E, :]
                for g in range(GROUPS):
                    v_ref[k * E : (k + 1) * E, g * E : (g + 1) * E] = jnp.where(
                        group == g, rows.astype(F32), 0.0
                    ).astype(BF)
        block = 256

        def add_up(b, carry):
            wanted = iota((block, E), 0) + b * block
            hits = jnp.concatenate(
                [
                    jnp.where(wanted == row_ref[k : k + 1, :], 1.0, 0.0).astype(BF)
                    for k in range(n_src * n_mark)
                ],
                axis=1,
            )
            o = dot(hits, v_ref[...])
            for g in range(GROUPS):
                start = pl.multiple_of(g * per_group + b * block, block)
                out[pl.ds(start, block), :] = o[:, g * E : (g + 1) * E]
            return carry

        lax.fori_loop(0, per_group // block, add_up, 0)


def local(
    features, w_first, b_first, grad_out, admit, owner, adm_row, q_shard, q_local, r_shard, r_local
):
    n_dp = lax.axis_size("x") * lax.axis_size("core")
    n_core = lax.axis_size("core")
    n_y = lax.axis_size("ty")
    n_table = N_Z * n_y
    n_dev = n_dp * n_table
    n_plane = n_dp * n_y
    n_s, width = features.shape
    hidden = w_first.shape[1]
    n_feat = width // E
    count = n_s * n_feat
    cap = max(2, 3 * count // (2 * n_dev))
    seg = N_Z * cap
    n_bias = hidden // E
    my_z = lax.axis_index("tz")

    plain = admit == 0
    codes = jnp.stack(
        [
            jnp.where(plain, q_shard[:, :, 0] * QROWS_DEV + q_local, -1),
            jnp.where(plain, r_shard[:, :, 0] * QROWS_DEV + r_local, -1),
            jnp.where(admit == 1, owner[:, :, 0] * (ADM_DEV * n_table) + adm_row, -1),
        ]
    )
    codes = lax.all_gather(codes, "tz", axis=0)

    share = width // n_dev
    wide = width // (n_core * N_Z)
    cut = jnp.stack(
        [
            jnp.concatenate(
                [features[:, (c * N_Z + z) * wide : (c * N_Z + z + 1) * wide] for c in range(n_core)], axis=1
            )
            for z in range(N_Z)
        ]
    )
    feat_in = lax.all_to_all(cut, "tz", split_axis=0, concat_axis=0, tiled=True)
    feat_in = feat_in.reshape(N_Z * n_s, n_core * wide)

    pre = jnp.dot(features, w_first, preferred_element_type=F32) + b_first
    sig = jax.nn.sigmoid(pre)
    dpre = (grad_out.astype(F32) * sig * (1.0 + pre * (1.0 - sig))).astype(BF)
    dpre = lax.all_gather(dpre, "tz", axis=0, tiled=True)

    def in_plane(code, block):
        dev = code // block
        table = dev % n_table
        here = (code >= 0) & (table // n_y == my_z)
        return jnp.where(here, dev // n_table * n_y + table % n_y, -1), code % block

    rows = [codes[:, i].reshape(N_Z * n_s, n_feat) for i in range(3)]
    dq, lq = in_plane(rows[0], QROWS_DEV)
    dr, lr = in_plane(rows[1], QROWS_DEV)
    da, la = in_plane(rows[2], ADM_DEV)
    arow = jnp.where(da >= 0, da * ADM_DEV + la, -1)
    slots, labels = pl.pallas_call(
        functools.partial(slots_kernel, n_plane, cap),
        out_shape=(
            jax.ShapeDtypeStruct((3, N_Z, n_feat, n_s), jnp.int32),
            jax.ShapeDtypeStruct((N_Z, count, E), BF),
        ),
        compiler_params=pltpu.CompilerParams(vmem_limit_bytes=VMEM_LIMIT),
        cost_estimate=pl.CostEstimate(flops=10**9, bytes_accessed=3 * 10**6, transcendentals=0),
        name="slots",
    )(dq, lq, dr, lr, arow)

    w_part = lax.dot_general(feat_in, dpre, (((0,), (0,)), ((), ())), preferred_element_type=F32).astype(BF)
    w_part = lax.all_to_all(
        w_part.reshape(n_plane, share, hidden), ("core", "x", "ty"), split_axis=0, concat_axis=0, tiled=True
    )

    n_rows = 2 * seg + ADM_DEV + 16 + 2 * n_bias
    chunks = pl.pallas_call(
        functools.partial(bucket_kernel, n_plane, cap),
        out_shape=jax.ShapeDtypeStruct((n_plane, n_rows, E), BF),
        scratch_shapes=[
            pltpu.VMEM((N_Z, count, 2 * E), BF),
            pltpu.VMEM((2, n_plane, seg, E), F32),
        ],
        compiler_params=pltpu.CompilerParams(vmem_limit_bytes=VMEM_LIMIT),
        cost_estimate=pl.CostEstimate(flops=20 * 10**9, bytes_accessed=4 * 10**7, transcendentals=0),
        name="buckets",
    )(dpre, w_first, slots, labels)

    w_part, chunks = lax.optimization_barrier((w_part, chunks))
    w_own = jnp.sum(w_part.astype(F32), axis=0).astype(BF)
    w_own, chunks = lax.optimization_barrier((w_own, chunks))
    chunks = lax.all_to_all(chunks, ("x", "core", "ty"), split_axis=0, concat_axis=0, tiled=True)
    w_own = lax.all_gather(w_own, ("x", "ty"), axis=0, tiled=True)
    w_own, chunks = lax.optimization_barrier((w_own, chunks))
    w_own = lax.all_gather(w_own, "tz", axis=0, tiled=True)
    w_all = lax.all_gather(w_own, "core", axis=0, tiled=True)

    n_tall = n_plane * -(-seg // E)
    b_grad, adm_grad, q_grad, r_grad = pl.pallas_call(
        functools.partial(sums_kernel, n_plane, seg, n_bias),
        out_shape=(
            jax.ShapeDtypeStruct((n_bias, E), F32),
            jax.ShapeDtypeStruct((ADM_DEV, E), F32),
            jax.ShapeDtypeStruct((QROWS_DEV, E), F32),
            jax.ShapeDtypeStruct((QROWS_DEV, E), F32),
        ),
        scratch_shapes=[
            pltpu.VMEM((n_tall * E, GROUPS * E), BF),
            pltpu.VMEM((-(-n_tall // 8) * 8, E), jnp.int32),
        ],
        compiler_params=pltpu.CompilerParams(vmem_limit_bytes=VMEM_LIMIT),
        cost_estimate=pl.CostEstimate(flops=7 * 10**9, bytes_accessed=7 * 10**6, transcendentals=0),
        name="sums",
    )(chunks)
    return (w_all.astype(F32), b_grad.reshape(hidden), adm_grad, q_grad, r_grad)


def solution(mesh):
    n_dp, n_table = mesh.devices.shape
    every = ("x", "core", "tz", "ty")
    fine = Mesh(mesh.devices.reshape(n_dp // 2, 2, N_Z, n_table // N_Z), every)
    two, three = P(every, None), P(every, None, None)
    in_specs = (two, P(), P(), two, two, three, two, three, two, three, two)
    out_specs = (P(), P(), two, two, two)
    return jax.shard_map(local, mesh=fine, in_specs=in_specs, out_specs=out_specs, check_vma=False)
```

```python
import functools

import jax
import jax.numpy as jnp
from jax import lax
from jax.experimental import pallas as pl
from jax.experimental.pallas import tpu as pltpu
from jax.sharding import Mesh, PartitionSpec as P

E = 128
ADM_DEV = 128
QROWS_DEV = 4096
N_Z = 4
N_CODE = 8
GROUPS = 4
VMEM_LIMIT = 50 * 1024 * 1024
BF = jnp.bfloat16
F32 = jnp.float32


def iota(shape, dim):
    return lax.broadcasted_iota(jnp.int32, shape, dim)


def dot(a, b, dims=((1,), (0,))):
    return lax.dot_general(a, b, (dims, ((), ())), preferred_element_type=F32)


def one_hot(wanted, row):
    row = jnp.broadcast_to(row, (16, E)).astype(jnp.int16)
    hit = jnp.where(wanted == row[None], jnp.ones((), BF), jnp.zeros((), BF))
    return hit.reshape(wanted.shape[0] * 16, E)


def rows_from(n, base=0):
    return (iota((n, E), 0) + base).astype(jnp.int16).reshape(n // 16, 16, E)


def call(kernel, name, out_shape, flops, traffic, **kwargs):
    return pl.pallas_call(
        kernel,
        out_shape=out_shape,
        compiler_params=pltpu.CompilerParams(vmem_limit_bytes=VMEM_LIMIT),
        cost_estimate=pl.CostEstimate(flops=flops, bytes_accessed=traffic, transcendentals=0),
        name=name,
        **kwargs,
    )


def cut_kernel(n_dp, n_y, n_table, x_ref, admit, owner, adm_row, q_shard, q_local, r_shard, r_local, out_ref):
    piece = x_ref.shape[1] // (n_dp * N_Z)
    wide = n_dp * piece
    plain = admit[...] == 0
    a_row = owner[...] * (ADM_DEV * n_table) + adm_row[...]
    a_dev = a_row // ADM_DEV

    def in_plane(dev, live, z):
        table = dev % n_table
        here = live & (table // n_y == z)
        return here, dev // n_table * n_y + table % n_y

    for z in range(N_Z):
        for d in range(n_dp):
            at = (d * N_Z + z) * piece
            out_ref[z, :, d * piece : (d + 1) * piece] = x_ref[:, at : at + piece]
        codes = []
        for shard, low in ((q_shard, q_local), (r_shard, r_local)):
            here, dest = in_plane(shard[...], plain, z)
            codes += [jnp.where(here, dest, -1), low[...] // 256, low[...] % 256]
        here, dest = in_plane(a_dev, jnp.logical_not(plain), z)
        codes += [jnp.where(here, dest, -1), a_row % ADM_DEV]
        block = jnp.concatenate(codes, axis=0).astype(F32).astype(BF)
        out_ref[z, :, wide : wide + block.shape[1]] = block


def dpre_kernel(x_ref, w_ref, b_ref, g_ref, out_ref):
    pre = dot(x_ref[...], w_ref[...]) + b_ref[...]
    sig = jax.nn.sigmoid(pre)
    dpre = (g_ref[...].astype(F32) * sig * (1.0 + pre * (1.0 - sig))).astype(BF)
    for z in range(N_Z):
        out_ref[z] = dpre


def slots_kernel(n_dest, cap, wide, in_ref, slot_ref, labels_ref, group_ref):
    n_s = in_ref.shape[1]
    n_feat = n_s // N_CODE
    sample = iota((n_s, n_s), 0)
    earlier = (sample < iota((n_s, n_s), 1)).astype(F32).astype(BF)
    ones = jnp.ones((n_s, n_s), BF)
    count = n_dest * n_feat
    at_row, at_col = iota((count, count), 0), iota((count, count), 1)
    before = ((at_row // n_feat == at_col // n_feat) & (at_col < at_row)).astype(F32).astype(BF)
    half = n_dest // 2
    lane = iota((n_s, E), 1) % 4
    for z in range(N_Z):
        codes = in_ref[z, :, wide : wide + n_s].astype(F32)
        plane = [codes[i * n_feat : (i + 1) * n_feat, :] for i in range(N_CODE)]
        for table in range(2):
            dest = plane[table * 3]
            hits = jnp.concatenate([jnp.where(dest == d, 1.0, 0.0) for d in range(n_dest)], axis=0)
            hits_bf = hits.astype(BF)
            rank = dot(hits_bf, earlier) + dot(before, dot(hits_bf, ones).astype(BF))
            rank = rank * hits
            total = rank[0:n_feat, :]
            for d in range(1, n_dest):
                total = total + rank[d * n_feat : (d + 1) * n_feat, :]
            slot = jnp.where(dest >= 0, dest * cap + total, -1.0)
            slot_ref[table, z, :, :] = slot.astype(jnp.int32)
        dest = plane[6]
        folded = jnp.where(dest >= half, dest - half, dest)
        slot_ref[2, z, :, :] = jnp.where(dest >= 0, folded * ADM_DEV + plane[7], -1.0).astype(jnp.int32)
        down = codes.T
        group_ref[z] = down[:, 6 * n_feat : 7 * n_feat]
        for f in range(n_feat):
            col = [down[:, i * n_feat + f : i * n_feat + f + 1] for i in (1, 2, 4, 5)]
            one = jnp.where(lane == 0, col[0], jnp.where(lane == 1, col[1], jnp.where(lane == 2, col[2], col[3])))
            labels_ref[z, f * n_s : (f + 1) * n_s, :] = one.astype(BF)


def w_kernel(n_plane, x_ref, d_ref, out_ref):
    wide = x_ref.shape[2] - E
    share = wide // n_plane
    x = jnp.concatenate([x_ref[z, :, 0:wide] for z in range(N_Z)], axis=0)
    res = dot(x, d_ref[...], ((0,), (0,))).astype(BF)
    for p in range(n_plane):
        out_ref[p] = res[p * share : (p + 1) * share, :]


def bucket_kernel(n_dest, cap, d_ref, w_ref, slot_ref, labels_ref, group_ref, out_ref, v_ref, a_ref, p_ref, mark_ref):
    n_rows, depth = d_ref.shape
    n_s = n_rows // N_Z
    n_feat = w_ref.shape[0] // E
    seg = N_Z * cap
    n_mark = -(-seg // E)
    half = n_dest // 2

    def lookups(step, carry):
        wide = 2 * E
        start = pl.multiple_of(step * wide, wide)
        res = dot(d_ref[...], w_ref[pl.ds(start, wide), :], ((1,), (1,)))
        for z in range(N_Z):
            for h in range(2):
                row = pl.multiple_of((step * 2 + h) * n_s, n_s)
                v_ref[z, pl.ds(row, n_s), 0:E] = res[z * n_s : (z + 1) * n_s, h * E : (h + 1) * E].astype(BF)
        return carry

    lax.fori_loop(0, n_feat // 2, lookups, 0)
    for z in range(N_Z):
        v_ref[z, :, E : 2 * E] = labels_ref[z]

    slots = n_dest * cap
    wanted = rows_from(slots)
    for z in range(N_Z):
        for which in range(2):
            for f in range(n_feat):
                p_ref[which * slots : (which + 1) * slots, f * n_s : (f + 1) * n_s] = one_hot(
                    wanted, slot_ref[which, z, f : f + 1, :]
                )
        for which in range(2):
            o = dot(p_ref[which * slots : (which + 1) * slots, :], v_ref[z])
            for d in range(n_dest):
                rows = o[d * cap : (d + 1) * cap, :]
                out_ref[d, which * seg + z * cap : which * seg + (z + 1) * cap, :] = rows[:, 0:E].astype(BF)
                mark_ref[which, d, z * cap : (z + 1) * cap, :] = rows[:, E : 2 * E]

    tall = half * ADM_DEV
    wanted = rows_from(tall)
    o = jnp.zeros((tall, 2 * E), F32)
    for z in range(N_Z):
        for f in range(n_feat):
            at = f * n_s
            p_ref[0:tall, at : at + n_s] = one_hot(wanted, slot_ref[2, z, f : f + 1, :])
            upper = group_ref[z, :, f : f + 1] >= half
            v = v_ref[z, at : at + n_s, 0:E].astype(F32)
            a_ref[at : at + n_s, 0:E] = jnp.where(upper, 0.0, v).astype(BF)
            a_ref[at : at + n_s, E : 2 * E] = jnp.where(upper, v, 0.0).astype(BF)
        o = o + dot(p_ref[0:tall, :], a_ref[...])
    for d in range(n_dest):
        at = d % half * ADM_DEV
        side = d // half * E
        out_ref[d, 2 * seg : 2 * seg + ADM_DEV, :] = o[at : at + ADM_DEV, side : side + E].astype(BF)

    bias = jnp.sum(d_ref[...].astype(F32), axis=0, keepdims=True)
    high = bias.astype(BF)
    low = (bias - high.astype(F32)).astype(BF)
    n_bias = depth // E
    bias_rows = jnp.concatenate(
        [part[:, i * E : (i + 1) * E].astype(F32) for part in (high, low) for i in range(n_bias)], axis=0
    ).astype(BF)
    at_mark = 2 * seg + ADM_DEV

    def finish(d, carry):
        lane = iota((seg, E), 1) % 4
        mixed = jnp.where(lane < 2, mark_ref[0, d], mark_ref[1, d])
        if seg % E:
            mixed = jnp.concatenate([mixed, jnp.zeros((n_mark * E - seg, E), F32)], axis=0)
        rows = iota((16, E), 0) // 4
        marks = jnp.zeros((16, E), F32)
        for j in range(n_mark):
            across = mixed[j * E : (j + 1) * E, :].T
            marks = jnp.where(rows == j, across[0:16, :], marks)
        out_ref[d, at_mark : at_mark + 16, :] = marks.astype(BF)
        out_ref[d, at_mark + 16 : at_mark + 16 + 2 * n_bias, :] = bias_rows
        return carry

    lax.fori_loop(0, n_dest, finish, 0)


def sums_kernel(n_src, seg, n_bias, in_ref, bias_ref, adm_ref, q_ref, r_ref, v_ref, p_ref):
    n_mark = -(-seg // E)
    at_mark = 2 * seg + ADM_DEV
    adm = jnp.zeros((ADM_DEV, E), F32)
    bias = jnp.zeros((2 * n_bias, E), F32)
    for s in range(n_src):
        adm = adm + in_ref[s, 2 * seg : at_mark, :].astype(F32)
        bias = bias + in_ref[s, at_mark + 16 : at_mark + 16 + 2 * n_bias, :].astype(F32)
    adm_ref[...] = adm
    bias_ref[...] = bias[0:n_bias, :] + bias[n_bias:, :]

    per_group = QROWS_DEV // GROUPS
    wanted = rows_from(per_group)
    for table, out in enumerate((q_ref, r_ref)):

        def spread(s, carry):
            marks = in_ref[s, at_mark : at_mark + 16, :].astype(F32)
            down = jnp.concatenate([marks, jnp.zeros((E - 16, E), F32)], axis=0).T
            for j in range(n_mark):
                at = j * 4 + table * 2
                label = marks[at : at + 1, :] * 256.0 + marks[at + 1 : at + 2, :]
                label = label.astype(jnp.int32) % per_group
                if (j + 1) * E > seg:
                    label = jnp.where(iota((1, E), 1) + j * E < seg, label, -1)
                start = pl.multiple_of((s * n_mark + j) * E, E)
                p_ref[:, pl.ds(start, E)] = one_hot(wanted, label)
                group = (down[:, at : at + 1] * 256.0 + down[:, at + 1 : at + 2]).astype(jnp.int32) // per_group
                rows = in_ref[s, table * seg + j * E : table * seg + (j + 1) * E, :].astype(F32)
                for g in range(GROUPS):
                    v_ref[pl.ds(start, E), g * E : (g + 1) * E] = jnp.where(group == g, rows, 0.0).astype(BF)
            return carry

        lax.fori_loop(0, n_src, spread, 0)
        block = 512
        for b in range(per_group // block):
            o = dot(p_ref[b * block : (b + 1) * block, :], v_ref[...])
            for g in range(GROUPS):
                start = g * per_group + b * block
                out[start : start + block, :] = o[:, g * E : (g + 1) * E]


def widen_kernel(x_ref, *refs):
    refs[-1][...] = x_ref[...].astype(F32)


def widen(x, half, hidden, so_far):
    rows, cols = x.shape
    block = 256
    spec = pl.BlockSpec((block, cols), lambda i: (i, 0))
    more = {} if so_far is None else {"input_output_aliases": {1: 0}}
    args = (x,) if so_far is None else (x, so_far)
    return call(
        widen_kernel,
        "widen",
        jax.ShapeDtypeStruct((rows, hidden), F32),
        rows * cols,
        rows * cols * 6,
        grid=(rows // block,),
        in_specs=[spec] + [pl.BlockSpec(memory_space=pl.ANY)] * (len(args) - 1),
        out_specs=pl.BlockSpec((block, cols), lambda i: (i, half)),
        **more,
    )(*args)


def after(x, *others):
    return lax.optimization_barrier((x,) + others)[0]


def local(
    features, w_first, b_first, grad_out, admit, owner, adm_row, q_shard, q_local, r_shard, r_local
):
    n_dp = lax.axis_size("dp")
    n_y = lax.axis_size("ty")
    n_table = N_Z * n_y
    n_dev = n_dp * n_table
    n_plane = n_dp * n_y
    n_s, width = features.shape
    hidden = w_first.shape[1]
    n_feat = width // E
    count = n_s * n_feat
    cap = max(2, 3 * count // (2 * n_dev))
    seg = N_Z * cap
    n_bias = hidden // E
    share = width // n_dev
    wide = width // N_Z
    shape = jax.ShapeDtypeStruct

    lookup_args = [a.reshape(n_s, n_feat).T for a in (admit, owner, adm_row, q_shard, q_local, r_shard, r_local)]
    cut = call(
        functools.partial(cut_kernel, n_dp, n_y, n_table),
        "cut",
        shape((N_Z, n_s, wide + E), BF),
        10**7,
        2 * 10**6,
    )(features, *lookup_args)
    feat_in = lax.all_to_all(cut, "tz", split_axis=0, concat_axis=0, tiled=True)

    block = min(256, hidden)
    dpre = call(
        dpre_kernel,
        "dpre",
        shape((N_Z, n_s, hidden), BF),
        2 * n_s * width * hidden,
        6 * 10**6,
        grid=(hidden // block,),
        in_specs=[
            pl.BlockSpec((n_s, width), lambda i: (0, 0)),
            pl.BlockSpec((width, block), lambda i: (0, i)),
            pl.BlockSpec((1, block), lambda i: (0, i)),
            pl.BlockSpec((n_s, block), lambda i: (0, i)),
        ],
        out_specs=pl.BlockSpec((N_Z, n_s, block), lambda i: (0, 0, i)),
    )(after(features, cut), w_first, b_first.reshape(1, hidden), grad_out)
    feat_in = after(feat_in, dpre)
    dpre = lax.all_to_all(dpre, "tz", split_axis=0, concat_axis=0, tiled=True).reshape(N_Z * n_s, hidden)

    slots, labels, group = call(
        functools.partial(slots_kernel, n_plane, cap, wide),
        "slots",
        (
            shape((3, N_Z, n_feat, n_s), jnp.int32),
            shape((N_Z, count, E), BF),
            shape((N_Z, n_s, n_feat), F32),
        ),
        10**9,
        3 * 10**6,
    )(feat_in)
    dpre = after(dpre, slots)

    w_part = call(
        functools.partial(w_kernel, n_plane),
        "w_part",
        shape((n_plane, share, hidden), BF),
        2 * N_Z * n_s * wide * hidden,
        3 * 10**6,
    )(feat_in, dpre)
    dpre = after(dpre, w_part)
    w_part = lax.all_to_all(w_part, ("dp", "ty"), split_axis=0, concat_axis=0, tiled=True)

    n_rows = 2 * seg + ADM_DEV + 16 + 2 * n_bias
    tallest = max(2 * n_plane * cap, n_plane // 2 * ADM_DEV)
    chunks = call(
        functools.partial(bucket_kernel, n_plane, cap),
        "buckets",
        shape((n_plane, n_rows, E), BF),
        15 * 10**9,
        4 * 10**7,
        scratch_shapes=[
            pltpu.VMEM((N_Z, count, 2 * E), BF),
            pltpu.VMEM((count, 2 * E), BF),
            pltpu.VMEM((tallest, count), BF),
            pltpu.VMEM((2, n_plane, seg, E), F32),
        ],
    )(dpre, w_first, slots, labels, group)

    w_part = after(w_part, chunks)
    w_own = jnp.sum(w_part.astype(F32), axis=0).astype(BF)
    w_own, chunks = lax.optimization_barrier((w_own, chunks))
    halves = [
        lax.all_gather(w_own[:, h * (hidden // 2) : (h + 1) * (hidden // 2)], ("dp", "tz", "ty"), axis=0, tiled=True)
        for h in range(2)
    ]
    chunks = lax.all_to_all(chunks, ("dp", "ty"), split_axis=0, concat_axis=0, tiled=True)

    tall = n_plane * -(-seg // E) * E
    b_grad, adm_grad, q_grad, r_grad = call(
        functools.partial(sums_kernel, n_plane, seg, n_bias),
        "sums",
        (
            shape((n_bias, E), F32),
            shape((ADM_DEV, E), F32),
            shape((QROWS_DEV, E), F32),
            shape((QROWS_DEV, E), F32),
        ),
        7 * 10**9,
        7 * 10**6,
        scratch_shapes=[
            pltpu.VMEM((tall, GROUPS * E), BF),
            pltpu.VMEM((QROWS_DEV // GROUPS, tall), BF),
        ],
    )(chunks)
    w_grad = widen(after(halves[0], b_grad), 0, hidden, None)
    w_grad = widen(halves[1], 1, hidden, w_grad)
    return (w_grad, b_grad.reshape(hidden), adm_grad, q_grad, r_grad)


def solution(mesh):
    n_dp, n_table = mesh.devices.shape
    every = ("dp", "tz", "ty")
    fine = Mesh(mesh.devices.reshape(n_dp, N_Z, n_table // N_Z), every)
    two, three = P(every, None), P(every, None, None)
    in_specs = (two, P(), P(), two, two, three, two, three, two, three, two)
    out_specs = (P(), P(), two, two, two)
    return jax.shard_map(local, mesh=fine, in_specs=in_specs, out_specs=out_specs, check_vma=False)
```

```python
import functools

import jax
import jax.numpy as jnp
from jax import lax
from jax.experimental import pallas as pl
from jax.experimental.pallas import tpu as pltpu
from jax.sharding import Mesh, PartitionSpec as P

E = 128
ADM_DEV = 128
QROWS_DEV = 4096
N_Z = 4
N_CODE = 8
GROUPS = 4
LOG_ADM = 7
LOG_GROUP = 10
VMEM_LIMIT = 50 * 1024 * 1024
BF = jnp.bfloat16
F32 = jnp.float32


def iota(shape, dim):
    return lax.broadcasted_iota(jnp.int32, shape, dim)


def dot(a, b, dims=((1,), (0,))):
    return lax.dot_general(a, b, (dims, ((), ())), preferred_element_type=F32)


def one_hot(wanted, row):
    row = jnp.broadcast_to(row, (16, E)).astype(jnp.int16)
    hit = jnp.where(wanted == row[None], jnp.ones((), BF), jnp.zeros((), BF))
    return hit.reshape(wanted.shape[0] * 16, E)


def rows_from(n, base=0):
    return (iota((n, E), 0) + base).astype(jnp.int16).reshape(n // 16, 16, E)


def call(kernel, name, out_shape, flops, traffic, **kwargs):
    return pl.pallas_call(
        kernel,
        out_shape=out_shape,
        compiler_params=pltpu.CompilerParams(vmem_limit_bytes=VMEM_LIMIT),
        cost_estimate=pl.CostEstimate(flops=flops, bytes_accessed=traffic, transcendentals=0),
        name=name,
        **kwargs,
    )


def cut_kernel(n_dp, n_y, n_table, x_ref, *refs):
    labels, (out_ref, held, sems) = refs[:-3], refs[-3:]
    copies = [pltpu.make_async_copy(ref, held.at[i], sems.at[i]) for i, ref in enumerate(labels)]
    for copy in copies:
        copy.start()
    piece = x_ref.shape[1] // (n_dp * N_Z)
    wide = n_dp * piece
    for z in range(N_Z):
        for d in range(n_dp):
            at = (d * N_Z + z) * piece
            out_ref[z, :, d * piece : (d + 1) * piece] = x_ref[:, at : at + piece]
    for copy in copies:
        copy.wait()
    admit, owner, adm_row, q_shard, q_local, r_shard, r_local = [held[i] for i in range(len(labels))]
    plain = admit == 0
    a_row = owner * (ADM_DEV * n_table) + adm_row
    a_dev = a_row >> LOG_ADM
    y_bits, table_bits = n_y.bit_length() - 1, n_table.bit_length() - 1

    def in_plane(dev, live, z):
        here = live & (((dev & (n_table - 1)) >> y_bits) == z)
        return jnp.where(here, ((dev >> table_bits) << y_bits) + (dev & (n_y - 1)), -1)

    for z in range(N_Z):
        codes = []
        for shard, low in ((q_shard, q_local), (r_shard, r_local)):
            codes += [in_plane(shard, plain, z), low >> 8, low & 255]
        codes += [in_plane(a_dev, jnp.logical_not(plain), z), a_row & (ADM_DEV - 1)]
        block = jnp.concatenate(codes, axis=0).astype(F32).astype(BF)
        out_ref[z, :, wide : wide + block.shape[1]] = block


def dpre_kernel(x_ref, w_ref, b_ref, g_ref, out_ref):
    pre = dot(x_ref[...], w_ref[...]) + b_ref[...]
    sig = jax.nn.sigmoid(pre)
    dpre = (g_ref[...].astype(F32) * sig * (1.0 + pre * (1.0 - sig))).astype(BF)
    out_ref[...] = dpre


def slots_kernel(n_dest, cap, wide, z_ref, in_ref, slot_ref, labels_ref, group_ref):
    n_s = in_ref.shape[1]
    n_feat = n_s // N_CODE
    sample = iota((n_s, n_s), 0)
    earlier = (sample < iota((n_s, n_s), 1)).astype(F32).astype(BF)
    ones = jnp.ones((n_s, n_s), BF)
    count = n_dest * n_feat
    feat_bits = n_feat.bit_length() - 1
    at_row, at_col = iota((count, count), 0), iota((count, count), 1)
    before = ((at_row >> feat_bits == at_col >> feat_bits) & (at_col < at_row)).astype(F32).astype(BF)
    half = n_dest // 2
    lane = iota((n_s, E), 1) & 3
    for z in range(N_Z):
        codes = in_ref[z_ref[0] ^ z, :, wide : wide + n_s].astype(F32)
        plane = [codes[i * n_feat : (i + 1) * n_feat, :] for i in range(N_CODE)]
        for table in range(2):
            dest = plane[table * 3]
            hits = jnp.concatenate([jnp.where(dest == d, 1.0, 0.0) for d in range(n_dest)], axis=0)
            hits_bf = hits.astype(BF)
            rank = dot(hits_bf, earlier) + dot(before, dot(hits_bf, ones).astype(BF))
            rank = rank * hits
            total = rank[0:n_feat, :]
            for d in range(1, n_dest):
                total = total + rank[d * n_feat : (d + 1) * n_feat, :]
            slot = jnp.where(dest >= 0, dest * cap + total, -1.0)
            slot_ref[table, z, :, :] = slot.astype(jnp.int32)
        dest = plane[6]
        folded = jnp.where(dest >= half, dest - half, dest)
        slot_ref[2, z, :, :] = jnp.where(dest >= 0, folded * ADM_DEV + plane[7], -1.0).astype(jnp.int32)
        down = codes.T
        group_ref[z] = down[:, 6 * n_feat : 7 * n_feat]
        for f in range(n_feat):
            col = [down[:, i * n_feat + f : i * n_feat + f + 1] for i in (1, 2, 4, 5)]
            one = jnp.where(lane == 0, col[0], jnp.where(lane == 1, col[1], jnp.where(lane == 2, col[2], col[3])))
            labels_ref[z, f * n_s : (f + 1) * n_s, :] = one.astype(BF)


def w_kernel(n_plane, z_ref, x_ref, d0_ref, d1_ref, d2_ref, d3_ref, out_ref):
    wide = x_ref.shape[2] - E
    share = wide // n_plane
    x = jnp.concatenate([x_ref[z_ref[0] ^ z, :, 0:wide] for z in range(N_Z)], axis=0)
    d = jnp.concatenate([ref[...] for ref in (d0_ref, d1_ref, d2_ref, d3_ref)], axis=0)
    res = dot(x, d, ((0,), (0,))).astype(BF)
    for p in range(n_plane):
        out_ref[p] = res[p * share : (p + 1) * share, :]


def bucket_kernel(
    n_dest, cap, d0_ref, d1_ref, d2_ref, d3_ref, w_ref, slot_ref, labels_ref, group_ref, out_ref, d_ref, v_ref, a_ref,
    p_ref, mark_ref,
):
    for z, ref in enumerate((d0_ref, d1_ref, d2_ref, d3_ref)):
        d_ref[z * ref.shape[0] : (z + 1) * ref.shape[0], :] = ref[...]
    n_rows, depth = d_ref.shape
    n_s = n_rows // N_Z
    n_feat = w_ref.shape[0] // E
    seg = N_Z * cap
    n_mark = -(-seg // E)
    half = n_dest // 2

    def lookups(step, carry):
        wide = 2 * E
        start = pl.multiple_of(step * wide, wide)
        res = dot(d_ref[...], w_ref[pl.ds(start, wide), :], ((1,), (1,)))
        for z in range(N_Z):
            for h in range(2):
                row = pl.multiple_of((step * 2 + h) * n_s, n_s)
                v_ref[z, pl.ds(row, n_s), 0:E] = res[z * n_s : (z + 1) * n_s, h * E : (h + 1) * E].astype(BF)
        return carry

    lax.fori_loop(0, n_feat // 2, lookups, 0)
    for z in range(N_Z):
        v_ref[z, :, E : 2 * E] = labels_ref[z]

    slots = n_dest * cap
    wanted = rows_from(slots)
    for z in range(N_Z):
        for which in range(2):
            for f in range(n_feat):
                p_ref[which * slots : (which + 1) * slots, f * n_s : (f + 1) * n_s] = one_hot(
                    wanted, slot_ref[which, z, f : f + 1, :]
                )
        for which in range(2):
            o = dot(p_ref[which * slots : (which + 1) * slots, :], v_ref[z])
            for d in range(n_dest):
                rows = o[d * cap : (d + 1) * cap, :]
                out_ref[d, which * seg + z * cap : which * seg + (z + 1) * cap, :] = rows[:, 0:E].astype(BF)
                mark_ref[which, d, z * cap : (z + 1) * cap, :] = rows[:, E : 2 * E]

    tall = half * ADM_DEV
    wanted = rows_from(tall)
    o = jnp.zeros((tall, 2 * E), F32)
    for z in range(N_Z):
        for f in range(n_feat):
            at = f * n_s
            p_ref[0:tall, at : at + n_s] = one_hot(wanted, slot_ref[2, z, f : f + 1, :])
            upper = group_ref[z, :, f : f + 1] >= half
            v = v_ref[z, at : at + n_s, 0:E].astype(F32)
            a_ref[at : at + n_s, 0:E] = jnp.where(upper, 0.0, v).astype(BF)
            a_ref[at : at + n_s, E : 2 * E] = jnp.where(upper, v, 0.0).astype(BF)
        o = o + dot(p_ref[0:tall, :], a_ref[...])
    for d in range(n_dest):
        at = d % half * ADM_DEV
        side = d // half * E
        out_ref[d, 2 * seg : 2 * seg + ADM_DEV, :] = o[at : at + ADM_DEV, side : side + E].astype(BF)

    bias = jnp.sum(d_ref[...].astype(F32), axis=0, keepdims=True)
    high = bias.astype(BF)
    low = (bias - high.astype(F32)).astype(BF)
    n_bias = depth // E
    bias_rows = jnp.concatenate(
        [part[:, i * E : (i + 1) * E].astype(F32) for part in (high, low) for i in range(n_bias)], axis=0
    ).astype(BF)
    at_mark = 2 * seg + ADM_DEV

    def finish(d, carry):
        lane = iota((seg, E), 1) & 3
        mixed = jnp.where(lane < 2, mark_ref[0, d], mark_ref[1, d])
        if seg % E:
            mixed = jnp.concatenate([mixed, jnp.zeros((n_mark * E - seg, E), F32)], axis=0)
        rows = iota((16, E), 0) >> 2
        marks = jnp.zeros((16, E), F32)
        for j in range(n_mark):
            across = mixed[j * E : (j + 1) * E, :].T
            marks = jnp.where(rows == j, across[0:16, :], marks)
        out_ref[d, at_mark : at_mark + 16, :] = marks.astype(BF)
        out_ref[d, at_mark + 16 : at_mark + 16 + 2 * n_bias, :] = bias_rows
        return carry

    lax.fori_loop(0, n_dest, finish, 0)


def sums_kernel(n_src, seg, n_bias, in_ref, bias_ref, adm_ref, q_ref, r_ref, v_ref, p_ref):
    n_mark = -(-seg // E)
    at_mark = 2 * seg + ADM_DEV
    adm = jnp.zeros((ADM_DEV, E), F32)
    bias = jnp.zeros((2 * n_bias, E), F32)
    for s in range(n_src):
        adm = adm + in_ref[s, 2 * seg : at_mark, :].astype(F32)
        bias = bias + in_ref[s, at_mark + 16 : at_mark + 16 + 2 * n_bias, :].astype(F32)
    adm_ref[...] = adm
    bias_ref[...] = bias[0:n_bias, :] + bias[n_bias:, :]

    per_group = QROWS_DEV // GROUPS
    wanted = rows_from(per_group)
    for table, out in enumerate((q_ref, r_ref)):

        def spread(s, carry):
            marks = in_ref[s, at_mark : at_mark + 16, :].astype(F32)
            down = jnp.concatenate([marks, jnp.zeros((E - 16, E), F32)], axis=0).T
            for j in range(n_mark):
                at = j * 4 + table * 2
                label = marks[at : at + 1, :] * 256.0 + marks[at + 1 : at + 2, :]
                label = label.astype(jnp.int32) & (per_group - 1)
                if (j + 1) * E > seg:
                    label = jnp.where(iota((1, E), 1) + j * E < seg, label, -1)
                start = pl.multiple_of((s * n_mark + j) * E, E)
                p_ref[:, pl.ds(start, E)] = one_hot(wanted, label)
                group = down[:, at : at + 1].astype(jnp.int32) >> (LOG_GROUP - 8)
                rows = in_ref[s, table * seg + j * E : table * seg + (j + 1) * E, :].astype(F32)
                for g in range(GROUPS):
                    v_ref[pl.ds(start, E), g * E : (g + 1) * E] = jnp.where(group == g, rows, 0.0).astype(BF)
            return carry

        lax.fori_loop(0, n_src, spread, 0)
        block = 512
        for b in range(per_group // block):
            o = dot(p_ref[b * block : (b + 1) * block, :], v_ref[...])
            for g in range(GROUPS):
                start = g * per_group + b * block
                out[start : start + block, :] = o[:, g * E : (g + 1) * E]


def widen_kernel(core_ref, x_ref, *refs):
    refs[-1][...] = x_ref[...].astype(F32)


def widen(core, x, tall, so_far):
    rows, hidden = x.shape
    block = tall // 2
    alias = {} if so_far is None else {"input_output_aliases": {2: 0}}
    args = (core, x) if so_far is None else (core, x, so_far)
    grid_spec = pltpu.PrefetchScalarGridSpec(
        num_scalar_prefetch=1,
        grid=(rows // block,),
        in_specs=[pl.BlockSpec((block, hidden), lambda i, core: (i, 0))]
        + [pl.BlockSpec(memory_space=pl.ANY)] * (len(args) - 2),
        out_specs=pl.BlockSpec((block, hidden), lambda i, core: ((i // 2 * 2 + core[0]) * 2 + i % 2, 0)),
    )
    return call(
        widen_kernel,
        "widen",
        jax.ShapeDtypeStruct((2 * rows, hidden), F32),
        rows * hidden,
        rows * hidden * 6,
        grid_spec=grid_spec,
        **alias,
    )(*args)


def after(x, *others):
    return lax.optimization_barrier((x,) + others)[0]


def local(
    features, w_first, b_first, grad_out, admit, owner, adm_row, q_shard, q_local, r_shard, r_local
):
    n_core = lax.axis_size("core")
    n_dp = lax.axis_size("x") * n_core
    n_y = lax.axis_size("ty")
    n_table = N_Z * n_y
    n_dev = n_dp * n_table
    n_plane = n_dp * n_y
    n_s, width = features.shape
    hidden = w_first.shape[1]
    n_feat = width // E
    count = n_s * n_feat
    cap = max(2, 3 * count // (2 * n_dev))
    seg = N_Z * cap
    n_bias = hidden // E
    share = width // n_dev
    wide = width // N_Z
    plane = ("x", "core", "ty")
    shape = jax.ShapeDtypeStruct
    my_z = lax.axis_index("tz").astype(jnp.int32).reshape(1)
    my_core = lax.axis_index("core").astype(jnp.int32).reshape(1)
    scalar = pl.BlockSpec(memory_space=pltpu.SMEM)
    array = pl.BlockSpec(memory_space=pltpu.VMEM)

    lookup_args = [a.reshape(n_s, n_feat).T for a in (admit, owner, adm_row, q_shard, q_local, r_shard, r_local)]
    cut = call(
        functools.partial(cut_kernel, n_dp, n_y, n_table),
        "cut",
        shape((N_Z, n_s, wide + E), BF),
        10**7,
        2 * 10**6,
        in_specs=[array] + [pl.BlockSpec(memory_space=pl.ANY)] * len(lookup_args),
        scratch_shapes=[
            pltpu.VMEM((len(lookup_args), n_feat, n_s), jnp.int32),
            pltpu.SemaphoreType.DMA((len(lookup_args),)),
        ],
    )(features, *lookup_args)
    feat_in = lax.all_to_all(cut, "tz", split_axis=0, concat_axis=0, tiled=True)

    block = min(256, hidden)
    dpre = call(
        dpre_kernel,
        "dpre",
        shape((n_s, hidden), BF),
        2 * n_s * width * hidden,
        6 * 10**6,
        grid=(hidden // block,),
        in_specs=[
            pl.BlockSpec((n_s, width), lambda i: (0, 0)),
            pl.BlockSpec((width, block), lambda i: (0, i)),
            pl.BlockSpec((1, block), lambda i: (0, i)),
            pl.BlockSpec((n_s, block), lambda i: (0, i)),
        ],
        out_specs=pl.BlockSpec((n_s, block), lambda i: (0, i)),
    )(after(features, cut), w_first, b_first.reshape(1, hidden), grad_out)

    def swap(x, k):
        return lax.ppermute(x, "tz", [(z, z ^ k) for z in range(N_Z)])

    far = swap(dpre, 2)
    near = swap(dpre, 1)
    sources = [dpre, near, far, swap(far, 1)]
    feat_in = after(feat_in, dpre)

    slots, labels, group = call(
        functools.partial(slots_kernel, n_plane, cap, wide),
        "slots",
        (
            shape((3, N_Z, n_feat, n_s), jnp.int32),
            shape((N_Z, count, E), BF),
            shape((N_Z, n_s, n_feat), F32),
        ),
        10**9,
        3 * 10**6,
        in_specs=[scalar, array],
    )(my_z, feat_in)
    sources[3] = after(sources[3], slots)

    w_part = call(
        functools.partial(w_kernel, n_plane),
        "w_part",
        shape((n_plane, share, hidden), BF),
        2 * N_Z * n_s * wide * hidden,
        3 * 10**6,
        in_specs=[scalar] + [array] * 5,
    )(my_z, feat_in, *sources)
    sources[3] = after(sources[3], w_part)
    w_part = lax.all_to_all(w_part, plane, split_axis=0, concat_axis=0, tiled=True)

    n_rows = 2 * seg + ADM_DEV + 16 + 2 * n_bias
    tallest = max(2 * n_plane * cap, n_plane // 2 * ADM_DEV)
    chunks = call(
        functools.partial(bucket_kernel, n_plane, cap),
        "buckets",
        shape((n_plane, n_rows, E), BF),
        15 * 10**9,
        4 * 10**7,
        scratch_shapes=[
            pltpu.VMEM((N_Z * n_s, hidden), BF),
            pltpu.VMEM((N_Z, count, 2 * E), BF),
            pltpu.VMEM((count, 2 * E), BF),
            pltpu.VMEM((tallest, count), BF),
            pltpu.VMEM((2, n_plane, seg, E), F32),
        ],
    )(*sources, w_first, slots, labels, group)

    w_part = after(w_part, chunks)
    w_own = jnp.sum(w_part.astype(F32), axis=0).astype(BF)
    w_own, chunks = lax.optimization_barrier((w_own, chunks))
    w_half = lax.all_gather(w_own, ("x", "tz", "ty"), axis=0, tiled=True)
    chunks = lax.all_to_all(chunks, plane, split_axis=0, concat_axis=0, tiled=True)

    tall = n_plane * -(-seg // E) * E
    b_grad, adm_grad, q_grad, r_grad = call(
        functools.partial(sums_kernel, n_plane, seg, n_bias),
        "sums",
        (
            shape((n_bias, E), F32),
            shape((ADM_DEV, E), F32),
            shape((QROWS_DEV, E), F32),
            shape((QROWS_DEV, E), F32),
        ),
        7 * 10**9,
        7 * 10**6,
        scratch_shapes=[
            pltpu.VMEM((tall, GROUPS * E), BF),
            pltpu.VMEM((QROWS_DEV // GROUPS, tall), BF),
        ],
    )(chunks)
    w_half = after(w_half, b_grad)
    w_other = lax.ppermute(w_half, "core", [(c, n_core - 1 - c) for c in range(n_core)])
    w_grad = widen(my_core, w_half, n_table * share, None)
    w_grad = widen(1 - my_core, w_other, n_table * share, w_grad)
    return (w_grad, b_grad.reshape(hidden), adm_grad, q_grad, r_grad)


def solution(mesh):
    n_dp, n_table = mesh.devices.shape
    every = ("x", "core", "tz", "ty")
    fine = Mesh(mesh.devices.reshape(n_dp // 2, 2, N_Z, n_table // N_Z), every)
    two, three = P(every, None), P(every, None, None)
    in_specs = (two, P(), P(), two, two, three, two, three, two, three, two)
    out_specs = (P(), P(), two, two, two)
    return jax.shard_map(local, mesh=fine, in_specs=in_specs, out_specs=out_specs, check_vma=False)
```

```python
import functools

import jax
import jax.numpy as jnp
from jax import lax
from jax.experimental import pallas as pl
from jax.experimental.pallas import tpu as pltpu
from jax.sharding import Mesh, PartitionSpec as P

E = 128
ADM_DEV = 128
QROWS_DEV = 4096
N_Z = 4
N_CODE = 8
GROUPS = 4
LOG_ADM = 7
LOG_GROUP = 10
MIB = 1024 * 1024
BF = jnp.bfloat16
F32 = jnp.float32


def iota(shape, dim):
    return lax.broadcasted_iota(jnp.int32, shape, dim)


def dot(a, b, dims=((1,), (0,))):
    return lax.dot_general(a, b, (dims, ((), ())), preferred_element_type=F32)


def one_hot(wanted, row):
    row = jnp.broadcast_to(row, (16, E)).astype(jnp.int16)
    hit = jnp.where(wanted == row[None], jnp.ones((), BF), jnp.zeros((), BF))
    return hit.reshape(wanted.shape[0] * 16, E)


def rows_from(n, base=0):
    return (iota((n, E), 0) + base).astype(jnp.int16).reshape(n // 16, 16, E)


def call(kernel, name, out_shape, flops, traffic, vmem=24, **kwargs):
    return pl.pallas_call(
        kernel,
        out_shape=out_shape,
        compiler_params=pltpu.CompilerParams(vmem_limit_bytes=vmem * MIB),
        cost_estimate=pl.CostEstimate(flops=flops, bytes_accessed=traffic, transcendentals=0),
        name=name,
        **kwargs,
    )


def cut_kernel(n_dp, n_y, n_table, x_ref, *refs):
    labels, (out_ref, held, sems) = refs[:-3], refs[-3:]
    copies = [pltpu.make_async_copy(ref, held.at[i], sems.at[i]) for i, ref in enumerate(labels)]
    for copy in copies:
        copy.start()
    piece = x_ref.shape[1] // (n_dp * N_Z)
    wide = n_dp * piece
    for z in range(N_Z):
        for d in range(n_dp):
            at = (d * N_Z + z) * piece
            out_ref[z, :, d * piece : (d + 1) * piece] = x_ref[:, at : at + piece]
    for copy in copies:
        copy.wait()
    admit, owner, adm_row, q_shard, q_local, r_shard, r_local = [held[i] for i in range(len(labels))]
    plain = admit == 0
    a_row = owner * (ADM_DEV * n_table) + adm_row
    a_dev = a_row >> LOG_ADM
    y_bits, table_bits = n_y.bit_length() - 1, n_table.bit_length() - 1

    def in_plane(dev, live, z):
        here = live & (((dev & (n_table - 1)) >> y_bits) == z)
        return jnp.where(here, ((dev >> table_bits) << y_bits) + (dev & (n_y - 1)), -1)

    for z in range(N_Z):
        codes = []
        for shard, low in ((q_shard, q_local), (r_shard, r_local)):
            codes += [in_plane(shard, plain, z), low >> 8, low & 255]
        codes += [in_plane(a_dev, jnp.logical_not(plain), z), a_row & (ADM_DEV - 1)]
        block = jnp.concatenate(codes, axis=0).astype(F32).astype(BF)
        out_ref[z, :, wide : wide + block.shape[1]] = block


def dpre_kernel(x_ref, w_ref, b_ref, g_ref, out_ref):
    pre = dot(x_ref[...], w_ref[...]) + b_ref[...]
    sig = jax.nn.sigmoid(pre)
    dpre = (g_ref[...].astype(F32) * sig * (1.0 + pre * (1.0 - sig))).astype(BF)
    out_ref[...] = dpre


def slots_kernel(n_dest, cap, wide, z_ref, in_ref, slot_ref, labels_ref, group_ref):
    n_s = in_ref.shape[1]
    n_feat = n_s // N_CODE
    sample = iota((n_s, n_s), 0)
    earlier = (sample < iota((n_s, n_s), 1)).astype(F32).astype(BF)
    ones = jnp.ones((n_s, n_s), BF)
    count = n_dest * n_feat
    feat_bits = n_feat.bit_length() - 1
    at_row, at_col = iota((count, count), 0), iota((count, count), 1)
    before = ((at_row >> feat_bits == at_col >> feat_bits) & (at_col < at_row)).astype(F32).astype(BF)
    half = n_dest // 2
    lane = iota((n_s, E), 1) & 3
    for z in range(N_Z):
        codes = in_ref[z_ref[0] ^ z, :, wide : wide + n_s].astype(F32)
        plane = [codes[i * n_feat : (i + 1) * n_feat, :] for i in range(N_CODE)]
        for table in range(2):
            dest = plane[table * 3]
            hits = jnp.concatenate([jnp.where(dest == d, 1.0, 0.0) for d in range(n_dest)], axis=0)
            hits_bf = hits.astype(BF)
            rank = dot(hits_bf, earlier) + dot(before, dot(hits_bf, ones).astype(BF))
            rank = rank * hits
            total = rank[0:n_feat, :]
            for d in range(1, n_dest):
                total = total + rank[d * n_feat : (d + 1) * n_feat, :]
            slot = jnp.where(dest >= 0, dest * cap + total, -1.0)
            slot_ref[table, z, :, :] = slot.astype(jnp.int32)
        dest = plane[6]
        folded = jnp.where(dest >= half, dest - half, dest)
        slot_ref[2, z, :, :] = jnp.where(dest >= 0, folded * ADM_DEV + plane[7], -1.0).astype(jnp.int32)
        down = codes.T
        group_ref[z] = down[:, 6 * n_feat : 7 * n_feat]
        for f in range(n_feat):
            col = [down[:, i * n_feat + f : i * n_feat + f + 1] for i in (1, 2, 4, 5)]
            one = jnp.where(lane == 0, col[0], jnp.where(lane == 1, col[1], jnp.where(lane == 2, col[2], col[3])))
            labels_ref[z, f * n_s : (f + 1) * n_s, :] = one.astype(BF)


def w_kernel(n_plane, z_ref, x_ref, d0_ref, d1_ref, d2_ref, d3_ref, out_ref):
    wide = x_ref.shape[2] - E
    share = wide // n_plane
    x = jnp.concatenate([x_ref[z_ref[0] ^ z, :, 0:wide] for z in range(N_Z)], axis=0)
    d = jnp.concatenate([ref[...] for ref in (d0_ref, d1_ref, d2_ref, d3_ref)], axis=0)
    res = dot(x, d, ((0,), (0,))).astype(BF)
    for p in range(n_plane):
        out_ref[p] = res[p * share : (p + 1) * share, :]


def bucket_kernel(
    n_dest, cap, d0_ref, d1_ref, d2_ref, d3_ref, w_ref, slot_ref, labels_ref, group_ref, out_ref, d_ref, v_ref,
    mark_ref,
):
    for z, ref in enumerate((d0_ref, d1_ref, d2_ref, d3_ref)):
        d_ref[z * ref.shape[0] : (z + 1) * ref.shape[0], :] = ref[...]
    n_rows, depth = d_ref.shape
    n_s = n_rows // N_Z
    n_feat = w_ref.shape[0] // E
    seg = N_Z * cap
    n_mark = -(-seg // E)
    half = n_dest // 2

    def lookups(step, carry):
        wide = 2 * E
        start = pl.multiple_of(step * wide, wide)
        res = dot(d_ref[...], w_ref[pl.ds(start, wide), :], ((1,), (1,)))
        for z in range(N_Z):
            for h in range(2):
                row = pl.multiple_of((step * 2 + h) * n_s, n_s)
                v_ref[z, pl.ds(row, n_s), 0:E] = res[z * n_s : (z + 1) * n_s, h * E : (h + 1) * E].astype(BF)
        return carry

    lax.fori_loop(0, n_feat // 2, lookups, 0)
    for z in range(N_Z):
        v_ref[z, :, E : 2 * E] = labels_ref[z]

    slots = n_dest * cap
    wanted = rows_from(slots)
    for z in range(N_Z):
        for which in range(2):
            hits = [one_hot(wanted, slot_ref[which, z, f : f + 1, :]) for f in range(n_feat)]
            o = dot(jnp.concatenate(hits, axis=1), v_ref[z])
            for d in range(n_dest):
                rows = o[d * cap : (d + 1) * cap, :]
                out_ref[d, which * seg + z * cap : which * seg + (z + 1) * cap, :] = rows[:, 0:E].astype(BF)
                mark_ref[which, d, z * cap : (z + 1) * cap, :] = rows[:, E : 2 * E]

    tall = half * ADM_DEV
    wanted = rows_from(tall)
    o = jnp.zeros((tall, 2 * E), F32)
    for z in range(N_Z):
        hits = [one_hot(wanted, slot_ref[2, z, f : f + 1, :]) for f in range(n_feat)]
        sides = []
        for f in range(n_feat):
            upper = group_ref[z, :, f : f + 1] >= half
            v = v_ref[z, f * n_s : (f + 1) * n_s, 0:E].astype(F32)
            sides.append(jnp.concatenate([jnp.where(upper, 0.0, v), jnp.where(upper, v, 0.0)], axis=1).astype(BF))
        o = o + dot(jnp.concatenate(hits, axis=1), jnp.concatenate(sides, axis=0))
    for d in range(n_dest):
        at = d % half * ADM_DEV
        side = d // half * E
        out_ref[d, 2 * seg : 2 * seg + ADM_DEV, :] = o[at : at + ADM_DEV, side : side + E].astype(BF)

    bias = jnp.sum(d_ref[...].astype(F32), axis=0, keepdims=True)
    high = bias.astype(BF)
    low = (bias - high.astype(F32)).astype(BF)
    n_bias = depth // E
    bias_rows = jnp.concatenate(
        [part[:, i * E : (i + 1) * E].astype(F32) for part in (high, low) for i in range(n_bias)], axis=0
    ).astype(BF)
    at_mark = 2 * seg + ADM_DEV

    def finish(d, carry):
        lane = iota((seg, E), 1) & 3
        mixed = jnp.where(lane < 2, mark_ref[0, d], mark_ref[1, d])
        if seg % E:
            mixed = jnp.concatenate([mixed, jnp.zeros((n_mark * E - seg, E), F32)], axis=0)
        rows = iota((16, E), 0) >> 2
        marks = jnp.zeros((16, E), F32)
        for j in range(n_mark):
            across = mixed[j * E : (j + 1) * E, :].T
            marks = jnp.where(rows == j, across[0:16, :], marks)
        out_ref[d, at_mark : at_mark + 16, :] = marks.astype(BF)
        out_ref[d, at_mark + 16 : at_mark + 16 + 2 * n_bias, :] = bias_rows
        return carry

    lax.fori_loop(0, n_dest, finish, 0)


def sums_kernel(n_src, seg, n_bias, table, in_ref, *outs):
    n_mark = -(-seg // E)
    at_mark = 2 * seg + ADM_DEV
    if table == 0:
        adm = jnp.zeros((ADM_DEV, E), F32)
        bias = jnp.zeros((2 * n_bias, E), F32)
        for s in range(n_src):
            adm = adm + in_ref[s, 2 * seg : at_mark, :].astype(F32)
            bias = bias + in_ref[s, at_mark + 16 : at_mark + 16 + 2 * n_bias, :].astype(F32)
        outs[1][...] = bias[0:n_bias, :] + bias[n_bias:, :]
        outs[2][...] = adm

    per_group = QROWS_DEV // GROUPS
    labels, sides = [], []
    for s in range(n_src):
        marks = in_ref[s, at_mark : at_mark + 16, :].astype(F32)
        down = jnp.concatenate([marks, jnp.zeros((E - 16, E), F32)], axis=0).T
        for j in range(n_mark):
            at = j * 4 + table * 2
            label = marks[at : at + 1, :] * 256.0 + marks[at + 1 : at + 2, :]
            label = label.astype(jnp.int32) & (per_group - 1)
            if (j + 1) * E > seg:
                label = jnp.where(iota((1, E), 1) + j * E < seg, label, -1)
            labels.append(label)
            group = down[:, at : at + 1].astype(jnp.int32) >> (LOG_GROUP - 8)
            rows = in_ref[s, table * seg + j * E : table * seg + (j + 1) * E, :].astype(F32)
            sides.append(
                jnp.concatenate([jnp.where(group == g, rows, 0.0) for g in range(GROUPS)], axis=1).astype(BF)
            )
    spread = jnp.concatenate(sides, axis=0)
    block = 512
    for b in range(per_group // block):
        wanted = rows_from(block, b * block)
        o = dot(jnp.concatenate([one_hot(wanted, label) for label in labels], axis=1), spread)
        for g in range(GROUPS):
            start = g * per_group + b * block
            outs[0][start : start + block, :] = o[:, g * E : (g + 1) * E]


def doubling(n):
    return [1 << i for i in range(n.bit_length() - 1)]


def swap(x, axis, k):
    n = lax.axis_size(axis)
    return lax.ppermute(x, axis, [(i, i ^ k) for i in range(n)])


def widen_kernel(n_x, n_y, share, at_ref, a_ref, b_ref, *refs):
    out_ref, held_ref, sems = refs[-3:]
    half = a_ref.shape[1]
    copies = []
    for b in range(a_ref.shape[0] // share):
        z = at_ref[2] ^ (((b & 1) << 1) | ((b >> 1) & 1))
        rest = b >> 2
        rows = slice(b * share, (b + 1) * share)
        for side, ref in enumerate((a_ref, b_ref)):
            y, x = (rest % n_y, rest // n_y) if side == 0 else (rest // n_x, rest % n_x)
            row = ((((at_ref[0] ^ x) * 2 + at_ref[1]) * N_Z + z) * n_y + (at_ref[3] ^ y)) * share
            cols = slice(side * half, (side + 1) * half)
            held_ref[rows, cols] = ref[rows, :].astype(F32)
            copy = pltpu.make_async_copy(
                held_ref.at[rows, cols], out_ref.at[pl.ds(pl.multiple_of(row, share), share), cols], sems.at[len(copies)]
            )
            copy.start()
            copies.append(copy)
    for copy in copies:
        copy.wait()


def widen(n_x, n_y, share, at, sides, so_far):
    rows, half = sides[0].shape
    array = pl.BlockSpec(memory_space=pltpu.VMEM)
    more = () if so_far is None else (so_far,)
    alias = {} if so_far is None else {"input_output_aliases": {3: 0}}
    return call(
        functools.partial(widen_kernel, n_x, n_y, share),
        "widen",
        jax.ShapeDtypeStruct((2 * rows, 2 * half), F32),
        rows * half * 2,
        rows * half * 12,
        in_specs=[pl.BlockSpec(memory_space=pltpu.SMEM), array, array] + [pl.BlockSpec(memory_space=pltpu.HBM)] * len(more),
        out_specs=pl.BlockSpec(memory_space=pltpu.HBM),
        scratch_shapes=[
            pltpu.VMEM((rows, 2 * half), F32),
            pltpu.SemaphoreType.DMA((2 * (rows // share),)),
        ],
        **alias,
    )(at, *sides, *more)


def after(x, *others):
    return lax.optimization_barrier((x,) + others)[0]


def local(
    features, w_first, b_first, grad_out, admit, owner, adm_row, q_shard, q_local, r_shard, r_local
):
    n_core = lax.axis_size("core")
    n_dp = lax.axis_size("x") * n_core
    n_y = lax.axis_size("ty")
    n_table = N_Z * n_y
    n_dev = n_dp * n_table
    n_plane = n_dp * n_y
    n_s, width = features.shape
    hidden = w_first.shape[1]
    n_feat = width // E
    count = n_s * n_feat
    cap = max(2, 3 * count // (2 * n_dev))
    seg = N_Z * cap
    n_bias = hidden // E
    share = width // n_dev
    wide = width // N_Z
    plane = ("x", "core", "ty")
    shape = jax.ShapeDtypeStruct
    my_z = lax.axis_index("tz").astype(jnp.int32).reshape(1)
    scalar = pl.BlockSpec(memory_space=pltpu.SMEM)
    array = pl.BlockSpec(memory_space=pltpu.VMEM)

    lookup_args = [a.reshape(n_s, n_feat).T for a in (admit, owner, adm_row, q_shard, q_local, r_shard, r_local)]
    cut = call(
        functools.partial(cut_kernel, n_dp, n_y, n_table),
        "cut",
        shape((N_Z, n_s, wide + E), BF),
        10**7,
        2 * 10**6,
        in_specs=[array] + [pl.BlockSpec(memory_space=pltpu.HBM)] * len(lookup_args),
        scratch_shapes=[
            pltpu.VMEM((len(lookup_args), n_feat, n_s), jnp.int32),
            pltpu.SemaphoreType.DMA((len(lookup_args),)),
        ],
    )(features, *lookup_args)
    feat_in = lax.all_to_all(cut, "tz", split_axis=0, concat_axis=0, tiled=True)

    block = min(256, hidden)
    dpre = call(
        dpre_kernel,
        "dpre",
        shape((n_s, hidden), BF),
        2 * n_s * width * hidden,
        6 * 10**6,
        grid=(hidden // block,),
        in_specs=[
            pl.BlockSpec((n_s, width), lambda i: (0, 0)),
            pl.BlockSpec((width, block), lambda i: (0, i)),
            pl.BlockSpec((1, block), lambda i: (0, i)),
            pl.BlockSpec((n_s, block), lambda i: (0, i)),
        ],
        out_specs=pl.BlockSpec((n_s, block), lambda i: (0, i)),
    )(after(features, cut), w_first, b_first.reshape(1, hidden), grad_out)

    far = swap(dpre, "tz", 2)
    near = swap(dpre, "tz", 1)
    far = after(far, near)
    sources = [dpre, near, far, swap(far, "tz", 1)]
    feat_in = after(feat_in, dpre)

    slots, labels, group = call(
        functools.partial(slots_kernel, n_plane, cap, wide),
        "slots",
        (
            shape((3, N_Z, n_feat, n_s), jnp.int32),
            shape((N_Z, count, E), BF),
            shape((N_Z, n_s, n_feat), F32),
        ),
        10**9,
        3 * 10**6,
        in_specs=[scalar, array],
    )(my_z, feat_in)
    sources[3] = after(sources[3], slots)

    w_part = call(
        functools.partial(w_kernel, n_plane),
        "w_part",
        shape((n_plane, share, hidden), BF),
        2 * N_Z * n_s * wide * hidden,
        3 * 10**6,
        in_specs=[scalar] + [array] * 5,
    )(my_z, feat_in, *sources)
    sources[3] = after(sources[3], w_part)
    w_part = lax.all_to_all(w_part, plane, split_axis=0, concat_axis=0, tiled=True)

    n_rows = 2 * seg + ADM_DEV + 16 + 2 * n_bias
    chunks = call(
        functools.partial(bucket_kernel, n_plane, cap),
        "buckets",
        shape((n_plane, n_rows, E), BF),
        15 * 10**9,
        4 * 10**7,
        scratch_shapes=[
            pltpu.VMEM((N_Z * n_s, hidden), BF),
            pltpu.VMEM((N_Z, count, 2 * E), BF),
            pltpu.VMEM((2, n_plane, seg, E), F32),
        ],
        vmem=44,
    )(*sources, w_first, slots, labels, group)

    w_part = after(w_part, chunks)
    w_own = jnp.sum(w_part.astype(F32), axis=0).astype(BF)
    w_own, chunks = lax.optimization_barrier((w_own, chunks))
    chunks = lax.all_to_all(chunks, plane, split_axis=0, concat_axis=0, tiled=True)

    w_two = jnp.concatenate([w_own, swap(w_own, "tz", 2)], axis=0)
    w_four = jnp.concatenate([w_two, swap(w_two, "tz", 1)], axis=0)
    sides = [w_four[:, : hidden // 2], w_four[:, hidden // 2 :]]
    over_y = [("ty", k) for k in doubling(n_y)]
    over_x = [("x", k) for k in doubling(n_dp // n_core)]
    before = sides
    for steps in zip(over_y + over_x, over_x + over_y):
        before = sides
        sides = [jnp.concatenate([side, swap(side, *step)], axis=0) for side, step in zip(sides, steps)]
    chunks = after(chunks, *before)

    def sums(table, chunks):
        outs = (shape((QROWS_DEV, E), F32), shape((n_bias, E), F32), shape((ADM_DEV, E), F32))
        return call(
            functools.partial(sums_kernel, n_plane, seg, n_bias, table),
            ("q_sums", "r_sums")[table],
            outs if table == 0 else outs[:1],
            4 * 10**9,
            4 * 10**6,
            vmem=40,
        )(chunks)

    q_grad, b_grad, adm_grad = sums(0, chunks)
    sides = [after(side, q_grad) for side in sides]
    (r_grad,) = sums(1, after(chunks, *sides))
    others = [swap(side, "core", 1) for side in sides]
    at = jnp.stack([lax.axis_index(name) for name in ("x", "core", "tz", "ty")]).astype(jnp.int32)
    n_x = n_dp // n_core
    w_grad = widen(n_x, n_y, share, at, [after(side, r_grad) for side in sides], None)
    flip = at ^ jnp.array([0, 1, 0, 0], jnp.int32)
    w_grad = widen(n_x, n_y, share, flip, others, w_grad)
    return (w_grad, b_grad.reshape(hidden), adm_grad, q_grad, r_grad)


def solution(mesh):
    n_dp, n_table = mesh.devices.shape
    every = ("x", "core", "tz", "ty")
    fine = Mesh(mesh.devices.reshape(n_dp // 2, 2, N_Z, n_table // N_Z), every)
    two, three = P(every, None), P(every, None, None)
    in_specs = (two, P(), P(), two, two, three, two, three, two, three, two)
    out_specs = (P(), P(), two, two, two)
    return jax.shard_map(local, mesh=fine, in_specs=in_specs, out_specs=out_specs, check_vma=False)
```

```python
import functools

import jax
import jax.numpy as jnp
from jax import lax
from jax.experimental import pallas as pl
from jax.experimental.pallas import tpu as pltpu
from jax.sharding import Mesh, PartitionSpec as P

E = 128
ADM_DEV = 128
QROWS_DEV = 4096
N_Z = 4
N_CODE = 8
GROUPS = 4
LOG_ADM = 7
LOG_QROWS = 12
LOG_GROUP = 10
MIB = 1024 * 1024
BF = jnp.bfloat16
F32 = jnp.float32


def iota(shape, dim):
    return lax.broadcasted_iota(jnp.int32, shape, dim)


def dot(a, b, dims=((1,), (0,))):
    return lax.dot_general(a, b, (dims, ((), ())), preferred_element_type=F32)


def one_hot(wanted, row):
    row = jnp.broadcast_to(row, (16, E)).astype(jnp.int16)
    hit = jnp.where(wanted == row[None], jnp.ones((), BF), jnp.zeros((), BF))
    return hit.reshape(wanted.shape[0] * 16, E)


def rows_from(n, base=0):
    return (iota((n, E), 0) + base).astype(jnp.int16).reshape(n // 16, 16, E)


def call(kernel, name, out_shape, flops, traffic, vmem=24, **kwargs):
    return pl.pallas_call(
        kernel,
        out_shape=out_shape,
        compiler_params=pltpu.CompilerParams(vmem_limit_bytes=vmem * MIB),
        cost_estimate=pl.CostEstimate(flops=flops, bytes_accessed=traffic, transcendentals=0),
        name=name,
        **kwargs,
    )


def cut_kernel(n_dp, n_y, n_table, x_ref, q_ref, r_ref, a_ref, out_ref):
    piece = x_ref.shape[1] // (n_dp * N_Z)
    wide = n_dp * piece
    y_bits, table_bits = n_y.bit_length() - 1, n_table.bit_length() - 1

    def in_plane(code, bits, z):
        dev = code >> bits
        here = (code >= 0) & (((dev & (n_table - 1)) >> y_bits) == z)
        return jnp.where(here, ((dev >> table_bits) << y_bits) + (dev & (n_y - 1)), -1)

    for z in range(N_Z):
        for d in range(n_dp):
            at = (d * N_Z + z) * piece
            out_ref[z, :, d * piece : (d + 1) * piece] = x_ref[:, at : at + piece]
        codes = []
        for ref in (q_ref, r_ref):
            low = ref[...] & (QROWS_DEV - 1)
            codes += [in_plane(ref[...], LOG_QROWS, z), low >> 8, low & 255]
        codes += [in_plane(a_ref[...], LOG_ADM, z), a_ref[...] & (ADM_DEV - 1)]
        block = jnp.concatenate(codes, axis=0).astype(F32).astype(BF)
        out_ref[z, :, wide : wide + block.shape[1]] = block


def dpre_kernel(x_ref, w_ref, b_ref, g_ref, out_ref):
    pre = dot(x_ref[...], w_ref[...]) + b_ref[...]
    sig = jax.nn.sigmoid(pre)
    dpre = (g_ref[...].astype(F32) * sig * (1.0 + pre * (1.0 - sig))).astype(BF)
    out_ref[...] = dpre


def slots_kernel(n_dest, cap, wide, z_ref, in_ref, slot_ref, labels_ref, group_ref):
    n_s = in_ref.shape[1]
    n_feat = n_s // N_CODE
    sample = iota((n_s, n_s), 0)
    earlier = (sample < iota((n_s, n_s), 1)).astype(F32).astype(BF)
    ones = jnp.ones((n_s, n_s), BF)
    count = n_dest * n_feat
    feat_bits = n_feat.bit_length() - 1
    at_row, at_col = iota((count, count), 0), iota((count, count), 1)
    before = ((at_row >> feat_bits == at_col >> feat_bits) & (at_col < at_row)).astype(F32).astype(BF)
    half = n_dest // 2
    lane = iota((n_s, E), 1) & 3
    for z in range(N_Z):
        codes = in_ref[z_ref[0] ^ z, :, wide : wide + n_s].astype(F32)
        plane = [codes[i * n_feat : (i + 1) * n_feat, :] for i in range(N_CODE)]
        for table in range(2):
            dest = plane[table * 3]
            hits = jnp.concatenate([jnp.where(dest == d, 1.0, 0.0) for d in range(n_dest)], axis=0)
            hits_bf = hits.astype(BF)
            rank = dot(hits_bf, earlier) + dot(before, dot(hits_bf, ones).astype(BF))
            rank = rank * hits
            total = rank[0:n_feat, :]
            for d in range(1, n_dest):
                total = total + rank[d * n_feat : (d + 1) * n_feat, :]
            slot = jnp.where(dest >= 0, dest * cap + total, -1.0)
            slot_ref[table, z, :, :] = slot.astype(jnp.int32)
        dest = plane[6]
        folded = jnp.where(dest >= half, dest - half, dest)
        slot_ref[2, z, :, :] = jnp.where(dest >= 0, folded * ADM_DEV + plane[7], -1.0).astype(jnp.int32)
        down = codes.T
        group_ref[z] = down[:, 6 * n_feat : 7 * n_feat]
        for f in range(n_feat):
            col = [down[:, i * n_feat + f : i * n_feat + f + 1] for i in (1, 2, 4, 5)]
            one = jnp.where(lane == 0, col[0], jnp.where(lane == 1, col[1], jnp.where(lane == 2, col[2], col[3])))
            labels_ref[z, f * n_s : (f + 1) * n_s, :] = one.astype(BF)


def w_kernel(n_plane, z_ref, x_ref, d0_ref, d1_ref, d2_ref, d3_ref, out_ref):
    wide = x_ref.shape[2] - E
    share = wide // n_plane
    x = jnp.concatenate([x_ref[z_ref[0] ^ z, :, 0:wide] for z in range(N_Z)], axis=0)
    d = jnp.concatenate([ref[...] for ref in (d0_ref, d1_ref, d2_ref, d3_ref)], axis=0)
    res = dot(x, d, ((0,), (0,))).astype(BF)
    for p in range(n_plane):
        out_ref[p] = res[p * share : (p + 1) * share, :]


def lookup_kernel(d0_ref, d1_ref, d2_ref, d3_ref, w_ref, out_ref, bias_ref, d_ref):
    n_s, depth = d0_ref.shape
    for z, ref in enumerate((d0_ref, d1_ref, d2_ref, d3_ref)):
        d_ref[z * n_s : (z + 1) * n_s, :] = ref[...]
    for step in range(w_ref.shape[0] // (2 * E)):
        res = dot(d_ref[...], w_ref[step * 2 * E : (step + 1) * 2 * E, :], ((1,), (1,))).astype(BF)
        for z in range(N_Z):
            for h in range(2):
                row = (step * 2 + h) * n_s
                out_ref[z, row : row + n_s, :] = res[z * n_s : (z + 1) * n_s, h * E : (h + 1) * E]
    bias = jnp.sum(d_ref[...].astype(F32), axis=0, keepdims=True)
    high = bias.astype(BF)
    low = (bias - high.astype(F32)).astype(BF)
    bias_ref[...] = jnp.concatenate(
        [part[:, i * E : (i + 1) * E].astype(F32) for part in (high, low) for i in range(depth // E)], axis=0
    ).astype(BF)


def bucket_kernel(n_dest, cap, look_ref, slot_ref, labels_ref, group_ref, bias_ref, out_ref, mark_ref):
    n_feat, n_s = slot_ref.shape[2:]
    seg = N_Z * cap
    n_mark = -(-seg // E)
    half = n_dest // 2

    slots = n_dest * cap
    wanted = rows_from(slots)
    for z in range(N_Z):
        for which in range(2):
            hits = [one_hot(wanted, slot_ref[which, z, f : f + 1, :]) for f in range(n_feat)]
            o = dot(jnp.concatenate(hits, axis=1), jnp.concatenate([look_ref[z], labels_ref[z]], axis=1))
            for d in range(n_dest):
                rows = o[d * cap : (d + 1) * cap, :]
                out_ref[d, which * seg + z * cap : which * seg + (z + 1) * cap, :] = rows[:, 0:E].astype(BF)
                mark_ref[which, d, z * cap : (z + 1) * cap, :] = rows[:, E : 2 * E]

    tall = half * ADM_DEV
    wanted = rows_from(tall)
    o = jnp.zeros((tall, 2 * E), F32)
    for z in range(N_Z):
        hits = [one_hot(wanted, slot_ref[2, z, f : f + 1, :]) for f in range(n_feat)]
        sides = []
        for f in range(n_feat):
            upper = group_ref[z, :, f : f + 1] >= half
            v = look_ref[z, f * n_s : (f + 1) * n_s, :].astype(F32)
            sides.append(jnp.concatenate([jnp.where(upper, 0.0, v), jnp.where(upper, v, 0.0)], axis=1).astype(BF))
        o = o + dot(jnp.concatenate(hits, axis=1), jnp.concatenate(sides, axis=0))
    for d in range(n_dest):
        at = d % half * ADM_DEV
        side = d // half * E
        out_ref[d, 2 * seg : 2 * seg + ADM_DEV, :] = o[at : at + ADM_DEV, side : side + E].astype(BF)

    at_mark = 2 * seg + ADM_DEV

    def finish(d, carry):
        lane = iota((seg, E), 1) & 3
        mixed = jnp.where(lane < 2, mark_ref[0, d], mark_ref[1, d])
        if seg % E:
            mixed = jnp.concatenate([mixed, jnp.zeros((n_mark * E - seg, E), F32)], axis=0)
        rows = iota((16, E), 0) >> 2
        marks = jnp.zeros((16, E), F32)
        for j in range(n_mark):
            across = mixed[j * E : (j + 1) * E, :].T
            marks = jnp.where(rows == j, across[0:16, :], marks)
        out_ref[d, at_mark : at_mark + 16, :] = marks.astype(BF)
        out_ref[d, at_mark + 16 : at_mark + 16 + bias_ref.shape[0], :] = bias_ref[...]
        return carry

    lax.fori_loop(0, n_dest, finish, 0)


def sums_kernel(n_src, seg, n_bias, table, in_ref, *outs):
    n_mark = -(-seg // E)
    at_mark = 2 * seg + ADM_DEV
    if table == 0:
        adm = jnp.zeros((ADM_DEV, E), F32)
        bias = jnp.zeros((2 * n_bias, E), F32)
        for s in range(n_src):
            adm = adm + in_ref[s, 2 * seg : at_mark, :].astype(F32)
            bias = bias + in_ref[s, at_mark + 16 : at_mark + 16 + 2 * n_bias, :].astype(F32)
        outs[1][...] = bias[0:n_bias, :] + bias[n_bias:, :]
        outs[2][...] = adm

    per_group = QROWS_DEV // GROUPS
    labels, sides = [], []
    for s in range(n_src):
        marks = in_ref[s, at_mark : at_mark + 16, :].astype(F32)
        down = jnp.concatenate([marks, jnp.zeros((E - 16, E), F32)], axis=0).T
        for j in range(n_mark):
            at = j * 4 + table * 2
            label = marks[at : at + 1, :] * 256.0 + marks[at + 1 : at + 2, :]
            label = label.astype(jnp.int32) & (per_group - 1)
            if (j + 1) * E > seg:
                label = jnp.where(iota((1, E), 1) + j * E < seg, label, -1)
            labels.append(label)
            group = down[:, at : at + 1].astype(jnp.int32) >> (LOG_GROUP - 8)
            rows = in_ref[s, table * seg + j * E : table * seg + (j + 1) * E, :].astype(F32)
            sides.append(
                jnp.concatenate([jnp.where(group == g, rows, 0.0) for g in range(GROUPS)], axis=1).astype(BF)
            )
    spread = jnp.concatenate(sides, axis=0)
    block = 512
    for b in range(per_group // block):
        wanted = rows_from(block, b * block)
        o = dot(jnp.concatenate([one_hot(wanted, label) for label in labels], axis=1), spread)
        for g in range(GROUPS):
            start = g * per_group + b * block
            outs[0][start : start + block, :] = o[:, g * E : (g + 1) * E]


def doubling(n):
    return [1 << i for i in range(n.bit_length() - 1)]


def swap(x, axis, k):
    n = lax.axis_size(axis)
    return lax.ppermute(x, axis, [(i, i ^ k) for i in range(n)])


def widen_kernel(n_x, n_y, share, at_ref, a_ref, b_ref, *refs):
    out_ref, held_ref, sems = refs[-3:]
    half = a_ref.shape[1]
    copies = []
    for b in range(a_ref.shape[0] // share):
        z = at_ref[2] ^ (((b & 1) << 1) | ((b >> 1) & 1))
        rest = b >> 2
        rows = slice(b * share, (b + 1) * share)
        for side, ref in enumerate((a_ref, b_ref)):
            y, x = (rest % n_y, rest // n_y) if side == 0 else (rest // n_x, rest % n_x)
            row = ((((at_ref[0] ^ x) * 2 + at_ref[1]) * N_Z + z) * n_y + (at_ref[3] ^ y)) * share
            cols = slice(side * half, (side + 1) * half)
            held_ref[rows, cols] = ref[rows, :].astype(F32)
            copy = pltpu.make_async_copy(
                held_ref.at[rows, cols], out_ref.at[pl.ds(pl.multiple_of(row, share), share), cols], sems.at[len(copies)]
            )
            copy.start()
            copies.append(copy)
    for copy in copies:
        copy.wait()


def widen(n_x, n_y, share, at, sides, so_far):
    rows, half = sides[0].shape
    array = pl.BlockSpec(memory_space=pltpu.VMEM)
    more = () if so_far is None else (so_far,)
    alias = {} if so_far is None else {"input_output_aliases": {3: 0}}
    return call(
        functools.partial(widen_kernel, n_x, n_y, share),
        "widen",
        jax.ShapeDtypeStruct((2 * rows, 2 * half), F32),
        rows * half * 2,
        rows * half * 12,
        in_specs=[pl.BlockSpec(memory_space=pltpu.SMEM), array, array] + [pl.BlockSpec(memory_space=pltpu.HBM)] * len(more),
        out_specs=pl.BlockSpec(memory_space=pltpu.HBM),
        scratch_shapes=[
            pltpu.VMEM((rows, 2 * half), F32),
            pltpu.SemaphoreType.DMA((2 * (rows // share),)),
        ],
        **alias,
    )(at, *sides, *more)


def after(x, *others):
    return lax.optimization_barrier((x,) + others)[0]


def local(
    features, w_first, b_first, grad_out, admit, owner, adm_row, q_shard, q_local, r_shard, r_local
):
    n_core = lax.axis_size("core")
    n_dp = lax.axis_size("x") * n_core
    n_y = lax.axis_size("ty")
    n_table = N_Z * n_y
    n_dev = n_dp * n_table
    n_plane = n_dp * n_y
    n_s, width = features.shape
    hidden = w_first.shape[1]
    n_feat = width // E
    count = n_s * n_feat
    cap = max(2, 3 * count // (2 * n_dev))
    seg = N_Z * cap
    n_bias = hidden // E
    share = width // n_dev
    wide = width // N_Z
    plane = ("x", "core", "ty")
    shape = jax.ShapeDtypeStruct
    my_z = lax.axis_index("tz").astype(jnp.int32).reshape(1)
    scalar = pl.BlockSpec(memory_space=pltpu.SMEM)
    array = pl.BlockSpec(memory_space=pltpu.VMEM)

    block = min(256, hidden)
    dpre = call(
        dpre_kernel,
        "dpre",
        shape((n_s, hidden), BF),
        2 * n_s * width * hidden,
        6 * 10**6,
        grid=(hidden // block,),
        in_specs=[
            pl.BlockSpec((n_s, width), lambda i: (0, 0)),
            pl.BlockSpec((width, block), lambda i: (0, i)),
            pl.BlockSpec((1, block), lambda i: (0, i)),
            pl.BlockSpec((n_s, block), lambda i: (0, i)),
        ],
        out_specs=pl.BlockSpec((n_s, block), lambda i: (0, i)),
    )(features, w_first, b_first.reshape(1, hidden), grad_out)

    far = swap(dpre, "tz", 2)
    near = swap(dpre, "tz", 1)
    far = after(far, near)
    sources = [dpre, near, far, swap(far, "tz", 1)]
    admit, owner, adm_row, q_shard, q_local, r_shard, r_local = [
        a.reshape(n_s, n_feat).T for a in (admit, owner, adm_row, q_shard, q_local, r_shard, r_local)
    ]
    cut = call(
        functools.partial(cut_kernel, n_dp, n_y, n_table),
        "cut",
        shape((N_Z, n_s, wide + E), BF),
        10**7,
        2 * 10**6,
    )(
        after(features, dpre),
        jnp.where(admit == 0, q_shard * QROWS_DEV + q_local, -1),
        jnp.where(admit == 0, r_shard * QROWS_DEV + r_local, -1),
        jnp.where(admit == 1, owner * (ADM_DEV * n_table) + adm_row, -1),
    )
    feat_in = lax.all_to_all(cut, "tz", split_axis=0, concat_axis=0, tiled=True)

    look, bias = call(
        lookup_kernel,
        "lookups",
        (shape((N_Z, count, E), BF), shape((2 * n_bias, E), BF)),
        2 * N_Z * n_s * width * hidden,
        7 * 10**6,
        scratch_shapes=[pltpu.VMEM((N_Z * n_s, hidden), BF)],
    )(*sources, w_first)
    feat_in = after(feat_in, look)

    w_part = call(
        functools.partial(w_kernel, n_plane),
        "w_part",
        shape((n_plane, share, hidden), BF),
        2 * N_Z * n_s * wide * hidden,
        3 * 10**6,
        in_specs=[scalar] + [array] * 5,
    )(my_z, feat_in, *sources)
    slots, labels, group = call(
        functools.partial(slots_kernel, n_plane, cap, wide),
        "slots",
        (
            shape((3, N_Z, n_feat, n_s), jnp.int32),
            shape((N_Z, count, E), BF),
            shape((N_Z, n_s, n_feat), F32),
        ),
        10**9,
        3 * 10**6,
        in_specs=[scalar, array],
    )(my_z, after(feat_in, w_part))
    w_part = lax.all_to_all(w_part, plane, split_axis=0, concat_axis=0, tiled=True)

    n_rows = 2 * seg + ADM_DEV + 16 + 2 * n_bias
    chunks = call(
        functools.partial(bucket_kernel, n_plane, cap),
        "buckets",
        shape((n_plane, n_rows, E), BF),
        15 * 10**9,
        4 * 10**7,
        scratch_shapes=[pltpu.VMEM((2, n_plane, seg, E), F32)],
        vmem=36,
    )(look, slots, labels, group, bias)

    w_part = after(w_part, chunks)
    w_own = jnp.sum(w_part.astype(F32), axis=0).astype(BF)
    w_own, chunks = lax.optimization_barrier((w_own, chunks))
    chunks = lax.all_to_all(chunks, plane, split_axis=0, concat_axis=0, tiled=True)

    w_two = jnp.concatenate([w_own, swap(w_own, "tz", 2)], axis=0)
    w_four = jnp.concatenate([w_two, swap(w_two, "tz", 1)], axis=0)
    w_four = after(w_four, chunks)
    sides = [w_four[:, : hidden // 2], w_four[:, hidden // 2 :]]
    over_y = [("ty", k) for k in doubling(n_y)]
    over_x = [("x", k) for k in doubling(n_dp // n_core)]
    last = sides

    def sums(table, chunks):
        outs = (shape((QROWS_DEV, E), F32), shape((n_bias, E), F32), shape((ADM_DEV, E), F32))
        return call(
            functools.partial(sums_kernel, n_plane, seg, n_bias, table),
            ("q_sums", "r_sums")[table],
            outs if table == 0 else outs[:1],
            4 * 10**9,
            4 * 10**6,
            vmem=40,
        )(chunks)

    q_grad, b_grad, adm_grad = sums(0, after(chunks, w_four))
    for i, steps in enumerate(zip(over_y + over_x, over_x + over_y)):
        moved = [swap(side, *step) for side, step in zip(sides, steps)]
        if i == 0:
            moved = [after(part, q_grad) for part in moved]
        sides = [jnp.concatenate(pair, axis=0) for pair in zip(sides, moved)]
        last = sides if i == len(over_x + over_y) - 2 else last
    (r_grad,) = sums(1, after(chunks, *last))
    sides = [after(side, r_grad) for side in sides]
    others = [swap(side, "core", 1) for side in sides]
    at = jnp.stack([lax.axis_index(name) for name in ("x", "core", "tz", "ty")]).astype(jnp.int32)
    n_x = n_dp // n_core
    w_grad = widen(n_x, n_y, share, at, [after(side, r_grad) for side in sides], None)
    flip = at ^ jnp.array([0, 1, 0, 0], jnp.int32)
    w_grad = widen(n_x, n_y, share, flip, others, w_grad)
    return (w_grad, b_grad.reshape(hidden), adm_grad, q_grad, r_grad)


def solution(mesh):
    n_dp, n_table = mesh.devices.shape
    every = ("x", "core", "tz", "ty")
    fine = Mesh(mesh.devices.reshape(n_dp // 2, 2, N_Z, n_table // N_Z), every)
    two, three = P(every, None), P(every, None, None)
    in_specs = (two, P(), P(), two, two, three, two, three, two, three, two)
    out_specs = (P(), P(), two, two, two)
    return jax.shard_map(local, mesh=fine, in_specs=in_specs, out_specs=out_specs, check_vma=False)
```

```python
import functools

import jax
import jax.numpy as jnp
from jax import lax
from jax.experimental import pallas as pl
from jax.experimental.pallas import tpu as pltpu
from jax.sharding import Mesh, PartitionSpec as P

E = 128
ADM_DEV = 128
QROWS_DEV = 4096
N_Z = 4
N_CODE = 8
GROUPS = 4
LOG_ADM = 7
LOG_QROWS = 12
LOG_GROUP = 10
MIB = 1024 * 1024
BF = jnp.bfloat16
F32 = jnp.float32


def iota(shape, dim):
    return lax.broadcasted_iota(jnp.int32, shape, dim)


def dot(a, b, dims=((1,), (0,))):
    return lax.dot_general(a, b, (dims, ((), ())), preferred_element_type=F32)


def one_hot(wanted, row):
    row = jnp.broadcast_to(row, (16, E)).astype(jnp.int16)
    hit = jnp.where(wanted == row[None], jnp.ones((), BF), jnp.zeros((), BF))
    return hit.reshape(wanted.shape[0] * 16, E)


def rows_from(n, base=0):
    return (iota((n, E), 0) + base).astype(jnp.int16).reshape(n // 16, 16, E)


def call(kernel, name, out_shape, flops, traffic, vmem=24, **kwargs):
    return pl.pallas_call(
        kernel,
        out_shape=out_shape,
        compiler_params=pltpu.CompilerParams(vmem_limit_bytes=vmem * MIB),
        cost_estimate=pl.CostEstimate(flops=flops, bytes_accessed=traffic, transcendentals=0),
        name=name,
        **kwargs,
    )


def cut_kernel(n_dp, n_y, n_table, x_ref, q_ref, r_ref, a_ref, out_ref):
    piece = x_ref.shape[1] // (n_dp * N_Z)
    wide = n_dp * piece
    y_bits, table_bits = n_y.bit_length() - 1, n_table.bit_length() - 1

    def in_plane(code, bits, z):
        dev = code >> bits
        here = (code >= 0) & (((dev & (n_table - 1)) >> y_bits) == z)
        return jnp.where(here, ((dev >> table_bits) << y_bits) + (dev & (n_y - 1)), -1)

    for z in range(N_Z):
        for d in range(n_dp):
            at = (d * N_Z + z) * piece
            out_ref[z, :, d * piece : (d + 1) * piece] = x_ref[:, at : at + piece]
        codes = []
        for ref in (q_ref, r_ref):
            low = ref[...] & (QROWS_DEV - 1)
            codes += [in_plane(ref[...], LOG_QROWS, z), low >> 8, low & 255]
        codes += [in_plane(a_ref[...], LOG_ADM, z), a_ref[...] & (ADM_DEV - 1)]
        block = jnp.concatenate(codes, axis=0).astype(F32).astype(BF)
        out_ref[z, :, wide : wide + block.shape[1]] = block


def dpre_kernel(x_ref, w_ref, b_ref, g_ref, out_ref):
    pre = dot(x_ref[...], w_ref[...]) + b_ref[...]
    sig = jax.nn.sigmoid(pre)
    dpre = (g_ref[...].astype(F32) * sig * (1.0 + pre * (1.0 - sig))).astype(BF)
    out_ref[...] = dpre


def slots_kernel(n_dest, cap, wide, z_ref, in_ref, slot_ref, labels_ref, group_ref):
    n_s = in_ref.shape[1]
    n_feat = n_s // N_CODE
    sample = iota((n_s, n_s), 0)
    earlier = (sample < iota((n_s, n_s), 1)).astype(F32).astype(BF)
    ones = jnp.ones((n_s, n_s), BF)
    count = n_dest * n_feat
    feat_bits = n_feat.bit_length() - 1
    at_row, at_col = iota((count, count), 0), iota((count, count), 1)
    before = ((at_row >> feat_bits == at_col >> feat_bits) & (at_col < at_row)).astype(F32).astype(BF)
    half = n_dest // 2
    lane = iota((n_s, E), 1) & 3
    for z in range(N_Z):
        codes = in_ref[z_ref[0] ^ z, :, wide : wide + n_s].astype(F32)
        plane = [codes[i * n_feat : (i + 1) * n_feat, :] for i in range(N_CODE)]
        for table in range(2):
            dest = plane[table * 3]
            hits = jnp.concatenate([jnp.where(dest == d, 1.0, 0.0) for d in range(n_dest)], axis=0)
            hits_bf = hits.astype(BF)
            rank = dot(hits_bf, earlier) + dot(before, dot(hits_bf, ones).astype(BF))
            rank = rank * hits
            total = rank[0:n_feat, :]
            for d in range(1, n_dest):
                total = total + rank[d * n_feat : (d + 1) * n_feat, :]
            slot = jnp.where(dest >= 0, dest * cap + total, -1.0)
            slot_ref[table, z, :, :] = slot.astype(jnp.int32)
        dest = plane[6]
        folded = jnp.where(dest >= half, dest - half, dest)
        slot_ref[2, z, :, :] = jnp.where(dest >= 0, folded * ADM_DEV + plane[7], -1.0).astype(jnp.int32)
        down = codes.T
        group_ref[z] = down[:, 6 * n_feat : 7 * n_feat]
        for f in range(n_feat):
            col = [down[:, i * n_feat + f : i * n_feat + f + 1] for i in (1, 2, 4, 5)]
            one = jnp.where(lane == 0, col[0], jnp.where(lane == 1, col[1], jnp.where(lane == 2, col[2], col[3])))
            labels_ref[z, f * n_s : (f + 1) * n_s, :] = one.astype(BF)


def w_kernel(n_plane, z_ref, x_ref, d0_ref, d1_ref, d2_ref, d3_ref, out_ref):
    wide = x_ref.shape[2] - E
    share = wide // n_plane
    x = jnp.concatenate([x_ref[z_ref[0] ^ z, :, 0:wide] for z in range(N_Z)], axis=0)
    d = jnp.concatenate([ref[...] for ref in (d0_ref, d1_ref, d2_ref, d3_ref)], axis=0)
    res = dot(x, d, ((0,), (0,))).astype(BF)
    for p in range(n_plane):
        out_ref[p] = res[p * share : (p + 1) * share, :]


def lookup_kernel(d0_ref, d1_ref, d2_ref, d3_ref, w_ref, out_ref, bias_ref, d_ref):
    n_s, depth = d0_ref.shape
    for z, ref in enumerate((d0_ref, d1_ref, d2_ref, d3_ref)):
        d_ref[z * n_s : (z + 1) * n_s, :] = ref[...]
    for step in range(w_ref.shape[0] // (2 * E)):
        res = dot(d_ref[...], w_ref[step * 2 * E : (step + 1) * 2 * E, :], ((1,), (1,))).astype(BF)
        for z in range(N_Z):
            for h in range(2):
                row = (step * 2 + h) * n_s
                out_ref[z, row : row + n_s, :] = res[z * n_s : (z + 1) * n_s, h * E : (h + 1) * E]
    bias = jnp.sum(d_ref[...].astype(F32), axis=0, keepdims=True)
    high = bias.astype(BF)
    low = (bias - high.astype(F32)).astype(BF)
    bias_ref[...] = jnp.concatenate(
        [part[:, i * E : (i + 1) * E].astype(F32) for part in (high, low) for i in range(depth // E)], axis=0
    ).astype(BF)


def bucket_kernel(n_dest, cap, look_ref, slot_ref, labels_ref, group_ref, bias_ref, out_ref, mark_ref):
    n_feat, n_s = slot_ref.shape[2:]
    seg = N_Z * cap
    n_mark = -(-seg // E)
    half = n_dest // 2

    slots = n_dest * cap
    wanted = rows_from(slots)
    for z in range(N_Z):
        for which in range(2):
            hits = [one_hot(wanted, slot_ref[which, z, f : f + 1, :]) for f in range(n_feat)]
            o = dot(jnp.concatenate(hits, axis=1), jnp.concatenate([look_ref[z], labels_ref[z]], axis=1))
            for d in range(n_dest):
                rows = o[d * cap : (d + 1) * cap, :]
                out_ref[d, which * seg + z * cap : which * seg + (z + 1) * cap, :] = rows[:, 0:E].astype(BF)
                mark_ref[which, d, z * cap : (z + 1) * cap, :] = rows[:, E : 2 * E]

    tall = half * ADM_DEV
    wanted = rows_from(tall)
    o = jnp.zeros((tall, 2 * E), F32)
    for z in range(N_Z):
        hits = [one_hot(wanted, slot_ref[2, z, f : f + 1, :]) for f in range(n_feat)]
        sides = []
        for f in range(n_feat):
            upper = group_ref[z, :, f : f + 1] >= half
            v = look_ref[z, f * n_s : (f + 1) * n_s, :].astype(F32)
            sides.append(jnp.concatenate([jnp.where(upper, 0.0, v), jnp.where(upper, v, 0.0)], axis=1).astype(BF))
        o = o + dot(jnp.concatenate(hits, axis=1), jnp.concatenate(sides, axis=0))
    for d in range(n_dest):
        at = d % half * ADM_DEV
        side = d // half * E
        out_ref[d, 2 * seg : 2 * seg + ADM_DEV, :] = o[at : at + ADM_DEV, side : side + E].astype(BF)

    at_mark = 2 * seg + ADM_DEV

    def finish(d, carry):
        lane = iota((seg, E), 1) & 3
        mixed = jnp.where(lane < 2, mark_ref[0, d], mark_ref[1, d])
        if seg % E:
            mixed = jnp.concatenate([mixed, jnp.zeros((n_mark * E - seg, E), F32)], axis=0)
        rows = iota((16, E), 0) >> 2
        marks = jnp.zeros((16, E), F32)
        for j in range(n_mark):
            across = mixed[j * E : (j + 1) * E, :].T
            marks = jnp.where(rows == j, across[0:16, :], marks)
        out_ref[d, at_mark : at_mark + 16, :] = marks.astype(BF)
        out_ref[d, at_mark + 16 : at_mark + 16 + bias_ref.shape[0], :] = bias_ref[...]
        return carry

    lax.fori_loop(0, n_dest, finish, 0)


def sums_kernel(n_src, seg, n_bias, table, in_ref, *outs):
    n_mark = -(-seg // E)
    at_mark = 2 * seg + ADM_DEV
    if table == 0:
        adm = jnp.zeros((ADM_DEV, E), F32)
        bias = jnp.zeros((2 * n_bias, E), F32)
        for s in range(n_src):
            adm = adm + in_ref[s, 2 * seg : at_mark, :].astype(F32)
            bias = bias + in_ref[s, at_mark + 16 : at_mark + 16 + 2 * n_bias, :].astype(F32)
        outs[1][...] = bias[0:n_bias, :] + bias[n_bias:, :]
        outs[2][...] = adm

    per_group = QROWS_DEV // GROUPS
    labels, sides = [], []
    for s in range(n_src):
        marks = in_ref[s, at_mark : at_mark + 16, :].astype(F32)
        down = jnp.concatenate([marks, jnp.zeros((E - 16, E), F32)], axis=0).T
        for j in range(n_mark):
            at = j * 4 + table * 2
            label = marks[at : at + 1, :] * 256.0 + marks[at + 1 : at + 2, :]
            label = label.astype(jnp.int32) & (per_group - 1)
            if (j + 1) * E > seg:
                label = jnp.where(iota((1, E), 1) + j * E < seg, label, -1)
            labels.append(label)
            group = down[:, at : at + 1].astype(jnp.int32) >> (LOG_GROUP - 8)
            rows = in_ref[s, table * seg + j * E : table * seg + (j + 1) * E, :].astype(F32)
            sides.append(
                jnp.concatenate([jnp.where(group == g, rows, 0.0) for g in range(GROUPS)], axis=1).astype(BF)
            )
    spread = jnp.concatenate(sides, axis=0)
    block = 512
    for b in range(per_group // block):
        wanted = rows_from(block, b * block)
        o = dot(jnp.concatenate([one_hot(wanted, label) for label in labels], axis=1), spread)
        for g in range(GROUPS):
            start = g * per_group + b * block
            outs[0][start : start + block, :] = o[:, g * E : (g + 1) * E]


def doubling(n):
    return [1 << i for i in range(n.bit_length() - 1)]


def swap(x, axis, k):
    n = lax.axis_size(axis)
    return lax.ppermute(x, axis, [(i, i ^ k) for i in range(n)])


def widen_kernel(n_x, n_y, share, at_ref, a_ref, b_ref, *refs):
    out_ref, held_ref, sems = refs[-3:]
    half = a_ref.shape[1]
    copies = []
    for b in range(a_ref.shape[0] // share):
        rows = slice(b * share, (b + 1) * share)
        for side, (ref, first) in enumerate(((a_ref, n_y), (b_ref, n_x))):
            low, mid, high = b % first, b // first % N_Z, b // (first * N_Z)
            y, x = (low, high) if side == 0 else (high, low)
            z = at_ref[2] ^ (((mid & 1) << 1) | (mid >> 1))
            row = ((((at_ref[0] ^ x) * 2 + at_ref[1]) * N_Z + z) * n_y + (at_ref[3] ^ y)) * share
            cols = slice(side * half, (side + 1) * half)
            held_ref[rows, cols] = ref[rows, :].astype(F32)
            copy = pltpu.make_async_copy(
                held_ref.at[rows, cols], out_ref.at[pl.ds(pl.multiple_of(row, share), share), cols], sems.at[len(copies)]
            )
            copy.start()
            copies.append(copy)
    for copy in copies:
        copy.wait()


def widen(n_x, n_y, share, at, sides, so_far):
    rows, half = sides[0].shape
    array = pl.BlockSpec(memory_space=pltpu.VMEM)
    more = () if so_far is None else (so_far,)
    alias = {} if so_far is None else {"input_output_aliases": {3: 0}}
    return call(
        functools.partial(widen_kernel, n_x, n_y, share),
        "widen",
        jax.ShapeDtypeStruct((2 * rows, 2 * half), F32),
        rows * half * 2,
        rows * half * 12,
        in_specs=[pl.BlockSpec(memory_space=pltpu.SMEM), array, array] + [pl.BlockSpec(memory_space=pltpu.HBM)] * len(more),
        out_specs=pl.BlockSpec(memory_space=pltpu.HBM),
        scratch_shapes=[
            pltpu.VMEM((rows, 2 * half), F32),
            pltpu.SemaphoreType.DMA((2 * (rows // share),)),
        ],
        **alias,
    )(at, *sides, *more)


def after(x, *others):
    return lax.optimization_barrier((x,) + others)[0]


def local(
    features, w_first, b_first, grad_out, admit, owner, adm_row, q_shard, q_local, r_shard, r_local
):
    n_core = lax.axis_size("core")
    n_dp = lax.axis_size("x") * n_core
    n_y = lax.axis_size("ty")
    n_table = N_Z * n_y
    n_dev = n_dp * n_table
    n_plane = n_dp * n_y
    n_s, width = features.shape
    hidden = w_first.shape[1]
    n_feat = width // E
    count = n_s * n_feat
    cap = max(2, 3 * count // (2 * n_dev))
    seg = N_Z * cap
    n_bias = hidden // E
    share = width // n_dev
    wide = width // N_Z
    plane = ("x", "core", "ty")
    shape = jax.ShapeDtypeStruct
    my_z = lax.axis_index("tz").astype(jnp.int32).reshape(1)
    scalar = pl.BlockSpec(memory_space=pltpu.SMEM)
    array = pl.BlockSpec(memory_space=pltpu.VMEM)

    block = min(256, hidden)
    dpre = call(
        dpre_kernel,
        "dpre",
        shape((n_s, hidden), BF),
        2 * n_s * width * hidden,
        6 * 10**6,
        grid=(hidden // block,),
        in_specs=[
            pl.BlockSpec((n_s, width), lambda i: (0, 0)),
            pl.BlockSpec((width, block), lambda i: (0, i)),
            pl.BlockSpec((1, block), lambda i: (0, i)),
            pl.BlockSpec((n_s, block), lambda i: (0, i)),
        ],
        out_specs=pl.BlockSpec((n_s, block), lambda i: (0, i)),
        vmem=58,
    )(features, w_first, b_first.reshape(1, hidden), grad_out)

    far = swap(dpre, "tz", 2)
    near = swap(dpre, "tz", 1)
    far = after(far, near)
    sources = [dpre, near, far, swap(far, "tz", 1)]
    admit, owner, adm_row, q_shard, q_local, r_shard, r_local = [
        a.reshape(n_s, n_feat).T for a in (admit, owner, adm_row, q_shard, q_local, r_shard, r_local)
    ]
    cut = call(
        functools.partial(cut_kernel, n_dp, n_y, n_table),
        "cut",
        shape((N_Z, n_s, wide + E), BF),
        10**7,
        2 * 10**6,
    )(
        after(features, dpre),
        jnp.where(admit == 0, q_shard * QROWS_DEV + q_local, -1),
        jnp.where(admit == 0, r_shard * QROWS_DEV + r_local, -1),
        jnp.where(admit == 1, owner * (ADM_DEV * n_table) + adm_row, -1),
    )
    feat_in = lax.all_to_all(after(cut, near), "tz", split_axis=0, concat_axis=0, tiled=True)

    w_part = call(
        functools.partial(w_kernel, n_plane),
        "w_part",
        shape((n_plane, share, hidden), BF),
        2 * N_Z * n_s * wide * hidden,
        3 * 10**6,
        in_specs=[scalar] + [array] * 5,
    )(my_z, feat_in, *sources)
    look, bias = call(
        lookup_kernel,
        "lookups",
        (shape((N_Z, count, E), BF), shape((2 * n_bias, E), BF)),
        2 * N_Z * n_s * width * hidden,
        7 * 10**6,
        scratch_shapes=[pltpu.VMEM((N_Z * n_s, hidden), BF)],
    )(*sources[:3], after(sources[3], w_part), w_first)
    slots, labels, group = call(
        functools.partial(slots_kernel, n_plane, cap, wide),
        "slots",
        (
            shape((3, N_Z, n_feat, n_s), jnp.int32),
            shape((N_Z, count, E), BF),
            shape((N_Z, n_s, n_feat), F32),
        ),
        10**9,
        3 * 10**6,
        in_specs=[scalar, array],
    )(my_z, after(feat_in, w_part))
    w_part = lax.all_to_all(w_part, plane, split_axis=0, concat_axis=0, tiled=True)

    n_rows = 2 * seg + ADM_DEV + 16 + 2 * n_bias
    chunks = call(
        functools.partial(bucket_kernel, n_plane, cap),
        "buckets",
        shape((n_plane, n_rows, E), BF),
        15 * 10**9,
        4 * 10**7,
        scratch_shapes=[pltpu.VMEM((2, n_plane, seg, E), F32)],
        vmem=28,
    )(look, slots, labels, group, bias)

    w_part = after(w_part, chunks)
    w_own = jnp.sum(w_part.astype(F32), axis=0).astype(BF)
    w_own, chunks = lax.optimization_barrier((w_own, chunks))
    chunks = lax.all_to_all(chunks, plane, split_axis=0, concat_axis=0, tiled=True)

    def spread(x, steps):
        for step in steps:
            x = jnp.concatenate([x, swap(x, *step)], axis=0)
        return x

    over_y = [("ty", k) for k in doubling(n_y)]
    over_x = [("x", k) for k in doubling(n_dp // n_core)]
    side = hidden // 2
    w_rows = jnp.concatenate([spread(w_own[:, :side], over_y), spread(w_own[:, side:], over_x)], axis=1)
    w_rows = after(spread(w_rows, [("tz", 2), ("tz", 1)]), chunks)

    def sums(table, chunks):
        outs = (shape((QROWS_DEV, E), F32), shape((n_bias, E), F32), shape((ADM_DEV, E), F32))
        return call(
            functools.partial(sums_kernel, n_plane, seg, n_bias, table),
            ("q_sums", "r_sums")[table],
            outs if table == 0 else outs[:1],
            4 * 10**9,
            4 * 10**6,
            vmem=40,
        )(chunks)

    q_grad, b_grad, adm_grad = sums(0, after(chunks, w_rows))
    (r_grad,) = sums(1, after(chunks, q_grad))
    sides = []
    for x, steps in ((w_rows[:, :side], over_x), (w_rows[:, side:], over_y)):
        x = spread(x, steps[:-1])
        sides.append(jnp.concatenate([x, after(swap(x, *steps[-1]), r_grad)], axis=0))
    others = [swap(x, "core", 1) for x in sides]
    at = jnp.stack([lax.axis_index(name) for name in ("x", "core", "tz", "ty")]).astype(jnp.int32)
    n_x = n_dp // n_core
    w_grad = widen(n_x, n_y, share, at, sides, None)
    flip = at ^ jnp.array([0, 1, 0, 0], jnp.int32)
    w_grad = widen(n_x, n_y, share, flip, others, w_grad)
    return (w_grad, b_grad.reshape(hidden), adm_grad, q_grad, r_grad)


def solution(mesh):
    n_dp, n_table = mesh.devices.shape
    every = ("x", "core", "tz", "ty")
    fine = Mesh(mesh.devices.reshape(n_dp // 2, 2, N_Z, n_table // N_Z), every)
    two, three = P(every, None), P(every, None, None)
    in_specs = (two, P(), P(), two, two, three, two, three, two, three, two)
    out_specs = (P(), P(), two, two, two)
    return jax.shard_map(local, mesh=fine, in_specs=in_specs, out_specs=out_specs, check_vma=False)
```

```python
import functools

import jax
import jax.numpy as jnp
from jax import lax
from jax.experimental import pallas as pl
from jax.experimental.pallas import tpu as pltpu
from jax.sharding import Mesh, PartitionSpec as P

E = 128
ADM_DEV = 128
QROWS_DEV = 4096
N_Z = 4
N_CODE = 8
GROUPS = 4
LOG_ADM = 7
LOG_QROWS = 12
LOG_GROUP = 10
MIB = 1024 * 1024
BF = jnp.bfloat16
F32 = jnp.float32


def iota(shape, dim):
    return lax.broadcasted_iota(jnp.int32, shape, dim)


def dot(a, b, dims=((1,), (0,))):
    return lax.dot_general(a, b, (dims, ((), ())), preferred_element_type=F32)


def one_hot(wanted, row):
    row = jnp.broadcast_to(row, (16, E)).astype(jnp.int16)
    hit = jnp.where(wanted == row[None], jnp.ones((), BF), jnp.zeros((), BF))
    return hit.reshape(wanted.shape[0] * 16, E)


def rows_from(n, base=0):
    return (iota((n, E), 0) + base).astype(jnp.int16).reshape(n // 16, 16, E)


def call(kernel, name, out_shape, flops, traffic, vmem=24, **kwargs):
    return pl.pallas_call(
        kernel,
        out_shape=out_shape,
        compiler_params=pltpu.CompilerParams(vmem_limit_bytes=vmem * MIB),
        cost_estimate=pl.CostEstimate(flops=flops, bytes_accessed=traffic, transcendentals=0),
        name=name,
        **kwargs,
    )


def codes_kernel(n_y, n_table, z_ref, q_ref, r_ref, a_ref, own_ref, near_ref, far_ref):
    y_bits, table_bits = n_y.bit_length() - 1, n_table.bit_length() - 1

    def in_plane(code, bits, z):
        dev = code >> bits
        here = (code >= 0) & (((dev & (n_table - 1)) >> y_bits) == z)
        return jnp.where(here, ((dev >> table_bits) << y_bits) + (dev & (n_y - 1)), -1)

    for k in range(N_Z):
        z = z_ref[0] ^ k
        codes = []
        for ref in (q_ref, r_ref):
            low = ref[...] & (QROWS_DEV - 1)
            codes += [in_plane(ref[...], LOG_QROWS, z), low >> 8, low & 255]
        codes += [in_plane(a_ref[...], LOG_ADM, z), a_ref[...] & (ADM_DEV - 1)]
        block = jnp.concatenate(codes, axis=0).astype(F32).astype(BF)
        if k < 2:
            (own_ref, near_ref)[k][...] = block
        else:
            far_ref[k - 2] = block


def cut_kernel(n_dp, x_ref, out_ref):
    piece = x_ref.shape[1] // (n_dp * N_Z)
    for z in range(N_Z):
        for d in range(n_dp):
            at = (d * N_Z + z) * piece
            out_ref[z, :, d * piece : (d + 1) * piece] = x_ref[:, at : at + piece]


def dpre_kernel(x_ref, w_ref, b_ref, g_ref, out_ref, acc_ref):
    step = pl.program_id(0)
    part = dot(x_ref[...], w_ref[...])

    @pl.when(step == 0)
    def _():
        acc_ref[...] = part

    @pl.when(step > 0)
    def _():
        acc_ref[...] += part

    @pl.when(step == pl.num_programs(0) - 1)
    def _():
        pre = acc_ref[...] + b_ref[...]
        sig = jax.nn.sigmoid(pre)
        out_ref[...] = (g_ref[...].astype(F32) * sig * (1.0 + pre * (1.0 - sig))).astype(BF)


def slots_kernel(n_dest, cap, own_ref, near_ref, far_ref, last_ref, slot_ref, labels_ref, group_ref):
    n_s = own_ref.shape[1]
    n_feat = own_ref.shape[0] // N_CODE
    sample = iota((n_s, n_s), 0)
    earlier = (sample < iota((n_s, n_s), 1)).astype(F32).astype(BF)
    ones = jnp.ones((n_s, n_s), BF)
    count = n_dest * n_feat
    feat_bits = n_feat.bit_length() - 1
    at_row, at_col = iota((count, count), 0), iota((count, count), 1)
    before = ((at_row >> feat_bits == at_col >> feat_bits) & (at_col < at_row)).astype(F32).astype(BF)
    half = n_dest // 2
    lane = iota((n_s, E), 1) & 3
    for z in range(N_Z):
        codes = (own_ref[...], near_ref[...], far_ref[0], last_ref[...])[z].astype(F32)
        plane = [codes[i * n_feat : (i + 1) * n_feat, :] for i in range(N_CODE)]
        for table in range(2):
            dest = plane[table * 3]
            hits = jnp.concatenate([jnp.where(dest == d, 1.0, 0.0) for d in range(n_dest)], axis=0)
            hits_bf = hits.astype(BF)
            rank = dot(hits_bf, earlier) + dot(before, dot(hits_bf, ones).astype(BF))
            rank = rank * hits
            total = rank[0:n_feat, :]
            for d in range(1, n_dest):
                total = total + rank[d * n_feat : (d + 1) * n_feat, :]
            slot = jnp.where(dest >= 0, dest * cap + total, -1.0)
            slot_ref[table, z, :, :] = slot.astype(jnp.int32)
        dest = plane[6]
        folded = jnp.where(dest >= half, dest - half, dest)
        slot_ref[2, z, :, :] = jnp.where(dest >= 0, folded * ADM_DEV + plane[7], -1.0).astype(jnp.int32)
        down = codes.T
        group_ref[z] = down[:, 6 * n_feat : 7 * n_feat]
        for f in range(n_feat):
            col = [down[:, i * n_feat + f : i * n_feat + f + 1] for i in (1, 2, 4, 5)]
            one = jnp.where(lane == 0, col[0], jnp.where(lane == 1, col[1], jnp.where(lane == 2, col[2], col[3])))
            labels_ref[z, f * n_s : (f + 1) * n_s, :] = one.astype(BF)


def w_kernel(n_plane, z_ref, x_ref, d0_ref, d1_ref, d2_ref, d3_ref, out_ref):
    wide = x_ref.shape[2]
    share = wide // n_plane
    x = jnp.concatenate([x_ref[z_ref[0] ^ z, :, 0:wide] for z in range(N_Z)], axis=0)
    d = jnp.concatenate([ref[...] for ref in (d0_ref, d1_ref, d2_ref, d3_ref)], axis=0)
    res = dot(x, d, ((0,), (0,))).astype(BF)
    for p in range(n_plane):
        out_ref[p] = res[p * share : (p + 1) * share, :]


def lookup_kernel(d0_ref, d1_ref, d2_ref, d3_ref, w_ref, out_ref, bias_ref, d_ref):
    n_s, depth = d0_ref.shape
    for z, ref in enumerate((d0_ref, d1_ref, d2_ref, d3_ref)):
        d_ref[z * n_s : (z + 1) * n_s, :] = ref[...]
    for step in range(w_ref.shape[0] // (2 * E)):
        res = dot(d_ref[...], w_ref[step * 2 * E : (step + 1) * 2 * E, :], ((1,), (1,))).astype(BF)
        for z in range(N_Z):
            for h in range(2):
                row = (step * 2 + h) * n_s
                out_ref[z, row : row + n_s, :] = res[z * n_s : (z + 1) * n_s, h * E : (h + 1) * E]
    bias = jnp.sum(d_ref[...].astype(F32), axis=0, keepdims=True)
    high = bias.astype(BF)
    low = (bias - high.astype(F32)).astype(BF)
    bias_ref[...] = jnp.concatenate(
        [part[:, i * E : (i + 1) * E].astype(F32) for part in (high, low) for i in range(depth // E)], axis=0
    ).astype(BF)


def bucket_kernel(n_dest, cap, look_ref, slot_ref, labels_ref, group_ref, bias_ref, out_ref, mark_ref):
    n_feat, n_s = slot_ref.shape[2:]
    seg = N_Z * cap
    n_mark = -(-seg // E)
    half = n_dest // 2

    slots = n_dest * cap
    wanted = rows_from(slots)
    for z in range(N_Z):
        for which in range(2):
            hits = [one_hot(wanted, slot_ref[which, z, f : f + 1, :]) for f in range(n_feat)]
            o = dot(jnp.concatenate(hits, axis=1), jnp.concatenate([look_ref[z], labels_ref[z]], axis=1))
            for d in range(n_dest):
                rows = o[d * cap : (d + 1) * cap, :]
                out_ref[d, which * seg + z * cap : which * seg + (z + 1) * cap, :] = rows[:, 0:E].astype(BF)
                mark_ref[which, d, z * cap : (z + 1) * cap, :] = rows[:, E : 2 * E]

    tall = half * ADM_DEV
    wanted = rows_from(tall)
    o = jnp.zeros((tall, 2 * E), F32)
    for z in range(N_Z):
        hits = [one_hot(wanted, slot_ref[2, z, f : f + 1, :]) for f in range(n_feat)]
        sides = []
        for f in range(n_feat):
            upper = group_ref[z, :, f : f + 1] >= half
            v = look_ref[z, f * n_s : (f + 1) * n_s, :].astype(F32)
            sides.append(jnp.concatenate([jnp.where(upper, 0.0, v), jnp.where(upper, v, 0.0)], axis=1).astype(BF))
        o = o + dot(jnp.concatenate(hits, axis=1), jnp.concatenate(sides, axis=0))
    for d in range(n_dest):
        at = d % half * ADM_DEV
        side = d // half * E
        out_ref[d, 2 * seg : 2 * seg + ADM_DEV, :] = o[at : at + ADM_DEV, side : side + E].astype(BF)

    at_mark = 2 * seg + ADM_DEV

    def finish(d, carry):
        lane = iota((seg, E), 1) & 3
        mixed = jnp.where(lane < 2, mark_ref[0, d], mark_ref[1, d])
        if seg % E:
            mixed = jnp.concatenate([mixed, jnp.zeros((n_mark * E - seg, E), F32)], axis=0)
        rows = iota((16, E), 0) >> 2
        marks = jnp.zeros((16, E), F32)
        for j in range(n_mark):
            across = mixed[j * E : (j + 1) * E, :].T
            marks = jnp.where(rows == j, across[0:16, :], marks)
        out_ref[d, at_mark : at_mark + 16, :] = marks.astype(BF)
        out_ref[d, at_mark + 16 : at_mark + 16 + bias_ref.shape[0], :] = bias_ref[...]
        return carry

    lax.fori_loop(0, n_dest, finish, 0)


def sums_kernel(n_src, seg, n_bias, table, in_ref, *outs):
    n_mark = -(-seg // E)
    at_mark = 2 * seg + ADM_DEV
    if table == 0:
        adm = jnp.zeros((ADM_DEV, E), F32)
        bias = jnp.zeros((2 * n_bias, E), F32)
        for s in range(n_src):
            adm = adm + in_ref[s, 2 * seg : at_mark, :].astype(F32)
            bias = bias + in_ref[s, at_mark + 16 : at_mark + 16 + 2 * n_bias, :].astype(F32)
        outs[1][...] = bias[0:n_bias, :] + bias[n_bias:, :]
        outs[2][...] = adm

    per_group = QROWS_DEV // GROUPS
    labels, sides = [], []
    for s in range(n_src):
        marks = in_ref[s, at_mark : at_mark + 16, :].astype(F32)
        down = jnp.concatenate([marks, jnp.zeros((E - 16, E), F32)], axis=0).T
        for j in range(n_mark):
            at = j * 4 + table * 2
            label = marks[at : at + 1, :] * 256.0 + marks[at + 1 : at + 2, :]
            label = label.astype(jnp.int32) & (per_group - 1)
            if (j + 1) * E > seg:
                label = jnp.where(iota((1, E), 1) + j * E < seg, label, -1)
            labels.append(label)
            group = down[:, at : at + 1].astype(jnp.int32) >> (LOG_GROUP - 8)
            rows = in_ref[s, table * seg + j * E : table * seg + (j + 1) * E, :].astype(F32)
            sides.append(
                jnp.concatenate([jnp.where(group == g, rows, 0.0) for g in range(GROUPS)], axis=1).astype(BF)
            )
    spread = jnp.concatenate(sides, axis=0)
    block = 512
    for b in range(per_group // block):
        wanted = rows_from(block, b * block)
        o = dot(jnp.concatenate([one_hot(wanted, label) for label in labels], axis=1), spread)
        for g in range(GROUPS):
            start = g * per_group + b * block
            outs[0][start : start + block, :] = o[:, g * E : (g + 1) * E]


def doubling(n):
    return [1 << i for i in range(n.bit_length() - 1)]


def swap(x, axis, k):
    n = lax.axis_size(axis)
    return lax.ppermute(x, axis, [(i, i ^ k) for i in range(n)])


def widen_kernel(n_x, n_y, share, at_ref, a_ref, b_ref, *refs):
    out_ref, held_ref, sems = refs[-3:]
    half = a_ref.shape[1]
    copies = []
    for b in range(a_ref.shape[0] // share):
        z = at_ref[2] ^ (((b & 1) << 1) | ((b >> 1) & 1))
        rest = b >> 2
        rows = slice(b * share, (b + 1) * share)
        for side, ref in enumerate((a_ref, b_ref)):
            y, x = (rest % n_y, rest // n_y) if side == 0 else (rest // n_x, rest % n_x)
            row = ((((at_ref[0] ^ x) * 2 + at_ref[1]) * N_Z + z) * n_y + (at_ref[3] ^ y)) * share
            cols = slice(side * half, (side + 1) * half)
            held_ref[rows, cols] = ref[rows, :].astype(F32)
            copy = pltpu.make_async_copy(
                held_ref.at[rows, cols], out_ref.at[pl.ds(pl.multiple_of(row, share), share), cols], sems.at[len(copies)]
            )
            copy.start()
            copies.append(copy)
    for copy in copies:
        copy.wait()


def widen(n_x, n_y, share, at, sides, so_far):
    rows, half = sides[0].shape
    array = pl.BlockSpec(memory_space=pltpu.VMEM)
    more = () if so_far is None else (so_far,)
    alias = {} if so_far is None else {"input_output_aliases": {3: 0}}
    return call(
        functools.partial(widen_kernel, n_x, n_y, share),
        "widen",
        jax.ShapeDtypeStruct((2 * rows, 2 * half), F32),
        rows * half * 2,
        rows * half * 12,
        in_specs=[pl.BlockSpec(memory_space=pltpu.SMEM), array, array] + [pl.BlockSpec(memory_space=pltpu.HBM)] * len(more),
        out_specs=pl.BlockSpec(memory_space=pltpu.HBM),
        scratch_shapes=[
            pltpu.VMEM((rows, 2 * half), F32),
            pltpu.SemaphoreType.DMA((2 * (rows // share),)),
        ],
        **alias,
    )(at, *sides, *more)


def after(x, *others):
    return lax.optimization_barrier((x,) + others)[0]


def local(
    features, w_first, b_first, grad_out, admit, owner, adm_row, q_shard, q_local, r_shard, r_local
):
    n_core = lax.axis_size("core")
    n_dp = lax.axis_size("x") * n_core
    n_y = lax.axis_size("ty")
    n_table = N_Z * n_y
    n_dev = n_dp * n_table
    n_plane = n_dp * n_y
    n_s, width = features.shape
    hidden = w_first.shape[1]
    n_feat = width // E
    count = n_s * n_feat
    cap = max(2, 3 * count // (2 * n_dev))
    seg = N_Z * cap
    n_bias = hidden // E
    share = width // n_dev
    wide = width // N_Z
    plane = ("x", "core", "ty")
    shape = jax.ShapeDtypeStruct
    my_z = lax.axis_index("tz").astype(jnp.int32).reshape(1)
    scalar = pl.BlockSpec(memory_space=pltpu.SMEM)
    array = pl.BlockSpec(memory_space=pltpu.VMEM)

    admit, owner, adm_row, q_shard, q_local, r_shard, r_local = [
        a.reshape(n_s, n_feat).T for a in (admit, owner, adm_row, q_shard, q_local, r_shard, r_local)
    ]
    n_code = N_CODE * n_feat
    own_codes, near_codes, far_codes = call(
        functools.partial(codes_kernel, n_y, n_table),
        "codes",
        (shape((n_code, n_s), BF), shape((n_code, n_s), BF), shape((2, n_code, n_s), BF)),
        10**6,
        2 * 10**5,
        in_specs=[scalar] + [array] * 3,
    )(
        my_z,
        jnp.where(admit == 0, q_shard * QROWS_DEV + q_local, -1),
        jnp.where(admit == 0, r_shard * QROWS_DEV + r_local, -1),
        jnp.where(admit == 1, owner * (ADM_DEV * n_table) + adm_row, -1),
    )
    far_codes = swap(far_codes, "tz", 2)
    near_codes = swap(near_codes, "tz", 1)
    last_codes = swap(after(far_codes[1], near_codes), "tz", 1)

    block = width // 4
    dpre = call(
        dpre_kernel,
        "dpre",
        shape((n_s, hidden), BF),
        2 * n_s * width * hidden,
        6 * 10**6,
        grid=(width // block,),
        in_specs=[
            pl.BlockSpec((n_s, block), lambda i: (0, i)),
            pl.BlockSpec((block, hidden), lambda i: (i, 0)),
            pl.BlockSpec((1, hidden), lambda i: (0, 0)),
            pl.BlockSpec((n_s, hidden), lambda i: (0, 0)),
        ],
        out_specs=pl.BlockSpec((n_s, hidden), lambda i: (0, 0)),
        scratch_shapes=[pltpu.VMEM((n_s, hidden), F32)],
        vmem=56,
    )(after(features, own_codes), w_first, b_first.reshape(1, hidden), grad_out)

    far = swap(dpre, "tz", 2)
    near = swap(dpre, "tz", 1)
    far = after(far, near)
    sources = [dpre, near, far, swap(far, "tz", 1)]

    cut = call(
        functools.partial(cut_kernel, n_dp), "cut", shape((N_Z, n_s, wide), BF), 10**6, 2 * 10**6
    )(after(features, dpre))
    feat_in = lax.all_to_all(after(cut, far), "tz", split_axis=0, concat_axis=0, tiled=True)

    slots, labels, group = call(
        functools.partial(slots_kernel, n_plane, cap),
        "slots",
        (
            shape((3, N_Z, n_feat, n_s), jnp.int32),
            shape((N_Z, count, E), BF),
            shape((N_Z, n_s, n_feat), F32),
        ),
        10**9,
        3 * 10**6,
    )(own_codes, near_codes, far_codes, last_codes)
    look, bias = call(
        lookup_kernel,
        "lookups",
        (shape((N_Z, count, E), BF), shape((2 * n_bias, E), BF)),
        2 * N_Z * n_s * width * hidden,
        7 * 10**6,
        scratch_shapes=[pltpu.VMEM((N_Z * n_s, hidden), BF)],
    )(*sources, w_first)
    feat_in = after(feat_in, look, slots)

    w_part = call(
        functools.partial(w_kernel, n_plane),
        "w_part",
        shape((n_plane, share, hidden), BF),
        2 * N_Z * n_s * wide * hidden,
        3 * 10**6,
        in_specs=[scalar] + [array] * 5,
    )(my_z, feat_in, *sources)
    look = after(look, w_part)
    w_part = lax.all_to_all(w_part, plane, split_axis=0, concat_axis=0, tiled=True)

    n_rows = 2 * seg + ADM_DEV + 16 + 2 * n_bias
    chunks = call(
        functools.partial(bucket_kernel, n_plane, cap),
        "buckets",
        shape((n_plane, n_rows, E), BF),
        15 * 10**9,
        4 * 10**7,
        scratch_shapes=[pltpu.VMEM((2, n_plane, seg, E), F32)],
        vmem=28,
    )(look, slots, labels, group, bias)

    w_part = after(w_part, chunks)
    w_own = jnp.sum(w_part.astype(F32), axis=0).astype(BF)
    chunks = lax.all_to_all(chunks, plane, split_axis=0, concat_axis=0, tiled=True)

    w_two = jnp.concatenate([w_own, swap(w_own, "tz", 2)], axis=0)
    w_four = jnp.concatenate([w_two, swap(w_two, "tz", 1)], axis=0)
    w_four = after(w_four, chunks)
    sides = [w_four[:, : hidden // 2], w_four[:, hidden // 2 :]]
    over_y = [("ty", k) for k in doubling(n_y)]
    over_x = [("x", k) for k in doubling(n_dp // n_core)]
    last = sides

    def sums(table, chunks):
        outs = (shape((QROWS_DEV, E), F32), shape((n_bias, E), F32), shape((ADM_DEV, E), F32))
        return call(
            functools.partial(sums_kernel, n_plane, seg, n_bias, table),
            ("q_sums", "r_sums")[table],
            outs if table == 0 else outs[:1],
            4 * 10**9,
            4 * 10**6,
            vmem=40,
        )(chunks)

    q_grad, b_grad, adm_grad = sums(0, after(chunks, w_four))
    for i, steps in enumerate(zip(over_y + over_x, over_x + over_y)):
        moved = [swap(side, *step) for side, step in zip(sides, steps)]
        if i == 0:
            moved = [after(part, q_grad) for part in moved]
        sides = [jnp.concatenate(pair, axis=0) for pair in zip(sides, moved)]
        last = sides if i == len(over_x + over_y) - 2 else last
    (r_grad,) = sums(1, after(chunks, *last))
    sides = [after(side, r_grad) for side in sides]
    others = [swap(side, "core", 1) for side in sides]
    at = jnp.stack([lax.axis_index(name) for name in ("x", "core", "tz", "ty")]).astype(jnp.int32)
    n_x = n_dp // n_core
    w_grad = widen(n_x, n_y, share, at, [after(side, r_grad) for side in sides], None)
    flip = at ^ jnp.array([0, 1, 0, 0], jnp.int32)
    w_grad = widen(n_x, n_y, share, flip, others, w_grad)
    return (w_grad, b_grad.reshape(hidden), adm_grad, q_grad, r_grad)


def solution(mesh):
    n_dp, n_table = mesh.devices.shape
    every = ("x", "core", "tz", "ty")
    fine = Mesh(mesh.devices.reshape(n_dp // 2, 2, N_Z, n_table // N_Z), every)
    two, three = P(every, None), P(every, None, None)
    in_specs = (two, P(), P(), two, two, three, two, three, two, three, two)
    out_specs = (P(), P(), two, two, two)
    return jax.shard_map(local, mesh=fine, in_specs=in_specs, out_specs=out_specs, check_vma=False)
```

```python
import functools

import jax
import jax.numpy as jnp
from jax import lax
from jax.experimental import pallas as pl
from jax.experimental.pallas import tpu as pltpu
from jax.sharding import Mesh, PartitionSpec as P

E = 128
ADM_DEV = 128
QROWS_DEV = 4096
N_Z = 4
N_CODE = 8
GROUPS = 4
LOG_ADM = 7
LOG_QROWS = 12
LOG_GROUP = 10
MIB = 1024 * 1024
BF = jnp.bfloat16
F32 = jnp.float32


def iota(shape, dim):
    return lax.broadcasted_iota(jnp.int32, shape, dim)


def dot(a, b, dims=((1,), (0,))):
    return lax.dot_general(a, b, (dims, ((), ())), preferred_element_type=F32)


def one_hot(wanted, row):
    row = jnp.broadcast_to(row, (16, E)).astype(jnp.int16)
    hit = jnp.where(wanted == row[None], jnp.ones((), BF), jnp.zeros((), BF))
    return hit.reshape(wanted.shape[0] * 16, E)


def rows_from(n, base=0):
    return (iota((n, E), 0) + base).astype(jnp.int16).reshape(n // 16, 16, E)


def call(kernel, name, out_shape, flops, traffic, vmem=24, **kwargs):
    return pl.pallas_call(
        kernel,
        out_shape=out_shape,
        compiler_params=pltpu.CompilerParams(vmem_limit_bytes=vmem * MIB),
        cost_estimate=pl.CostEstimate(flops=flops, bytes_accessed=traffic, transcendentals=0),
        name=name,
        **kwargs,
    )


def codes_kernel(n_y, n_table, z_ref, q_ref, r_ref, a_ref, own_ref, near_ref, far_ref):
    y_bits, table_bits = n_y.bit_length() - 1, n_table.bit_length() - 1

    def in_plane(code, bits, z):
        dev = code >> bits
        here = (code >= 0) & (((dev & (n_table - 1)) >> y_bits) == z)
        return jnp.where(here, ((dev >> table_bits) << y_bits) + (dev & (n_y - 1)), -1)

    for k in range(N_Z):
        z = z_ref[0] ^ k
        codes = []
        for ref in (q_ref, r_ref):
            low = ref[...] & (QROWS_DEV - 1)
            codes += [in_plane(ref[...], LOG_QROWS, z), low >> 8, low & 255]
        codes += [in_plane(a_ref[...], LOG_ADM, z), a_ref[...] & (ADM_DEV - 1)]
        block = jnp.concatenate(codes, axis=0).astype(F32).astype(BF)
        if k < 2:
            (own_ref, near_ref)[k][...] = block
        else:
            far_ref[k - 2] = block


def cut_kernel(n_dp, x_ref, out_ref):
    piece = x_ref.shape[1] // (n_dp * N_Z)
    for z in range(N_Z):
        for d in range(n_dp):
            at = (d * N_Z + z) * piece
            out_ref[z, :, d * piece : (d + 1) * piece] = x_ref[:, at : at + piece]


def dpre_kernel(x_ref, w_ref, b_ref, g_ref, out_ref, acc_ref):
    step = pl.program_id(0)
    part = dot(x_ref[...], w_ref[...])

    @pl.when(step == 0)
    def _():
        acc_ref[...] = part

    @pl.when(step > 0)
    def _():
        acc_ref[...] += part

    @pl.when(step == pl.num_programs(0) - 1)
    def _():
        pre = acc_ref[...] + b_ref[...]
        sig = jax.nn.sigmoid(pre)
        out_ref[...] = (g_ref[...].astype(F32) * sig * (1.0 + pre * (1.0 - sig))).astype(BF)


def slots_kernel(n_dest, cap, own_ref, near_ref, far_ref, last_ref, slot_ref, down_ref):
    n_s = own_ref.shape[1]
    n_feat = own_ref.shape[0] // N_CODE
    sample = iota((n_s, n_s), 0)
    earlier = (sample < iota((n_s, n_s), 1)).astype(F32).astype(BF)
    ones = jnp.ones((n_s, n_s), BF)
    count = n_dest * n_feat
    feat_bits = n_feat.bit_length() - 1
    at_row, at_col = iota((count, count), 0), iota((count, count), 1)
    before = ((at_row >> feat_bits == at_col >> feat_bits) & (at_col < at_row)).astype(F32).astype(BF)
    half = n_dest // 2
    for z in range(N_Z):
        codes = (own_ref[...], near_ref[...], far_ref[0], last_ref[...])[z].astype(F32)
        plane = [codes[i * n_feat : (i + 1) * n_feat, :] for i in range(N_CODE)]
        for table in range(2):
            dest = plane[table * 3]
            hits = jnp.concatenate([jnp.where(dest == d, 1.0, 0.0) for d in range(n_dest)], axis=0)
            hits_bf = hits.astype(BF)
            rank = dot(hits_bf, earlier) + dot(before, dot(hits_bf, ones).astype(BF))
            rank = rank * hits
            total = rank[0:n_feat, :]
            for d in range(1, n_dest):
                total = total + rank[d * n_feat : (d + 1) * n_feat, :]
            slot = jnp.where(dest >= 0, dest * cap + total, -1.0)
            slot_ref[table, z, :, :] = slot.astype(jnp.int32)
        dest = plane[6]
        folded = jnp.where(dest >= half, dest - half, dest)
        slot_ref[2, z, :, :] = jnp.where(dest >= 0, folded * ADM_DEV + plane[7], -1.0).astype(jnp.int32)
        down_ref[z] = codes.T


def w_kernel(n_plane, z_ref, x_ref, d0_ref, d1_ref, d2_ref, d3_ref, out_ref):
    wide = x_ref.shape[2]
    share = wide // n_plane
    x = jnp.concatenate([x_ref[z_ref[0] ^ z, :, 0:wide] for z in range(N_Z)], axis=0)
    d = jnp.concatenate([ref[...] for ref in (d0_ref, d1_ref, d2_ref, d3_ref)], axis=0)
    res = dot(x, d, ((0,), (0,))).astype(BF)
    for p in range(n_plane):
        out_ref[p] = res[p * share : (p + 1) * share, :]


def lookup_kernel(d0_ref, d1_ref, d2_ref, d3_ref, w_ref, out_ref, bias_ref, d_ref):
    n_s, depth = d0_ref.shape
    for z, ref in enumerate((d0_ref, d1_ref, d2_ref, d3_ref)):
        d_ref[z * n_s : (z + 1) * n_s, :] = ref[...]
    for step in range(w_ref.shape[0] // (2 * E)):
        res = dot(d_ref[...], w_ref[step * 2 * E : (step + 1) * 2 * E, :], ((1,), (1,))).astype(BF)
        for z in range(N_Z):
            for h in range(2):
                row = (step * 2 + h) * n_s
                out_ref[z, row : row + n_s, :] = res[z * n_s : (z + 1) * n_s, h * E : (h + 1) * E]
    bias = jnp.sum(d_ref[...].astype(F32), axis=0, keepdims=True)
    high = bias.astype(BF)
    low = (bias - high.astype(F32)).astype(BF)
    bias_ref[...] = jnp.concatenate(
        [part[:, i * E : (i + 1) * E].astype(F32) for part in (high, low) for i in range(depth // E)], axis=0
    ).astype(BF)


def bucket_kernel(n_dest, cap, look_ref, slot_ref, down_ref, bias_ref, all_ref, mark_ref, out_ref, sems):
    n_feat, n_s = slot_ref.shape[2:]
    seg = N_Z * cap
    n_mark = -(-seg // E)
    half = n_dest // 2

    slots = n_dest * cap
    wanted = rows_from(slots)
    kind = iota((n_s, E), 1) & 3
    for z in range(N_Z):
        labels = []
        for f in range(n_feat):
            col = [down_ref[z, :, i * n_feat + f : i * n_feat + f + 1] for i in (1, 2, 4, 5)]
            one = jnp.where(kind < 2, jnp.where(kind == 0, col[0], col[1]), jnp.where(kind == 2, col[2], col[3]))
            labels.append(one.astype(BF))
        values = jnp.concatenate([look_ref[z], jnp.concatenate(labels, axis=0)], axis=1)
        for which in range(2):
            hits = [one_hot(wanted, slot_ref[which, z, f : f + 1, :]) for f in range(n_feat)]
            o = dot(jnp.concatenate(hits, axis=1), values)
            for d in range(n_dest):
                rows = o[d * cap : (d + 1) * cap, :]
                out_ref[d, which * seg + z * cap : which * seg + (z + 1) * cap, :] = rows[:, 0:E].astype(BF)
                mark_ref[which, d, z * cap : (z + 1) * cap, :] = rows[:, E : 2 * E]

    tall = half * ADM_DEV
    wanted = rows_from(tall)
    o = jnp.zeros((tall, 2 * E), F32)
    for z in range(N_Z):
        hits = [one_hot(wanted, slot_ref[2, z, f : f + 1, :]) for f in range(n_feat)]
        sides = []
        for f in range(n_feat):
            upper = down_ref[z, :, 6 * n_feat + f : 6 * n_feat + f + 1] >= half
            v = look_ref[z, f * n_s : (f + 1) * n_s, :].astype(F32)
            sides.append(jnp.concatenate([jnp.where(upper, 0.0, v), jnp.where(upper, v, 0.0)], axis=1).astype(BF))
        o = o + dot(jnp.concatenate(hits, axis=1), jnp.concatenate(sides, axis=0))
    for d in range(n_dest):
        at = d % half * ADM_DEV
        side = d // half * E
        out_ref[d, 2 * seg : 2 * seg + ADM_DEV, :] = o[at : at + ADM_DEV, side : side + E].astype(BF)

    at_mark = 2 * seg + ADM_DEV

    lane = iota((seg, E), 1) & 3
    rows = iota((16, E), 0) >> 2
    copies = []
    for d in range(n_dest):
        mixed = jnp.where(lane < 2, mark_ref[0, d], mark_ref[1, d])
        if seg % E:
            mixed = jnp.concatenate([mixed, jnp.zeros((n_mark * E - seg, E), F32)], axis=0)
        marks = jnp.zeros((16, E), F32)
        for j in range(n_mark):
            across = mixed[j * E : (j + 1) * E, :].T
            marks = jnp.where(rows == j, across[0:16, :], marks)
        out_ref[d, at_mark : at_mark + 16, :] = marks.astype(BF)
        out_ref[d, at_mark + 16 : at_mark + 16 + bias_ref.shape[0], :] = bias_ref[...]
        copies.append(pltpu.make_async_copy(out_ref.at[d], all_ref.at[d], sems.at[d]))
        copies[-1].start()
    for copy in copies:
        copy.wait()


def sums_kernel(n_src, seg, n_bias, table, in_ref, *outs):
    n_mark = -(-seg // E)
    at_mark = 2 * seg + ADM_DEV
    if table == 0:
        adm = jnp.zeros((ADM_DEV, E), F32)
        bias = jnp.zeros((2 * n_bias, E), F32)
        for s in range(n_src):
            adm = adm + in_ref[s, 2 * seg : at_mark, :].astype(F32)
            bias = bias + in_ref[s, at_mark + 16 : at_mark + 16 + 2 * n_bias, :].astype(F32)
        outs[1][...] = bias[0:n_bias, :] + bias[n_bias:, :]
        outs[2][...] = adm

    per_group = QROWS_DEV // GROUPS
    labels, sides = [], []
    for s in range(n_src):
        marks = in_ref[s, at_mark : at_mark + 16, :].astype(F32)
        down = jnp.concatenate([marks, jnp.zeros((E - 16, E), F32)], axis=0).T
        for j in range(n_mark):
            at = j * 4 + table * 2
            label = marks[at : at + 1, :] * 256.0 + marks[at + 1 : at + 2, :]
            label = label.astype(jnp.int32) & (per_group - 1)
            if (j + 1) * E > seg:
                label = jnp.where(iota((1, E), 1) + j * E < seg, label, -1)
            labels.append(label)
            group = down[:, at : at + 1].astype(jnp.int32) >> (LOG_GROUP - 8)
            rows = in_ref[s, table * seg + j * E : table * seg + (j + 1) * E, :].astype(F32)
            sides.append(
                jnp.concatenate([jnp.where(group == g, rows, 0.0) for g in range(GROUPS)], axis=1).astype(BF)
            )
    spread = jnp.concatenate(sides, axis=0)
    block = 512
    for b in range(per_group // block):
        wanted = rows_from(block, b * block)
        o = dot(jnp.concatenate([one_hot(wanted, label) for label in labels], axis=1), spread)
        for g in range(GROUPS):
            start = g * per_group + b * block
            outs[0][start : start + block, :] = o[:, g * E : (g + 1) * E]


def doubling(n):
    return [1 << i for i in range(n.bit_length() - 1)]


def swap(x, axis, k):
    n = lax.axis_size(axis)
    return lax.ppermute(x, axis, [(i, i ^ k) for i in range(n)])


def widen_kernel(n_x, n_y, share, at_ref, a_ref, b_ref, *refs):
    out_ref, held_ref, sems = refs[-3:]
    half = a_ref.shape[1]
    copies = []
    for b in range(a_ref.shape[0] // share):
        z = at_ref[2] ^ (((b & 1) << 1) | ((b >> 1) & 1))
        rest = b >> 2
        rows = slice(b * share, (b + 1) * share)
        for side, ref in enumerate((a_ref, b_ref)):
            y, x = (rest % n_y, rest // n_y) if side == 0 else (rest // n_x, rest % n_x)
            row = ((((at_ref[0] ^ x) * 2 + at_ref[1]) * N_Z + z) * n_y + (at_ref[3] ^ y)) * share
            cols = slice(side * half, (side + 1) * half)
            held_ref[rows, cols] = ref[rows, :].astype(F32)
            copy = pltpu.make_async_copy(
                held_ref.at[rows, cols], out_ref.at[pl.ds(pl.multiple_of(row, share), share), cols], sems.at[len(copies)]
            )
            copy.start()
            copies.append(copy)
    for copy in copies:
        copy.wait()


def widen(n_x, n_y, share, at, sides, so_far):
    rows, half = sides[0].shape
    array = pl.BlockSpec(memory_space=pltpu.VMEM)
    more = () if so_far is None else (so_far,)
    alias = {} if so_far is None else {"input_output_aliases": {3: 0}}
    return call(
        functools.partial(widen_kernel, n_x, n_y, share),
        "widen",
        jax.ShapeDtypeStruct((2 * rows, 2 * half), F32),
        rows * half * 2,
        rows * half * 12,
        in_specs=[pl.BlockSpec(memory_space=pltpu.SMEM), array, array] + [pl.BlockSpec(memory_space=pltpu.HBM)] * len(more),
        out_specs=pl.BlockSpec(memory_space=pltpu.HBM),
        scratch_shapes=[
            pltpu.VMEM((rows, 2 * half), F32),
            pltpu.SemaphoreType.DMA((2 * (rows // share),)),
        ],
        vmem=16,
        **alias,
    )(at, *sides, *more)


def after(x, *others):
    return lax.optimization_barrier((x,) + others)[0]


def local(
    features, w_first, b_first, grad_out, admit, owner, adm_row, q_shard, q_local, r_shard, r_local
):
    n_core = lax.axis_size("core")
    n_dp = lax.axis_size("x") * n_core
    n_y = lax.axis_size("ty")
    n_table = N_Z * n_y
    n_dev = n_dp * n_table
    n_plane = n_dp * n_y
    n_s, width = features.shape
    hidden = w_first.shape[1]
    n_feat = width // E
    count = n_s * n_feat
    cap = max(2, 3 * count // (2 * n_dev))
    seg = N_Z * cap
    n_bias = hidden // E
    share = width // n_dev
    wide = width // N_Z
    plane = ("x", "core", "ty")
    shape = jax.ShapeDtypeStruct
    my_z = lax.axis_index("tz").astype(jnp.int32).reshape(1)
    scalar = pl.BlockSpec(memory_space=pltpu.SMEM)
    array = pl.BlockSpec(memory_space=pltpu.VMEM)

    admit, owner, adm_row, q_shard, q_local, r_shard, r_local = [
        a.reshape(n_s, n_feat).T for a in (admit, owner, adm_row, q_shard, q_local, r_shard, r_local)
    ]
    n_code = N_CODE * n_feat
    own_codes, near_codes, far_codes = call(
        functools.partial(codes_kernel, n_y, n_table),
        "codes",
        (shape((n_code, n_s), BF), shape((n_code, n_s), BF), shape((2, n_code, n_s), BF)),
        10**6,
        2 * 10**5,
        in_specs=[scalar] + [array] * 3,
    )(
        my_z,
        jnp.where(admit == 0, q_shard * QROWS_DEV + q_local, -1),
        jnp.where(admit == 0, r_shard * QROWS_DEV + r_local, -1),
        jnp.where(admit == 1, owner * (ADM_DEV * n_table) + adm_row, -1),
    )
    far_codes = swap(far_codes, "tz", 2)
    near_codes = swap(near_codes, "tz", 1)
    last_codes = swap(after(far_codes[1], near_codes), "tz", 1)

    block = width // 4
    dpre = call(
        dpre_kernel,
        "dpre",
        shape((n_s, hidden), BF),
        2 * n_s * width * hidden,
        6 * 10**6,
        grid=(width // block,),
        in_specs=[
            pl.BlockSpec((n_s, block), lambda i: (0, i)),
            pl.BlockSpec((block, hidden), lambda i: (i, 0)),
            pl.BlockSpec((1, hidden), lambda i: (0, 0)),
            pl.BlockSpec((n_s, hidden), lambda i: (0, 0)),
        ],
        out_specs=pl.BlockSpec((n_s, hidden), lambda i: (0, 0)),
        scratch_shapes=[pltpu.VMEM((n_s, hidden), F32)],
        vmem=56,
    )(after(features, own_codes), w_first, b_first.reshape(1, hidden), grad_out)
    dpre = after(dpre, far_codes, near_codes)

    far = swap(dpre, "tz", 2)
    near = swap(dpre, "tz", 1)
    slots, down = call(
        functools.partial(slots_kernel, n_plane, cap),
        "slots",
        (shape((3, N_Z, n_feat, n_s), jnp.int32), shape((N_Z, n_s, n_code), F32)),
        10**9,
        10**6,
        vmem=12,
    )(after(own_codes, dpre), near_codes, far_codes, last_codes)
    far = after(far, near, slots)
    sources = [dpre, near, far, swap(far, "tz", 1)]

    cut = call(
        functools.partial(cut_kernel, n_dp), "cut", shape((N_Z, n_s, wide), BF), 10**6, 2 * 10**6, vmem=8
    )(after(features, dpre))
    feat_in = lax.all_to_all(after(cut, far), "tz", split_axis=0, concat_axis=0, tiled=True)

    look, bias = call(
        lookup_kernel,
        "lookups",
        (shape((N_Z, count, E), BF), shape((2 * n_bias, E), BF)),
        2 * N_Z * n_s * width * hidden,
        7 * 10**6,
        scratch_shapes=[pltpu.VMEM((N_Z * n_s, hidden), BF)],
        vmem=16,
    )(*sources, w_first)
    feat_in = after(feat_in, look)

    w_part = call(
        functools.partial(w_kernel, n_plane),
        "w_part",
        shape((n_plane, share, hidden), BF),
        2 * N_Z * n_s * wide * hidden,
        3 * 10**6,
        in_specs=[scalar] + [array] * 5,
        vmem=12,
    )(my_z, feat_in, *sources)
    look = after(look, w_part)
    w_part = lax.all_to_all(w_part, plane, split_axis=0, concat_axis=0, tiled=True)

    n_rows = 2 * seg + ADM_DEV + 16 + 2 * n_bias
    chunks = call(
        functools.partial(bucket_kernel, n_plane, cap),
        "buckets",
        shape((n_plane, n_rows, E), BF),
        15 * 10**9,
        4 * 10**7,
        out_specs=pl.BlockSpec(memory_space=pltpu.HBM),
        scratch_shapes=[
            pltpu.VMEM((2, n_plane, seg, E), F32),
            pltpu.VMEM((n_plane, n_rows, E), BF),
            pltpu.SemaphoreType.DMA((n_plane,)),
        ],
        vmem=28,
    )(look, slots, down, bias)

    w_part = after(w_part, chunks)
    w_own = jnp.sum(w_part.astype(F32), axis=0).astype(BF)
    chunks = lax.all_to_all(chunks, plane, split_axis=0, concat_axis=0, tiled=True)

    w_two = jnp.concatenate([w_own, swap(w_own, "tz", 2)], axis=0)
    w_four = jnp.concatenate([w_two, swap(w_two, "tz", 1)], axis=0)
    sides = [w_four[:, : hidden // 2], w_four[:, hidden // 2 :]]
    over_y = [("ty", k) for k in doubling(n_y)]
    over_x = [("x", k) for k in doubling(n_dp // n_core)]
    last = sides

    def sums(table, chunks):
        outs = (shape((QROWS_DEV, E), F32), shape((n_bias, E), F32), shape((ADM_DEV, E), F32))
        return call(
            functools.partial(sums_kernel, n_plane, seg, n_bias, table),
            ("q_sums", "r_sums")[table],
            outs if table == 0 else outs[:1],
            4 * 10**9,
            4 * 10**6,
            vmem=28,
        )(chunks)

    for i, steps in enumerate(zip(over_y + over_x, over_x + over_y)):
        moved = [swap(side, *step) for side, step in zip(sides, steps)]
        sides = [jnp.concatenate(pair, axis=0) for pair in zip(sides, moved)]
        last = sides if i == len(over_x + over_y) - 2 else last
    chunks = after(chunks, *last)
    q_grad, b_grad, adm_grad = sums(0, chunks)
    (r_grad,) = sums(1, after(chunks, q_grad))
    sides = [after(side, r_grad) for side in sides]
    others = [swap(side, "core", 1) for side in sides]
    at = jnp.stack([lax.axis_index(name) for name in ("x", "core", "tz", "ty")]).astype(jnp.int32)
    n_x = n_dp // n_core
    w_grad = widen(n_x, n_y, share, at, [after(side, r_grad) for side in sides], None)
    flip = at ^ jnp.array([0, 1, 0, 0], jnp.int32)
    w_grad = widen(n_x, n_y, share, flip, others, w_grad)
    return (w_grad, b_grad.reshape(hidden), adm_grad, q_grad, r_grad)


def solution(mesh):
    n_dp, n_table = mesh.devices.shape
    every = ("x", "core", "tz", "ty")
    fine = Mesh(mesh.devices.reshape(n_dp // 2, 2, N_Z, n_table // N_Z), every)
    two, three = P(every, None), P(every, None, None)
    in_specs = (two, P(), P(), two, two, three, two, three, two, three, two)
    out_specs = (P(), P(), two, two, two)
    return jax.shard_map(local, mesh=fine, in_specs=in_specs, out_specs=out_specs, check_vma=False)
```

```python
import functools

import jax
import jax.numpy as jnp
from jax import lax
from jax.experimental import pallas as pl
from jax.experimental.pallas import tpu as pltpu
from jax.sharding import Mesh, PartitionSpec as P

E = 128
ADM_DEV = 128
QROWS_DEV = 4096
N_Z = 4
N_CODE = 8
GROUPS = 4
LOG_ADM = 7
LOG_QROWS = 12
LOG_GROUP = 10
MIB = 1024 * 1024
BF = jnp.bfloat16
F32 = jnp.float32


def iota(shape, dim):
    return lax.broadcasted_iota(jnp.int32, shape, dim)


def dot(a, b, dims=((1,), (0,))):
    return lax.dot_general(a, b, (dims, ((), ())), preferred_element_type=F32)


def one_hot(wanted, row):
    row = jnp.broadcast_to(row, (16, E)).astype(jnp.int16)
    hit = jnp.where(wanted == row[None], jnp.ones((), BF), jnp.zeros((), BF))
    return hit.reshape(wanted.shape[0] * 16, E)


def rows_from(n, base=0):
    return (iota((n, E), 0) + base).astype(jnp.int16).reshape(n // 16, 16, E)


def call(kernel, name, out_shape, flops, traffic, vmem=24, **kwargs):
    return pl.pallas_call(
        kernel,
        out_shape=out_shape,
        compiler_params=pltpu.CompilerParams(vmem_limit_bytes=vmem * MIB),
        cost_estimate=pl.CostEstimate(flops=flops, bytes_accessed=traffic, transcendentals=0),
        name=name,
        **kwargs,
    )


def codes_kernel(n_y, n_table, z_ref, q_ref, r_ref, a_ref, own_ref, near_ref, far_ref):
    y_bits, table_bits = n_y.bit_length() - 1, n_table.bit_length() - 1

    def in_plane(code, bits, z):
        dev = code >> bits
        here = (code >= 0) & (((dev & (n_table - 1)) >> y_bits) == z)
        return jnp.where(here, ((dev >> table_bits) << y_bits) + (dev & (n_y - 1)), -1)

    for k in range(N_Z):
        z = z_ref[0] ^ k
        codes = []
        for ref in (q_ref, r_ref):
            low = ref[...] & (QROWS_DEV - 1)
            codes += [in_plane(ref[...], LOG_QROWS, z), low >> 8, low & 255]
        codes += [in_plane(a_ref[...], LOG_ADM, z), a_ref[...] & (ADM_DEV - 1)]
        block = jnp.concatenate(codes, axis=0).astype(F32).astype(BF)
        if k < 2:
            (own_ref, near_ref)[k][...] = block
        else:
            far_ref[k - 2] = block


def cut_kernel(n_dp, x_ref, out_ref):
    piece = x_ref.shape[1] // (n_dp * N_Z)
    for z in range(N_Z):
        for d in range(n_dp):
            at = (d * N_Z + z) * piece
            out_ref[z, :, d * piece : (d + 1) * piece] = x_ref[:, at : at + piece]


def dpre_kernel(x_ref, w_ref, b_ref, g_ref, out_ref, acc_ref):
    step = pl.program_id(0)
    part = dot(x_ref[...], w_ref[...])

    @pl.when(step == 0)
    def _():
        acc_ref[...] = part

    @pl.when(step > 0)
    def _():
        acc_ref[...] += part

    @pl.when(step == pl.num_programs(0) - 1)
    def _():
        pre = acc_ref[...] + b_ref[...]
        sig = jax.nn.sigmoid(pre)
        out_ref[...] = (g_ref[...].astype(F32) * sig * (1.0 + pre * (1.0 - sig))).astype(BF)


def slots_kernel(n_dest, cap, own_ref, near_ref, far_ref, last_ref, slot_ref, down_ref):
    n_s = own_ref.shape[1]
    n_feat = own_ref.shape[0] // N_CODE
    sample = iota((n_s, n_s), 0)
    earlier = (sample < iota((n_s, n_s), 1)).astype(F32).astype(BF)
    ones = jnp.ones((n_s, n_s), BF)
    count = n_dest * n_feat
    feat_bits = n_feat.bit_length() - 1
    at_row, at_col = iota((count, count), 0), iota((count, count), 1)
    before = ((at_row >> feat_bits == at_col >> feat_bits) & (at_col < at_row)).astype(F32).astype(BF)
    half = n_dest // 2
    for z in range(N_Z):
        codes = (own_ref[...], near_ref[...], far_ref[0], last_ref[...])[z].astype(F32)
        plane = [codes[i * n_feat : (i + 1) * n_feat, :] for i in range(N_CODE)]
        for table in range(2):
            dest = plane[table * 3]
            hits = jnp.concatenate([jnp.where(dest == d, 1.0, 0.0) for d in range(n_dest)], axis=0)
            hits_bf = hits.astype(BF)
            rank = dot(hits_bf, earlier) + dot(before, dot(hits_bf, ones).astype(BF))
            rank = rank * hits
            total = rank[0:n_feat, :]
            for d in range(1, n_dest):
                total = total + rank[d * n_feat : (d + 1) * n_feat, :]
            slot = jnp.where(dest >= 0, dest * cap + total, -1.0)
            slot_ref[table, z, :, :] = slot.astype(jnp.int32)
        dest = plane[6]
        folded = jnp.where(dest >= half, dest - half, dest)
        slot_ref[2, z, :, :] = jnp.where(dest >= 0, folded * ADM_DEV + plane[7], -1.0).astype(jnp.int32)
        down_ref[z] = codes.T


def w_kernel(n_plane, z_ref, x_ref, d0_ref, d1_ref, d2_ref, d3_ref, out_ref):
    wide = x_ref.shape[2]
    share = wide // n_plane
    x = jnp.concatenate([x_ref[z_ref[0] ^ z, :, 0:wide] for z in range(N_Z)], axis=0)
    d = jnp.concatenate([ref[...] for ref in (d0_ref, d1_ref, d2_ref, d3_ref)], axis=0)
    res = dot(x, d, ((0,), (0,))).astype(BF)
    for p in range(n_plane):
        out_ref[p] = res[p * share : (p + 1) * share, :]


def lookup_kernel(d0_ref, d1_ref, d2_ref, d3_ref, w_ref, out_ref, bias_ref, d_ref):
    n_s, depth = d0_ref.shape
    for z, ref in enumerate((d0_ref, d1_ref, d2_ref, d3_ref)):
        d_ref[z * n_s : (z + 1) * n_s, :] = ref[...]
    for step in range(w_ref.shape[0] // (2 * E)):
        res = dot(d_ref[...], w_ref[step * 2 * E : (step + 1) * 2 * E, :], ((1,), (1,))).astype(BF)
        for z in range(N_Z):
            for h in range(2):
                row = (step * 2 + h) * n_s
                out_ref[z, row : row + n_s, :] = res[z * n_s : (z + 1) * n_s, h * E : (h + 1) * E]
    bias = jnp.sum(d_ref[...].astype(F32), axis=0, keepdims=True)
    high = bias.astype(BF)
    low = (bias - high.astype(F32)).astype(BF)
    bias_ref[...] = jnp.concatenate(
        [part[:, i * E : (i + 1) * E].astype(F32) for part in (high, low) for i in range(depth // E)], axis=0
    ).astype(BF)


def bucket_kernel(n_dest, cap, look_ref, slot_ref, down_ref, bias_ref, all_ref, mark_ref, out_ref, sems):
    n_feat, n_s = slot_ref.shape[2:]
    seg = N_Z * cap
    n_mark = -(-seg // E)
    half = n_dest // 2

    slots = n_dest * cap
    wanted = rows_from(slots)
    kind = iota((n_s, E), 1) & 3
    for z in range(N_Z):
        labels = []
        for f in range(n_feat):
            col = [down_ref[z, :, i * n_feat + f : i * n_feat + f + 1] for i in (1, 2, 4, 5)]
            one = jnp.where(kind < 2, jnp.where(kind == 0, col[0], col[1]), jnp.where(kind == 2, col[2], col[3]))
            labels.append(one.astype(BF))
        values = jnp.concatenate([look_ref[z], jnp.concatenate(labels, axis=0)], axis=1)
        for which in range(2):
            hits = [one_hot(wanted, slot_ref[which, z, f : f + 1, :]) for f in range(n_feat)]
            o = dot(jnp.concatenate(hits, axis=1), values)
            for d in range(n_dest):
                rows = o[d * cap : (d + 1) * cap, :]
                out_ref[d, which * seg + z * cap : which * seg + (z + 1) * cap, :] = rows[:, 0:E].astype(BF)
                mark_ref[which, d, z * cap : (z + 1) * cap, :] = rows[:, E : 2 * E]

    tall = half * ADM_DEV
    wanted = rows_from(tall)
    o = jnp.zeros((tall, 2 * E), F32)
    for z in range(N_Z):
        hits = [one_hot(wanted, slot_ref[2, z, f : f + 1, :]) for f in range(n_feat)]
        sides = []
        for f in range(n_feat):
            upper = down_ref[z, :, 6 * n_feat + f : 6 * n_feat + f + 1] >= half
            v = look_ref[z, f * n_s : (f + 1) * n_s, :].astype(F32)
            sides.append(jnp.concatenate([jnp.where(upper, 0.0, v), jnp.where(upper, v, 0.0)], axis=1).astype(BF))
        o = o + dot(jnp.concatenate(hits, axis=1), jnp.concatenate(sides, axis=0))
    for d in range(n_dest):
        at = d % half * ADM_DEV
        side = d // half * E
        out_ref[d, 2 * seg : 2 * seg + ADM_DEV, :] = o[at : at + ADM_DEV, side : side + E].astype(BF)

    at_mark = 2 * seg + ADM_DEV

    lane = iota((seg, E), 1) & 3
    rows = iota((16, E), 0) >> 2
    copies = []
    for d in range(n_dest):
        mixed = jnp.where(lane < 2, mark_ref[0, d], mark_ref[1, d])
        if seg % E:
            mixed = jnp.concatenate([mixed, jnp.zeros((n_mark * E - seg, E), F32)], axis=0)
        marks = jnp.zeros((16, E), F32)
        for j in range(n_mark):
            across = mixed[j * E : (j + 1) * E, :].T
            marks = jnp.where(rows == j, across[0:16, :], marks)
        out_ref[d, at_mark : at_mark + 16, :] = marks.astype(BF)
        out_ref[d, at_mark + 16 : at_mark + 16 + bias_ref.shape[0], :] = bias_ref[...]
        copies.append(pltpu.make_async_copy(out_ref.at[d], all_ref.at[d], sems.at[d]))
        copies[-1].start()
    for copy in copies:
        copy.wait()


def sums_kernel(n_src, seg, n_bias, table, in_ref, *outs):
    n_mark = -(-seg // E)
    at_mark = 2 * seg + ADM_DEV
    if table == 0:
        adm = jnp.zeros((ADM_DEV, E), F32)
        bias = jnp.zeros((2 * n_bias, E), F32)
        for s in range(n_src):
            adm = adm + in_ref[s, 2 * seg : at_mark, :].astype(F32)
            bias = bias + in_ref[s, at_mark + 16 : at_mark + 16 + 2 * n_bias, :].astype(F32)
        outs[1][...] = bias[0:n_bias, :] + bias[n_bias:, :]
        outs[2][...] = adm

    per_group = QROWS_DEV // GROUPS
    labels, sides = [], []
    for s in range(n_src):
        marks = in_ref[s, at_mark : at_mark + 16, :].astype(F32)
        down = jnp.concatenate([marks, jnp.zeros((E - 16, E), F32)], axis=0).T
        for j in range(n_mark):
            at = j * 4 + table * 2
            label = marks[at : at + 1, :] * 256.0 + marks[at + 1 : at + 2, :]
            label = label.astype(jnp.int32) & (per_group - 1)
            if (j + 1) * E > seg:
                label = jnp.where(iota((1, E), 1) + j * E < seg, label, -1)
            labels.append(label)
            group = down[:, at : at + 1].astype(jnp.int32) >> (LOG_GROUP - 8)
            rows = in_ref[s, table * seg + j * E : table * seg + (j + 1) * E, :].astype(F32)
            sides.append(
                jnp.concatenate([jnp.where(group == g, rows, 0.0) for g in range(GROUPS)], axis=1).astype(BF)
            )
    spread = jnp.concatenate(sides, axis=0)
    block = 512
    for b in range(per_group // block):
        wanted = rows_from(block, b * block)
        o = dot(jnp.concatenate([one_hot(wanted, label) for label in labels], axis=1), spread)
        for g in range(GROUPS):
            start = g * per_group + b * block
            outs[0][start : start + block, :] = o[:, g * E : (g + 1) * E]


def doubling(n):
    return [1 << i for i in range(n.bit_length() - 1)]


def swap(x, axis, k):
    n = lax.axis_size(axis)
    return lax.ppermute(x, axis, [(i, i ^ k) for i in range(n)])


def widen_kernel(n_x, n_y, share, at_ref, *refs):
    n = n_x * n_y
    out_ref, held_ref, sems = refs[-3:]
    half = refs[0].shape[1]
    tall = N_Z * share
    copies = []
    for piece in range(n):
        for side in range(2):
            cols = slice(side * half, (side + 1) * half)
            held_ref[piece * tall : (piece + 1) * tall, cols] = refs[side * n + piece][...].astype(F32)
            x, y = at_ref[0] ^ (piece // n_y), at_ref[3] ^ (piece % n_y)
            for b in range(N_Z):
                z = at_ref[2] ^ (((b & 1) << 1) | (b >> 1))
                row = (((x * 2 + at_ref[1]) * N_Z + z) * n_y + y) * share
                copy = pltpu.make_async_copy(
                    held_ref.at[piece * tall + b * share : piece * tall + (b + 1) * share, cols],
                    out_ref.at[pl.ds(pl.multiple_of(row, share), share), cols],
                    sems.at[len(copies)],
                )
                copy.start()
                copies.append(copy)
    for copy in copies:
        copy.wait()


def widen(n_x, n_y, share, at, pieces, so_far):
    tall, half = pieces[0].shape
    rows = n_x * n_y * tall
    array = pl.BlockSpec(memory_space=pltpu.VMEM)
    more = () if so_far is None else (so_far,)
    alias = {} if so_far is None else {"input_output_aliases": {1 + len(pieces): 0}}
    return call(
        functools.partial(widen_kernel, n_x, n_y, share),
        "widen",
        jax.ShapeDtypeStruct((2 * rows, 2 * half), F32),
        rows * half * 2,
        rows * half * 12,
        in_specs=[pl.BlockSpec(memory_space=pltpu.SMEM)]
        + [array] * len(pieces)
        + [pl.BlockSpec(memory_space=pltpu.HBM)] * len(more),
        out_specs=pl.BlockSpec(memory_space=pltpu.HBM),
        scratch_shapes=[
            pltpu.VMEM((rows, 2 * half), F32),
            pltpu.SemaphoreType.DMA((2 * (rows // share),)),
        ],
        vmem=16,
        **alias,
    )(at, *pieces, *more)


def after(x, *others):
    return lax.optimization_barrier((x,) + others)[0]


def local(
    features, w_first, b_first, grad_out, admit, owner, adm_row, q_shard, q_local, r_shard, r_local
):
    n_core = lax.axis_size("core")
    n_dp = lax.axis_size("x") * n_core
    n_y = lax.axis_size("ty")
    n_table = N_Z * n_y
    n_dev = n_dp * n_table
    n_plane = n_dp * n_y
    n_s, width = features.shape
    hidden = w_first.shape[1]
    n_feat = width // E
    count = n_s * n_feat
    cap = max(2, 3 * count // (2 * n_dev))
    seg = N_Z * cap
    n_bias = hidden // E
    share = width // n_dev
    wide = width // N_Z
    plane = ("x", "core", "ty")
    shape = jax.ShapeDtypeStruct
    my_z = lax.axis_index("tz").astype(jnp.int32).reshape(1)
    scalar = pl.BlockSpec(memory_space=pltpu.SMEM)
    array = pl.BlockSpec(memory_space=pltpu.VMEM)

    admit, owner, adm_row, q_shard, q_local, r_shard, r_local = [
        a.reshape(n_s, n_feat).T for a in (admit, owner, adm_row, q_shard, q_local, r_shard, r_local)
    ]
    n_code = N_CODE * n_feat
    own_codes, near_codes, far_codes = call(
        functools.partial(codes_kernel, n_y, n_table),
        "codes",
        (shape((n_code, n_s), BF), shape((n_code, n_s), BF), shape((2, n_code, n_s), BF)),
        10**6,
        2 * 10**5,
        in_specs=[scalar] + [array] * 3,
    )(
        my_z,
        jnp.where(admit == 0, q_shard * QROWS_DEV + q_local, -1),
        jnp.where(admit == 0, r_shard * QROWS_DEV + r_local, -1),
        jnp.where(admit == 1, owner * (ADM_DEV * n_table) + adm_row, -1),
    )
    far_codes = swap(far_codes, "tz", 2)
    near_codes = swap(near_codes, "tz", 1)
    last_codes = swap(after(far_codes[1], near_codes), "tz", 1)

    block = width // 4
    dpre = call(
        dpre_kernel,
        "dpre",
        shape((n_s, hidden), BF),
        2 * n_s * width * hidden,
        6 * 10**6,
        grid=(width // block,),
        in_specs=[
            pl.BlockSpec((n_s, block), lambda i: (0, i)),
            pl.BlockSpec((block, hidden), lambda i: (i, 0)),
            pl.BlockSpec((1, hidden), lambda i: (0, 0)),
            pl.BlockSpec((n_s, hidden), lambda i: (0, 0)),
        ],
        out_specs=pl.BlockSpec((n_s, hidden), lambda i: (0, 0)),
        scratch_shapes=[pltpu.VMEM((n_s, hidden), F32)],
        vmem=56,
    )(after(features, own_codes), w_first, b_first.reshape(1, hidden), grad_out)
    dpre = after(dpre, far_codes, near_codes)

    far = swap(dpre, "tz", 2)
    near = swap(dpre, "tz", 1)
    slots, down = call(
        functools.partial(slots_kernel, n_plane, cap),
        "slots",
        (shape((3, N_Z, n_feat, n_s), jnp.int32), shape((N_Z, n_s, n_code), F32)),
        10**9,
        10**6,
        vmem=12,
    )(after(own_codes, dpre), near_codes, far_codes, last_codes)
    far = after(far, near, slots)
    sources = [dpre, near, far, swap(far, "tz", 1)]

    cut = call(
        functools.partial(cut_kernel, n_dp), "cut", shape((N_Z, n_s, wide), BF), 10**6, 2 * 10**6, vmem=8
    )(after(features, dpre))
    feat_in = lax.all_to_all(after(cut, far), "tz", split_axis=0, concat_axis=0, tiled=True)

    w_part = call(
        functools.partial(w_kernel, n_plane),
        "w_part",
        shape((n_plane, share, hidden), BF),
        2 * N_Z * n_s * wide * hidden,
        3 * 10**6,
        in_specs=[scalar] + [array] * 5,
        vmem=12,
    )(my_z, feat_in, *sources)
    look, bias = call(
        lookup_kernel,
        "lookups",
        (shape((N_Z, count, E), BF), shape((2 * n_bias, E), BF)),
        2 * N_Z * n_s * width * hidden,
        7 * 10**6,
        scratch_shapes=[pltpu.VMEM((N_Z * n_s, hidden), BF)],
        vmem=16,
    )(*sources[:3], after(sources[3], w_part), w_first)
    w_part = lax.all_to_all(w_part, plane, split_axis=0, concat_axis=0, tiled=True)

    n_rows = 2 * seg + ADM_DEV + 16 + 2 * n_bias
    chunks = call(
        functools.partial(bucket_kernel, n_plane, cap),
        "buckets",
        shape((n_plane, n_rows, E), BF),
        15 * 10**9,
        4 * 10**7,
        out_specs=pl.BlockSpec(memory_space=pltpu.HBM),
        scratch_shapes=[
            pltpu.VMEM((2, n_plane, seg, E), F32),
            pltpu.VMEM((n_plane, n_rows, E), BF),
            pltpu.SemaphoreType.DMA((n_plane,)),
        ],
        vmem=28,
    )(look, slots, down, bias)

    w_part = after(w_part, chunks)
    w_own = jnp.sum(w_part.astype(F32), axis=0).astype(BF)
    chunks = lax.all_to_all(chunks, plane, split_axis=0, concat_axis=0, tiled=True)

    w_far, w_near = swap(w_own, "tz", 2), swap(w_own, "tz", 1)
    w_four = jnp.concatenate([w_own, w_far, w_near, swap(w_far, "tz", 1)], axis=0)
    n_x = n_dp // n_core
    over_y = [("ty", 1, k) for k in doubling(n_y)]
    over_x = [("x", n_y, k) for k in doubling(n_x)]
    side = hidden // 2
    halves = []
    for own, steps in ((w_four[:, :side], over_y + over_x), (w_four[:, side:], over_x + over_y)):
        pieces = {0: own}
        for axis, stride, k in steps:
            pieces.update({key ^ (k * stride): swap(piece, axis, k) for key, piece in pieces.items()})
        halves.append(pieces)
    late = n_x * n_y - 1
    through = [halves[0][n_y - 1], halves[1][late + 1 - n_y]]

    def sums(table, chunks):
        outs = (shape((QROWS_DEV, E), F32), shape((n_bias, E), F32), shape((ADM_DEV, E), F32))
        return call(
            functools.partial(sums_kernel, n_plane, seg, n_bias, table),
            ("q_sums", "r_sums")[table],
            outs if table == 0 else outs[:1],
            4 * 10**9,
            4 * 10**6,
            vmem=28,
        )(chunks)

    chunks = after(chunks, *through)
    q_grad, b_grad, adm_grad = sums(0, chunks)
    others = [{key: swap(piece, "core", 1) for key, piece in pieces.items() if key != late} for pieces in halves]
    early = [piece for other in others for piece in other.values()] + [pieces[late] for pieces in halves]
    (r_grad,) = sums(1, after(chunks, q_grad, *early))
    for pieces, other in zip(halves, others):
        other[late] = after(swap(pieces[late], "core", 1), r_grad)
    at = jnp.stack([lax.axis_index(name) for name in ("x", "core", "tz", "ty")]).astype(jnp.int32)
    order = range(n_x * n_y)
    w_grad = widen(n_x, n_y, share, at, [pieces[i] for pieces in halves for i in order], None)
    flip = at ^ jnp.array([0, 1, 0, 0], jnp.int32)
    w_grad = widen(n_x, n_y, share, flip, [other[i] for other in others for i in order], w_grad)
    return (w_grad, b_grad.reshape(hidden), adm_grad, q_grad, r_grad)


def solution(mesh):
    n_dp, n_table = mesh.devices.shape
    every = ("x", "core", "tz", "ty")
    fine = Mesh(mesh.devices.reshape(n_dp // 2, 2, N_Z, n_table // N_Z), every)
    two, three = P(every, None), P(every, None, None)
    in_specs = (two, P(), P(), two, two, three, two, three, two, three, two)
    out_specs = (P(), P(), two, two, two)
    return jax.shard_map(local, mesh=fine, in_specs=in_specs, out_specs=out_specs, check_vma=False)
```

```python
import functools

import jax
import jax.numpy as jnp
from jax import lax
from jax.experimental import pallas as pl
from jax.experimental.pallas import tpu as pltpu
from jax.sharding import Mesh, PartitionSpec as P

E = 128
ADM_DEV = 128
QROWS_DEV = 4096
N_Z = 4
N_CODE = 8
GROUPS = 4
LOG_ADM = 7
LOG_QROWS = 12
LOG_GROUP = 10
MIB = 1024 * 1024
BF = jnp.bfloat16
F32 = jnp.float32


def iota(shape, dim):
    return lax.broadcasted_iota(jnp.int32, shape, dim)


def dot(a, b, dims=((1,), (0,))):
    return lax.dot_general(a, b, (dims, ((), ())), preferred_element_type=F32)


def one_hot(wanted, row):
    row = jnp.broadcast_to(row, (16, E)).astype(jnp.int16)
    hit = jnp.where(wanted == row[None], jnp.ones((), BF), jnp.zeros((), BF))
    return hit.reshape(wanted.shape[0] * 16, E)


def rows_from(n, base=0):
    return (iota((n, E), 0) + base).astype(jnp.int16).reshape(n // 16, 16, E)


def call(kernel, name, out_shape, flops, traffic, vmem=24, **kwargs):
    return pl.pallas_call(
        kernel,
        out_shape=out_shape,
        compiler_params=pltpu.CompilerParams(vmem_limit_bytes=vmem * MIB),
        cost_estimate=pl.CostEstimate(flops=flops, bytes_accessed=traffic, transcendentals=0),
        name=name,
        **kwargs,
    )


def codes_kernel(n_y, n_table, z_ref, q_ref, r_ref, a_ref, own_ref, near_ref, far_ref):
    y_bits, table_bits = n_y.bit_length() - 1, n_table.bit_length() - 1

    def in_plane(code, bits, z):
        dev = code >> bits
        here = (code >= 0) & (((dev & (n_table - 1)) >> y_bits) == z)
        return jnp.where(here, ((dev >> table_bits) << y_bits) + (dev & (n_y - 1)), -1)

    for k in range(N_Z):
        z = z_ref[0] ^ k
        codes = []
        for ref in (q_ref, r_ref):
            low = ref[...] & (QROWS_DEV - 1)
            codes += [in_plane(ref[...], LOG_QROWS, z), low >> 8, low & 255]
        codes += [in_plane(a_ref[...], LOG_ADM, z), a_ref[...] & (ADM_DEV - 1)]
        block = jnp.concatenate(codes, axis=0).astype(F32).astype(BF)
        if k < 2:
            (own_ref, near_ref)[k][...] = block
        else:
            far_ref[k - 2] = block


def cut_kernel(n_dp, x_ref, out_ref):
    piece = x_ref.shape[1] // (n_dp * N_Z)
    for z in range(N_Z):
        for d in range(n_dp):
            at = (d * N_Z + z) * piece
            out_ref[z, :, d * piece : (d + 1) * piece] = x_ref[:, at : at + piece]


def dpre_kernel(x_ref, w_ref, b_ref, g_ref, out_ref, acc_ref):
    step = pl.program_id(0)
    part = dot(x_ref[...], w_ref[...])

    @pl.when(step == 0)
    def _():
        acc_ref[...] = part

    @pl.when(step > 0)
    def _():
        acc_ref[...] += part

    @pl.when(step == pl.num_programs(0) - 1)
    def _():
        pre = acc_ref[...] + b_ref[...]
        sig = jax.nn.sigmoid(pre)
        out_ref[...] = (g_ref[...].astype(F32) * sig * (1.0 + pre * (1.0 - sig))).astype(BF)


def slots_kernel(n_dest, cap, own_ref, near_ref, far_ref, last_ref, slot_ref, down_ref):
    n_s = own_ref.shape[1]
    n_feat = own_ref.shape[0] // N_CODE
    sample = iota((n_s, n_s), 0)
    earlier = (sample < iota((n_s, n_s), 1)).astype(F32).astype(BF)
    ones = jnp.ones((n_s, n_s), BF)
    count = n_dest * n_feat
    feat_bits = n_feat.bit_length() - 1
    at_row, at_col = iota((count, count), 0), iota((count, count), 1)
    before = ((at_row >> feat_bits == at_col >> feat_bits) & (at_col < at_row)).astype(F32).astype(BF)
    half = n_dest // 2
    for z in range(N_Z):
        codes = (own_ref[...], near_ref[...], far_ref[0], last_ref[...])[z].astype(F32)
        plane = [codes[i * n_feat : (i + 1) * n_feat, :] for i in range(N_CODE)]
        for table in range(2):
            dest = plane[table * 3]
            hits = jnp.concatenate([jnp.where(dest == d, 1.0, 0.0) for d in range(n_dest)], axis=0)
            hits_bf = hits.astype(BF)
            rank = dot(hits_bf, earlier) + dot(before, dot(hits_bf, ones).astype(BF))
            rank = rank * hits
            total = rank[0:n_feat, :]
            for d in range(1, n_dest):
                total = total + rank[d * n_feat : (d + 1) * n_feat, :]
            slot = jnp.where(dest >= 0, dest * cap + total, -1.0)
            slot_ref[table, z, :, :] = slot.astype(jnp.int32)
        dest = plane[6]
        folded = jnp.where(dest >= half, dest - half, dest)
        slot_ref[2, z, :, :] = jnp.where(dest >= 0, folded * ADM_DEV + plane[7], -1.0).astype(jnp.int32)
        down_ref[z] = codes.T


def w_kernel(n_plane, z_ref, x_ref, d0_ref, d1_ref, d2_ref, d3_ref, out_ref):
    wide = x_ref.shape[2]
    share = wide // n_plane
    x = jnp.concatenate([x_ref[z_ref[0] ^ z, :, 0:wide] for z in range(N_Z)], axis=0)
    d = jnp.concatenate([ref[...] for ref in (d0_ref, d1_ref, d2_ref, d3_ref)], axis=0)
    res = dot(x, d, ((0,), (0,))).astype(BF)
    for p in range(n_plane):
        out_ref[p] = res[p * share : (p + 1) * share, :]


def lookup_kernel(d0_ref, d1_ref, d2_ref, d3_ref, w_ref, out_ref, bias_ref, d_ref):
    n_s, depth = d0_ref.shape
    for z, ref in enumerate((d0_ref, d1_ref, d2_ref, d3_ref)):
        d_ref[z * n_s : (z + 1) * n_s, :] = ref[...]
    for step in range(w_ref.shape[0] // (2 * E)):
        res = dot(d_ref[...], w_ref[step * 2 * E : (step + 1) * 2 * E, :], ((1,), (1,))).astype(BF)
        for z in range(N_Z):
            for h in range(2):
                row = (step * 2 + h) * n_s
                out_ref[z, row : row + n_s, :] = res[z * n_s : (z + 1) * n_s, h * E : (h + 1) * E]
    bias = jnp.sum(d_ref[...].astype(F32), axis=0, keepdims=True)
    high = bias.astype(BF)
    low = (bias - high.astype(F32)).astype(BF)
    bias_ref[...] = jnp.concatenate(
        [part[:, i * E : (i + 1) * E].astype(F32) for part in (high, low) for i in range(depth // E)], axis=0
    ).astype(BF)


def bucket_kernel(n_dest, cap, look_ref, slot_ref, down_ref, bias_ref, out_ref, mark_ref):
    n_feat, n_s = slot_ref.shape[2:]
    seg = N_Z * cap
    n_mark = -(-seg // E)
    half = n_dest // 2

    slots = n_dest * cap
    wanted = rows_from(slots)
    kind = iota((n_s, E), 1) & 3
    for z in range(N_Z):
        labels = []
        for f in range(n_feat):
            col = [down_ref[z, :, i * n_feat + f : i * n_feat + f + 1] for i in (1, 2, 4, 5)]
            one = jnp.where(kind < 2, jnp.where(kind == 0, col[0], col[1]), jnp.where(kind == 2, col[2], col[3]))
            labels.append(one.astype(BF))
        values = jnp.concatenate([look_ref[z], jnp.concatenate(labels, axis=0)], axis=1)
        for which in range(2):
            hits = [one_hot(wanted, slot_ref[which, z, f : f + 1, :]) for f in range(n_feat)]
            o = dot(jnp.concatenate(hits, axis=1), values)
            for d in range(n_dest):
                rows = o[d * cap : (d + 1) * cap, :]
                out_ref[d, which * seg + z * cap : which * seg + (z + 1) * cap, :] = rows[:, 0:E].astype(BF)
                mark_ref[which, d, z * cap : (z + 1) * cap, :] = rows[:, E : 2 * E]

    tall = half * ADM_DEV
    wanted = rows_from(tall)
    o = jnp.zeros((tall, 2 * E), F32)
    for z in range(N_Z):
        hits = [one_hot(wanted, slot_ref[2, z, f : f + 1, :]) for f in range(n_feat)]
        sides = []
        for f in range(n_feat):
            upper = down_ref[z, :, 6 * n_feat + f : 6 * n_feat + f + 1] >= half
            v = look_ref[z, f * n_s : (f + 1) * n_s, :].astype(F32)
            sides.append(jnp.concatenate([jnp.where(upper, 0.0, v), jnp.where(upper, v, 0.0)], axis=1).astype(BF))
        o = o + dot(jnp.concatenate(hits, axis=1), jnp.concatenate(sides, axis=0))
    for d in range(n_dest):
        at = d % half * ADM_DEV
        side = d // half * E
        out_ref[d, 2 * seg : 2 * seg + ADM_DEV, :] = o[at : at + ADM_DEV, side : side + E].astype(BF)

    at_mark = 2 * seg + ADM_DEV

    lane = iota((seg, E), 1) & 3
    rows = iota((16, E), 0) >> 2
    for d in range(n_dest):
        mixed = jnp.where(lane < 2, mark_ref[0, d], mark_ref[1, d])
        if seg % E:
            mixed = jnp.concatenate([mixed, jnp.zeros((n_mark * E - seg, E), F32)], axis=0)
        marks = jnp.zeros((16, E), F32)
        for j in range(n_mark):
            across = mixed[j * E : (j + 1) * E, :].T
            marks = jnp.where(rows == j, across[0:16, :], marks)
        out_ref[d, at_mark : at_mark + 16, :] = marks.astype(BF)
        out_ref[d, at_mark + 16 : at_mark + 16 + bias_ref.shape[0], :] = bias_ref[...]


def sums_kernel(n_src, seg, n_bias, table, in_ref, *outs):
    n_mark = -(-seg // E)
    at_mark = 2 * seg + ADM_DEV
    if table == 0:
        adm = jnp.zeros((ADM_DEV, E), F32)
        bias = jnp.zeros((2 * n_bias, E), F32)
        for s in range(n_src):
            adm = adm + in_ref[s, 2 * seg : at_mark, :].astype(F32)
            bias = bias + in_ref[s, at_mark + 16 : at_mark + 16 + 2 * n_bias, :].astype(F32)
        outs[1][...] = bias[0:n_bias, :] + bias[n_bias:, :]
        outs[2][...] = adm

    per_group = QROWS_DEV // GROUPS
    labels, sides = [], []
    for s in range(n_src):
        marks = in_ref[s, at_mark : at_mark + 16, :].astype(F32)
        down = jnp.concatenate([marks, jnp.zeros((E - 16, E), F32)], axis=0).T
        for j in range(n_mark):
            at = j * 4 + table * 2
            label = marks[at : at + 1, :] * 256.0 + marks[at + 1 : at + 2, :]
            label = label.astype(jnp.int32) & (per_group - 1)
            if (j + 1) * E > seg:
                label = jnp.where(iota((1, E), 1) + j * E < seg, label, -1)
            labels.append(label)
            group = down[:, at : at + 1].astype(jnp.int32) >> (LOG_GROUP - 8)
            rows = in_ref[s, table * seg + j * E : table * seg + (j + 1) * E, :].astype(F32)
            sides.append(
                jnp.concatenate([jnp.where(group == g, rows, 0.0) for g in range(GROUPS)], axis=1).astype(BF)
            )
    spread = jnp.concatenate(sides, axis=0)
    block = 512
    for b in range(per_group // block):
        wanted = rows_from(block, b * block)
        o = dot(jnp.concatenate([one_hot(wanted, label) for label in labels], axis=1), spread)
        for g in range(GROUPS):
            start = g * per_group + b * block
            outs[0][start : start + block, :] = o[:, g * E : (g + 1) * E]


def doubling(n):
    return [1 << i for i in range(n.bit_length() - 1)]


def swap(x, axis, k):
    n = lax.axis_size(axis)
    return lax.ppermute(x, axis, [(i, i ^ k) for i in range(n)])


def widen_kernel(n_x, n_y, share, at_ref, *refs):
    n = n_x * n_y
    out_ref, held_ref, sems = refs[-3:]
    half = refs[0].shape[1]
    tall = N_Z * share
    copies = []
    for piece in range(n):
        for side in range(2):
            cols = slice(side * half, (side + 1) * half)
            held_ref[piece * tall : (piece + 1) * tall, cols] = refs[side * n + piece][...].astype(F32)
            x, y = at_ref[0] ^ (piece // n_y), at_ref[3] ^ (piece % n_y)
            for b in range(N_Z):
                z = at_ref[2] ^ (((b & 1) << 1) | (b >> 1))
                row = (((x * 2 + at_ref[1]) * N_Z + z) * n_y + y) * share
                copy = pltpu.make_async_copy(
                    held_ref.at[piece * tall + b * share : piece * tall + (b + 1) * share, cols],
                    out_ref.at[pl.ds(pl.multiple_of(row, share), share), cols],
                    sems.at[len(copies)],
                )
                copy.start()
                copies.append(copy)
    for copy in copies:
        copy.wait()


def widen(n_x, n_y, share, at, pieces, so_far):
    tall, half = pieces[0].shape
    rows = n_x * n_y * tall
    array = pl.BlockSpec(memory_space=pltpu.VMEM)
    more = () if so_far is None else (so_far,)
    alias = {} if so_far is None else {"input_output_aliases": {1 + len(pieces): 0}}
    return call(
        functools.partial(widen_kernel, n_x, n_y, share),
        "widen",
        jax.ShapeDtypeStruct((2 * rows, 2 * half), F32),
        rows * half * 2,
        rows * half * 12,
        in_specs=[pl.BlockSpec(memory_space=pltpu.SMEM)]
        + [array] * len(pieces)
        + [pl.BlockSpec(memory_space=pltpu.HBM)] * len(more),
        out_specs=pl.BlockSpec(memory_space=pltpu.HBM),
        scratch_shapes=[
            pltpu.VMEM((rows, 2 * half), F32),
            pltpu.SemaphoreType.DMA((2 * (rows // share),)),
        ],
        vmem=16,
        **alias,
    )(at, *pieces, *more)


def after(x, *others):
    return lax.optimization_barrier((x,) + others)[0]


def local(
    features, w_first, b_first, grad_out, admit, owner, adm_row, q_shard, q_local, r_shard, r_local
):
    n_core = lax.axis_size("core")
    n_dp = lax.axis_size("x") * n_core
    n_y = lax.axis_size("ty")
    n_table = N_Z * n_y
    n_dev = n_dp * n_table
    n_plane = n_dp * n_y
    n_s, width = features.shape
    hidden = w_first.shape[1]
    n_feat = width // E
    count = n_s * n_feat
    cap = max(2, 3 * count // (2 * n_dev))
    seg = N_Z * cap
    n_bias = hidden // E
    share = width // n_dev
    wide = width // N_Z
    plane = ("x", "core", "ty")
    shape = jax.ShapeDtypeStruct
    my_z = lax.axis_index("tz").astype(jnp.int32).reshape(1)
    scalar = pl.BlockSpec(memory_space=pltpu.SMEM)
    array = pl.BlockSpec(memory_space=pltpu.VMEM)

    block = width // 4
    dpre = call(
        dpre_kernel,
        "dpre",
        shape((n_s, hidden), BF),
        2 * n_s * width * hidden,
        6 * 10**6,
        grid=(width // block,),
        in_specs=[
            pl.BlockSpec((n_s, block), lambda i: (0, i)),
            pl.BlockSpec((block, hidden), lambda i: (i, 0)),
            pl.BlockSpec((1, hidden), lambda i: (0, 0)),
            pl.BlockSpec((n_s, hidden), lambda i: (0, 0)),
        ],
        out_specs=pl.BlockSpec((n_s, hidden), lambda i: (0, 0)),
        scratch_shapes=[pltpu.VMEM((n_s, hidden), F32)],
        vmem=56,
    )(features, w_first, b_first.reshape(1, hidden), grad_out)

    far = swap(dpre, "tz", 2)
    near = swap(dpre, "tz", 1)
    admit, owner, adm_row, q_shard, q_local, r_shard, r_local = [
        a.reshape(n_s, n_feat).T for a in (admit, owner, adm_row, q_shard, q_local, r_shard, r_local)
    ]
    n_code = N_CODE * n_feat
    own_codes, near_codes, far_codes = call(
        functools.partial(codes_kernel, n_y, n_table),
        "codes",
        (shape((n_code, n_s), BF), shape((n_code, n_s), BF), shape((2, n_code, n_s), BF)),
        10**6,
        2 * 10**5,
        in_specs=[scalar] + [array] * 3,
    )(
        after(my_z, dpre),
        jnp.where(admit == 0, q_shard * QROWS_DEV + q_local, -1),
        jnp.where(admit == 0, r_shard * QROWS_DEV + r_local, -1),
        jnp.where(admit == 1, owner * (ADM_DEV * n_table) + adm_row, -1),
    )
    far_codes = swap(far_codes, "tz", 2)
    near_codes = swap(near_codes, "tz", 1)
    last_codes = swap(after(far_codes[1], near_codes), "tz", 1)

    slots, down = call(
        functools.partial(slots_kernel, n_plane, cap),
        "slots",
        (shape((3, N_Z, n_feat, n_s), jnp.int32), shape((N_Z, n_s, n_code), F32)),
        10**9,
        10**6,
        vmem=12,
    )(own_codes, near_codes, far_codes, last_codes)
    far = after(far, near)
    sources = [dpre, near, far, swap(far, "tz", 1)]

    cut = call(
        functools.partial(cut_kernel, n_dp), "cut", shape((N_Z, n_s, wide), BF), 10**6, 2 * 10**6, vmem=8
    )(after(features, dpre))
    feat_in = lax.all_to_all(after(cut, far, far_codes, near_codes), "tz", split_axis=0, concat_axis=0, tiled=True)

    feat_in = after(feat_in, slots)

    w_part = call(
        functools.partial(w_kernel, n_plane),
        "w_part",
        shape((n_plane, share, hidden), BF),
        2 * N_Z * n_s * wide * hidden,
        3 * 10**6,
        in_specs=[scalar] + [array] * 5,
        vmem=12,
    )(my_z, feat_in, *sources)
    look, bias = call(
        lookup_kernel,
        "lookups",
        (shape((N_Z, count, E), BF), shape((2 * n_bias, E), BF)),
        2 * N_Z * n_s * width * hidden,
        7 * 10**6,
        scratch_shapes=[pltpu.VMEM((N_Z * n_s, hidden), BF)],
        vmem=16,
    )(*sources[:3], after(sources[3], w_part), w_first)
    w_part = lax.all_to_all(w_part, plane, split_axis=0, concat_axis=0, tiled=True)

    n_rows = 2 * seg + ADM_DEV + 16 + 2 * n_bias
    chunks = call(
        functools.partial(bucket_kernel, n_plane, cap),
        "buckets",
        shape((n_plane, n_rows, E), BF),
        15 * 10**9,
        4 * 10**7,
        scratch_shapes=[pltpu.VMEM((2, n_plane, seg, E), F32)],
        vmem=28,
    )(look, slots, down, bias)

    w_part = after(w_part, chunks)
    w_own = jnp.sum(w_part.astype(F32), axis=0).astype(BF)
    chunks = lax.all_to_all(chunks, plane, split_axis=0, concat_axis=0, tiled=True)

    w_far, w_near = swap(w_own, "tz", 2), swap(w_own, "tz", 1)
    w_four = jnp.concatenate([w_own, w_far, w_near, swap(w_far, "tz", 1)], axis=0)
    n_x = n_dp // n_core
    over_y = [("ty", 1, k) for k in doubling(n_y)]
    over_x = [("x", n_y, k) for k in doubling(n_x)]
    side = hidden // 2
    def sums(table, chunks):
        outs = (shape((QROWS_DEV, E), F32), shape((n_bias, E), F32), shape((ADM_DEV, E), F32))
        return call(
            functools.partial(sums_kernel, n_plane, seg, n_bias, table),
            ("q_sums", "r_sums")[table],
            outs if table == 0 else outs[:1],
            4 * 10**9,
            4 * 10**6,
            vmem=28,
        )(chunks)

    q_grad, b_grad, adm_grad = sums(0, chunks)
    late = n_x * n_y - 1
    halves, through = [], []
    for own, steps in ((w_four[:, :side], over_y + over_x), (w_four[:, side:], over_x + over_y)):
        pieces = {0: own}
        for axis, stride, k in steps:
            last = late ^ (k * stride)
            if last in pieces:
                pieces[last] = after(pieces[last], q_grad)
            pieces.update({key ^ (k * stride): swap(piece, axis, k) for key, piece in pieces.items()})
        pieces.update({key: after(piece, q_grad) for key, piece in pieces.items() if key not in (0, late)})
        through += [piece for key, piece in pieces.items() if key != late]
        halves.append(pieces)
    (r_grad,) = sums(1, after(chunks, q_grad, *through))
    others = [{key: swap(piece, "core", 1) for key, piece in pieces.items() if key != late} for pieces in halves]
    for pieces, other in zip(halves, others):
        pieces[late] = after(pieces[late], r_grad)
        other[late] = swap(pieces[late], "core", 1)
    at = jnp.stack([lax.axis_index(name) for name in ("x", "core", "tz", "ty")]).astype(jnp.int32)
    order = range(n_x * n_y)
    w_grad = widen(n_x, n_y, share, at, [pieces[i] for pieces in halves for i in order], None)
    flip = at ^ jnp.array([0, 1, 0, 0], jnp.int32)
    w_grad = widen(n_x, n_y, share, flip, [other[i] for other in others for i in order], w_grad)
    return (w_grad, b_grad.reshape(hidden), adm_grad, q_grad, r_grad)


def solution(mesh):
    n_dp, n_table = mesh.devices.shape
    every = ("x", "core", "tz", "ty")
    fine = Mesh(mesh.devices.reshape(n_dp // 2, 2, N_Z, n_table // N_Z), every)
    two, three = P(every, None), P(every, None, None)
    in_specs = (two, P(), P(), two, two, three, two, three, two, three, two)
    out_specs = (P(), P(), two, two, two)
    return jax.shard_map(local, mesh=fine, in_specs=in_specs, out_specs=out_specs, check_vma=False)
```

```python
import functools

import jax
import jax.numpy as jnp
from jax import lax
from jax.experimental import pallas as pl
from jax.experimental.pallas import tpu as pltpu
from jax.sharding import Mesh, PartitionSpec as P

E = 128
ADM_DEV = 128
QROWS_DEV = 4096
N_Z = 4
N_CODE = 8
GROUPS = 4
LOG_ADM = 7
LOG_QROWS = 12
LOG_GROUP = 10
MIB = 1024 * 1024
BF = jnp.bfloat16
F32 = jnp.float32


def iota(shape, dim):
    return lax.broadcasted_iota(jnp.int32, shape, dim)


def dot(a, b, dims=((1,), (0,))):
    return lax.dot_general(a, b, (dims, ((), ())), preferred_element_type=F32)


def one_hot(wanted, row):
    row = jnp.broadcast_to(row, (16, E)).astype(jnp.int16)
    hit = jnp.where(wanted == row[None], jnp.ones((), BF), jnp.zeros((), BF))
    return hit.reshape(wanted.shape[0] * 16, E)


def rows_from(n, base=0):
    return (iota((n, E), 0) + base).astype(jnp.int16).reshape(n // 16, 16, E)


def call(kernel, name, out_shape, flops, traffic, vmem=24, **kwargs):
    return pl.pallas_call(
        kernel,
        out_shape=out_shape,
        compiler_params=pltpu.CompilerParams(vmem_limit_bytes=vmem * MIB),
        cost_estimate=pl.CostEstimate(flops=flops, bytes_accessed=traffic, transcendentals=0),
        name=name,
        **kwargs,
    )


def codes_kernel(n_y, n_table, z_ref, q_ref, r_ref, a_ref, own_ref, near_ref, far_ref):
    y_bits, table_bits = n_y.bit_length() - 1, n_table.bit_length() - 1

    def in_plane(code, bits, z):
        dev = code >> bits
        here = (code >= 0) & (((dev & (n_table - 1)) >> y_bits) == z)
        return jnp.where(here, ((dev >> table_bits) << y_bits) + (dev & (n_y - 1)), -1)

    for k in range(N_Z):
        z = z_ref[0] ^ k
        codes = []
        for ref in (q_ref, r_ref):
            low = ref[...] & (QROWS_DEV - 1)
            codes += [in_plane(ref[...], LOG_QROWS, z), low >> 8, low & 255]
        codes += [in_plane(a_ref[...], LOG_ADM, z), a_ref[...] & (ADM_DEV - 1)]
        block = jnp.concatenate(codes, axis=0).astype(F32).astype(BF)
        if k < 2:
            (own_ref, near_ref)[k][...] = block
        else:
            far_ref[k - 2] = block


def cut_kernel(n_dp, x_ref, out_ref):
    piece = x_ref.shape[1] // (n_dp * N_Z)
    for z in range(N_Z):
        for d in range(n_dp):
            at = (d * N_Z + z) * piece
            out_ref[z, :, d * piece : (d + 1) * piece] = x_ref[:, at : at + piece]


def dpre_kernel(x_ref, w_ref, b_ref, g_ref, out_ref, acc_ref):
    step = pl.program_id(0)
    part = dot(x_ref[...], w_ref[...])

    @pl.when(step == 0)
    def _():
        acc_ref[...] = part

    @pl.when(step > 0)
    def _():
        acc_ref[...] += part

    @pl.when(step == pl.num_programs(0) - 1)
    def _():
        pre = acc_ref[...] + b_ref[...]
        sig = jax.nn.sigmoid(pre)
        out_ref[...] = (g_ref[...].astype(F32) * sig * (1.0 + pre * (1.0 - sig))).astype(BF)


def slots_kernel(n_dest, cap, own_ref, near_ref, far_ref, last_ref, slot_ref, down_ref):
    n_s = own_ref.shape[1]
    n_feat = own_ref.shape[0] // N_CODE
    sample = iota((n_s, n_s), 0)
    earlier = (sample < iota((n_s, n_s), 1)).astype(F32).astype(BF)
    ones = jnp.ones((n_s, n_s), BF)
    count = n_dest * n_feat
    feat_bits = n_feat.bit_length() - 1
    at_row, at_col = iota((count, count), 0), iota((count, count), 1)
    before = ((at_row >> feat_bits == at_col >> feat_bits) & (at_col < at_row)).astype(F32).astype(BF)
    half = n_dest // 2
    for z in range(N_Z):
        codes = (own_ref[...], near_ref[...], far_ref[0], last_ref[...])[z].astype(F32)
        plane = [codes[i * n_feat : (i + 1) * n_feat, :] for i in range(N_CODE)]
        for table in range(2):
            dest = plane[table * 3]
            hits = jnp.concatenate([jnp.where(dest == d, 1.0, 0.0) for d in range(n_dest)], axis=0)
            hits_bf = hits.astype(BF)
            rank = dot(hits_bf, earlier) + dot(before, dot(hits_bf, ones).astype(BF))
            rank = rank * hits
            total = rank[0:n_feat, :]
            for d in range(1, n_dest):
                total = total + rank[d * n_feat : (d + 1) * n_feat, :]
            slot = jnp.where(dest >= 0, dest * cap + total, -1.0)
            slot_ref[table, z, :, :] = slot.astype(jnp.int32)
        dest = plane[6]
        folded = jnp.where(dest >= half, dest - half, dest)
        slot_ref[2, z, :, :] = jnp.where(dest >= 0, folded * ADM_DEV + plane[7], -1.0).astype(jnp.int32)
        down_ref[z] = codes.T


def w_kernel(n_plane, z_ref, x_ref, d0_ref, d1_ref, d2_ref, d3_ref, out_ref):
    wide = x_ref.shape[2]
    share = wide // n_plane
    x = jnp.concatenate([x_ref[z_ref[0] ^ z, :, 0:wide] for z in range(N_Z)], axis=0)
    d = jnp.concatenate([ref[...] for ref in (d0_ref, d1_ref, d2_ref, d3_ref)], axis=0)
    res = dot(x, d, ((0,), (0,))).astype(BF)
    for p in range(n_plane):
        out_ref[p] = res[p * share : (p + 1) * share, :]


def lookup_kernel(d0_ref, d1_ref, d2_ref, d3_ref, w_ref, out_ref, bias_ref, d_ref):
    n_s, depth = d0_ref.shape
    for z, ref in enumerate((d0_ref, d1_ref, d2_ref, d3_ref)):
        d_ref[z * n_s : (z + 1) * n_s, :] = ref[...]
    for step in range(w_ref.shape[0] // (2 * E)):
        res = dot(d_ref[...], w_ref[step * 2 * E : (step + 1) * 2 * E, :], ((1,), (1,))).astype(BF)
        for z in range(N_Z):
            for h in range(2):
                row = (step * 2 + h) * n_s
                out_ref[z, row : row + n_s, :] = res[z * n_s : (z + 1) * n_s, h * E : (h + 1) * E]
    bias = jnp.sum(d_ref[...].astype(F32), axis=0, keepdims=True)
    high = bias.astype(BF)
    low = (bias - high.astype(F32)).astype(BF)
    bias_ref[...] = jnp.concatenate(
        [part[:, i * E : (i + 1) * E].astype(F32) for part in (high, low) for i in range(depth // E)], axis=0
    ).astype(BF)


def bucket_kernel(n_dest, cap, look_ref, slot_ref, down_ref, bias_ref, out_ref, mark_ref):
    n_feat, n_s = slot_ref.shape[2:]
    seg = N_Z * cap
    n_mark = -(-seg // E)
    half = n_dest // 2

    slots = n_dest * cap
    wanted = rows_from(slots)
    kind = iota((n_s, E), 1) & 3
    for z in range(N_Z):
        labels = []
        for f in range(n_feat):
            col = [down_ref[z, :, i * n_feat + f : i * n_feat + f + 1] for i in (1, 2, 4, 5)]
            one = jnp.where(kind < 2, jnp.where(kind == 0, col[0], col[1]), jnp.where(kind == 2, col[2], col[3]))
            labels.append(one.astype(BF))
        values = jnp.concatenate([look_ref[z], jnp.concatenate(labels, axis=0)], axis=1)
        for which in range(2):
            hits = [one_hot(wanted, slot_ref[which, z, f : f + 1, :]) for f in range(n_feat)]
            o = dot(jnp.concatenate(hits, axis=1), values)
            for d in range(n_dest):
                rows = o[d * cap : (d + 1) * cap, :]
                out_ref[d, which * seg + z * cap : which * seg + (z + 1) * cap, :] = rows[:, 0:E].astype(BF)
                mark_ref[which, d, z * cap : (z + 1) * cap, :] = rows[:, E : 2 * E]

    tall = half * ADM_DEV
    wanted = rows_from(tall)
    o = jnp.zeros((tall, 2 * E), F32)
    for z in range(N_Z):
        hits = [one_hot(wanted, slot_ref[2, z, f : f + 1, :]) for f in range(n_feat)]
        sides = []
        for f in range(n_feat):
            upper = down_ref[z, :, 6 * n_feat + f : 6 * n_feat + f + 1] >= half
            v = look_ref[z, f * n_s : (f + 1) * n_s, :].astype(F32)
            sides.append(jnp.concatenate([jnp.where(upper, 0.0, v), jnp.where(upper, v, 0.0)], axis=1).astype(BF))
        o = o + dot(jnp.concatenate(hits, axis=1), jnp.concatenate(sides, axis=0))
    for d in range(n_dest):
        at = d % half * ADM_DEV
        side = d // half * E
        out_ref[d, 2 * seg : 2 * seg + ADM_DEV, :] = o[at : at + ADM_DEV, side : side + E].astype(BF)

    at_mark = 2 * seg + ADM_DEV

    lane = iota((seg, E), 1) & 3
    rows = iota((16, E), 0) >> 2
    for d in range(n_dest):
        mixed = jnp.where(lane < 2, mark_ref[0, d], mark_ref[1, d])
        if seg % E:
            mixed = jnp.concatenate([mixed, jnp.zeros((n_mark * E - seg, E), F32)], axis=0)
        marks = jnp.zeros((16, E), F32)
        for j in range(n_mark):
            across = mixed[j * E : (j + 1) * E, :].T
            marks = jnp.where(rows == j, across[0:16, :], marks)
        out_ref[d, at_mark : at_mark + 16, :] = marks.astype(BF)
        out_ref[d, at_mark + 16 : at_mark + 16 + bias_ref.shape[0], :] = bias_ref[...]


def sums_kernel(n_src, seg, n_bias, table, in_ref, *outs):
    n_mark = -(-seg // E)
    at_mark = 2 * seg + ADM_DEV
    if table == 0:
        adm = jnp.zeros((ADM_DEV, E), F32)
        bias = jnp.zeros((2 * n_bias, E), F32)
        for s in range(n_src):
            adm = adm + in_ref[s, 2 * seg : at_mark, :].astype(F32)
            bias = bias + in_ref[s, at_mark + 16 : at_mark + 16 + 2 * n_bias, :].astype(F32)
        outs[1][...] = bias[0:n_bias, :] + bias[n_bias:, :]
        outs[2][...] = adm

    per_group = QROWS_DEV // GROUPS
    labels, sides = [], []
    for s in range(n_src):
        marks = in_ref[s, at_mark : at_mark + 16, :].astype(F32)
        down = jnp.concatenate([marks, jnp.zeros((E - 16, E), F32)], axis=0).T
        for j in range(n_mark):
            at = j * 4 + table * 2
            label = marks[at : at + 1, :] * 256.0 + marks[at + 1 : at + 2, :]
            label = label.astype(jnp.int32) & (per_group - 1)
            if (j + 1) * E > seg:
                label = jnp.where(iota((1, E), 1) + j * E < seg, label, -1)
            labels.append(label)
            group = down[:, at : at + 1].astype(jnp.int32) >> (LOG_GROUP - 8)
            rows = in_ref[s, table * seg + j * E : table * seg + (j + 1) * E, :].astype(F32)
            sides.append(
                jnp.concatenate([jnp.where(group == g, rows, 0.0) for g in range(GROUPS)], axis=1).astype(BF)
            )
    spread = jnp.concatenate(sides, axis=0)
    block = 512
    for b in range(per_group // block):
        wanted = rows_from(block, b * block)
        o = dot(jnp.concatenate([one_hot(wanted, label) for label in labels], axis=1), spread)
        for g in range(GROUPS):
            start = g * per_group + b * block
            outs[0][start : start + block, :] = o[:, g * E : (g + 1) * E]


def doubling(n):
    return [1 << i for i in range(n.bit_length() - 1)]


def swap(x, axis, k):
    n = lax.axis_size(axis)
    return lax.ppermute(x, axis, [(i, i ^ k) for i in range(n)])


def widen_kernel(n_y, share, places, at_ref, *refs):
    out_ref, held_ref, sems = refs[-3:]
    half = refs[0].shape[1]
    tall = N_Z * share
    copies = []
    for i, (key, side, flip) in enumerate(places):
        held_ref[i * tall : (i + 1) * tall, :] = refs[i][...].astype(F32)
        x, y = at_ref[0] ^ (key // n_y), at_ref[3] ^ (key % n_y)
        for b in range(N_Z):
            z = at_ref[2] ^ (((b & 1) << 1) | (b >> 1))
            row = (((x * 2 + (at_ref[1] ^ flip)) * N_Z + z) * n_y + y) * share
            copy = pltpu.make_async_copy(
                held_ref.at[i * tall + b * share : i * tall + (b + 1) * share, :],
                out_ref.at[pl.ds(pl.multiple_of(row, share), share), side * half : (side + 1) * half],
                sems.at[len(copies)],
            )
            copy.start()
            copies.append(copy)
    for copy in copies:
        copy.wait()


def widen(n_y, share, rows, at, parts, so_far):
    places, pieces = tuple(parts), list(parts.values())
    tall, half = pieces[0].shape
    array = pl.BlockSpec(memory_space=pltpu.VMEM)
    more = () if so_far is None else (so_far,)
    alias = {} if so_far is None else {"input_output_aliases": {1 + len(pieces): 0}}
    return call(
        functools.partial(widen_kernel, n_y, share, places),
        "widen",
        jax.ShapeDtypeStruct((rows, 2 * half), F32),
        len(pieces) * tall * half,
        len(pieces) * tall * half * 6,
        in_specs=[pl.BlockSpec(memory_space=pltpu.SMEM)]
        + [array] * len(pieces)
        + [pl.BlockSpec(memory_space=pltpu.HBM)] * len(more),
        out_specs=pl.BlockSpec(memory_space=pltpu.HBM),
        scratch_shapes=[
            pltpu.VMEM((len(pieces) * tall, half), F32),
            pltpu.SemaphoreType.DMA((len(pieces) * N_Z,)),
        ],
        **alias,
    )(at, *pieces, *more)


def after(x, *others):
    return lax.optimization_barrier((x,) + others)[0]


def local(
    features, w_first, b_first, grad_out, admit, owner, adm_row, q_shard, q_local, r_shard, r_local
):
    n_core = lax.axis_size("core")
    n_dp = lax.axis_size("x") * n_core
    n_y = lax.axis_size("ty")
    n_table = N_Z * n_y
    n_dev = n_dp * n_table
    n_plane = n_dp * n_y
    n_s, width = features.shape
    hidden = w_first.shape[1]
    n_feat = width // E
    count = n_s * n_feat
    cap = max(2, 3 * count // (2 * n_dev))
    seg = N_Z * cap
    n_bias = hidden // E
    share = width // n_dev
    wide = width // N_Z
    plane = ("x", "core", "ty")
    shape = jax.ShapeDtypeStruct
    my_z = lax.axis_index("tz").astype(jnp.int32).reshape(1)
    scalar = pl.BlockSpec(memory_space=pltpu.SMEM)
    array = pl.BlockSpec(memory_space=pltpu.VMEM)

    block = width // 4
    dpre = call(
        dpre_kernel,
        "dpre",
        shape((n_s, hidden), BF),
        2 * n_s * width * hidden,
        6 * 10**6,
        grid=(width // block,),
        in_specs=[
            pl.BlockSpec((n_s, block), lambda i: (0, i)),
            pl.BlockSpec((block, hidden), lambda i: (i, 0)),
            pl.BlockSpec((1, hidden), lambda i: (0, 0)),
            pl.BlockSpec((n_s, hidden), lambda i: (0, 0)),
        ],
        out_specs=pl.BlockSpec((n_s, hidden), lambda i: (0, 0)),
        scratch_shapes=[pltpu.VMEM((n_s, hidden), F32)],
        vmem=56,
    )(features, w_first, b_first.reshape(1, hidden), grad_out)

    far = swap(dpre, "tz", 2)
    near = swap(dpre, "tz", 1)
    admit, owner, adm_row, q_shard, q_local, r_shard, r_local = [
        a.reshape(n_s, n_feat).T for a in (admit, owner, adm_row, q_shard, q_local, r_shard, r_local)
    ]
    n_code = N_CODE * n_feat
    own_codes, near_codes, far_codes = call(
        functools.partial(codes_kernel, n_y, n_table),
        "codes",
        (shape((n_code, n_s), BF), shape((n_code, n_s), BF), shape((2, n_code, n_s), BF)),
        10**6,
        2 * 10**5,
        in_specs=[scalar] + [array] * 3,
    )(
        after(my_z, dpre),
        jnp.where(admit == 0, q_shard * QROWS_DEV + q_local, -1),
        jnp.where(admit == 0, r_shard * QROWS_DEV + r_local, -1),
        jnp.where(admit == 1, owner * (ADM_DEV * n_table) + adm_row, -1),
    )
    far_codes = swap(far_codes, "tz", 2)
    near_codes = swap(near_codes, "tz", 1)
    last_codes = swap(after(far_codes[1], near_codes), "tz", 1)

    slots, down = call(
        functools.partial(slots_kernel, n_plane, cap),
        "slots",
        (shape((3, N_Z, n_feat, n_s), jnp.int32), shape((N_Z, n_s, n_code), F32)),
        10**9,
        10**6,
        vmem=12,
    )(own_codes, near_codes, far_codes, last_codes)
    far = after(far, near)
    sources = [dpre, near, far, swap(far, "tz", 1)]

    cut = call(
        functools.partial(cut_kernel, n_dp), "cut", shape((N_Z, n_s, wide), BF), 10**6, 2 * 10**6, vmem=8
    )(after(features, dpre))
    feat_in = lax.all_to_all(after(cut, far, far_codes, near_codes), "tz", split_axis=0, concat_axis=0, tiled=True)

    feat_in = after(feat_in, slots)

    w_part = call(
        functools.partial(w_kernel, n_plane),
        "w_part",
        shape((n_plane, share, hidden), BF),
        2 * N_Z * n_s * wide * hidden,
        3 * 10**6,
        in_specs=[scalar] + [array] * 5,
        vmem=12,
    )(my_z, feat_in, *sources)
    look, bias = call(
        lookup_kernel,
        "lookups",
        (shape((N_Z, count, E), BF), shape((2 * n_bias, E), BF)),
        2 * N_Z * n_s * width * hidden,
        7 * 10**6,
        scratch_shapes=[pltpu.VMEM((N_Z * n_s, hidden), BF)],
        vmem=16,
    )(*sources[:3], after(sources[3], w_part), w_first)
    w_part = lax.all_to_all(w_part, plane, split_axis=0, concat_axis=0, tiled=True)

    n_rows = 2 * seg + ADM_DEV + 16 + 2 * n_bias
    chunks = call(
        functools.partial(bucket_kernel, n_plane, cap),
        "buckets",
        shape((n_plane, n_rows, E), BF),
        15 * 10**9,
        4 * 10**7,
        scratch_shapes=[pltpu.VMEM((2, n_plane, seg, E), F32)],
        vmem=28,
    )(look, slots, down, bias)

    w_part = after(w_part, chunks)
    w_own = jnp.sum(w_part.astype(F32), axis=0).astype(BF)
    chunks = lax.all_to_all(chunks, plane, split_axis=0, concat_axis=0, tiled=True)

    w_far, w_near = swap(w_own, "tz", 2), swap(w_own, "tz", 1)
    w_four = jnp.concatenate([w_own, w_far, w_near, swap(w_far, "tz", 1)], axis=0)
    n_x = n_dp // n_core
    over_y = [("ty", 1, k) for k in doubling(n_y)]
    over_x = [("x", n_y, k) for k in doubling(n_x)]
    side = hidden // 2
    def sums(table, chunks):
        outs = (shape((QROWS_DEV, E), F32), shape((n_bias, E), F32), shape((ADM_DEV, E), F32))
        return call(
            functools.partial(sums_kernel, n_plane, seg, n_bias, table),
            ("q_sums", "r_sums")[table],
            outs if table == 0 else outs[:1],
            4 * 10**9,
            4 * 10**6,
            vmem=28,
        )(chunks)

    q_grad, b_grad, adm_grad = sums(0, after(chunks, w_four))
    late = n_x * n_y - 1
    (r_grad,) = sums(1, after(chunks, q_grad))
    early, mine, theirs = {}, {}, {}
    for h, steps in enumerate((over_y + over_x, over_x + over_y)):
        own = w_four[:, h * side : (h + 1) * side]
        pieces = {0: own}
        for axis, stride, k in steps:
            last = late ^ (k * stride)
            if last in pieces:
                pieces[last] = after(pieces[last], r_grad)
            pieces.update({key ^ (k * stride): swap(piece, axis, k) for key, piece in pieces.items()})
        mine[late, h, 0] = pieces.pop(late)
        pieces.update({key: after(piece, r_grad) for key, piece in pieces.items() if key > 0})
        early.update({(key, h, 0): piece for key, piece in pieces.items()})
        early.update({(key, h, 1): swap(piece, "core", 1) for key, piece in pieces.items()})
    at = jnp.stack([lax.axis_index(name) for name in ("x", "core", "tz", "ty")]).astype(jnp.int32)
    w_grad = widen(n_y, share, width, at, early, None)
    mine = {key: after(piece, w_grad) for key, piece in mine.items()}
    theirs = {(key, h, 1): swap(piece, "core", 1) for (key, h, _), piece in mine.items()}
    w_grad = widen(n_y, share, width, at, mine, w_grad)
    w_grad = widen(n_y, share, width, at, theirs, w_grad)
    return (w_grad, b_grad.reshape(hidden), adm_grad, q_grad, r_grad)


def solution(mesh):
    n_dp, n_table = mesh.devices.shape
    every = ("x", "core", "tz", "ty")
    fine = Mesh(mesh.devices.reshape(n_dp // 2, 2, N_Z, n_table // N_Z), every)
    two, three = P(every, None), P(every, None, None)
    in_specs = (two, P(), P(), two, two, three, two, three, two, three, two)
    out_specs = (P(), P(), two, two, two)
    return jax.shard_map(local, mesh=fine, in_specs=in_specs, out_specs=out_specs, check_vma=False)
```

```python
import functools

import jax
import jax.numpy as jnp
from jax import lax
from jax.experimental import pallas as pl
from jax.experimental.pallas import tpu as pltpu
from jax.sharding import Mesh, PartitionSpec as P

E = 128
ADM_DEV = 128
QROWS_DEV = 4096
N_Z = 4
N_CODE = 8
GROUPS = 4
LOG_ADM = 7
LOG_QROWS = 12
LOG_GROUP = 10
MIB = 1024 * 1024
BF = jnp.bfloat16
F32 = jnp.float32


def iota(shape, dim):
    return lax.broadcasted_iota(jnp.int32, shape, dim)


def dot(a, b, dims=((1,), (0,))):
    return lax.dot_general(a, b, (dims, ((), ())), preferred_element_type=F32)


def one_hot(wanted, row):
    row = jnp.broadcast_to(row, (16, E)).astype(jnp.int16)
    hit = jnp.where(wanted == row[None], jnp.ones((), BF), jnp.zeros((), BF))
    return hit.reshape(wanted.shape[0] * 16, E)


def rows_from(n, base=0):
    return (iota((n, E), 0) + base).astype(jnp.int16).reshape(n // 16, 16, E)


def call(kernel, name, out_shape, flops, traffic, vmem=24, **kwargs):
    return pl.pallas_call(
        kernel,
        out_shape=out_shape,
        compiler_params=pltpu.CompilerParams(vmem_limit_bytes=vmem * MIB),
        cost_estimate=pl.CostEstimate(flops=flops, bytes_accessed=traffic, transcendentals=0),
        name=name,
        **kwargs,
    )


def codes_kernel(n_y, n_table, z_ref, q_ref, r_ref, a_ref, own_ref, near_ref, far_ref):
    y_bits, table_bits = n_y.bit_length() - 1, n_table.bit_length() - 1

    def in_plane(code, bits, z):
        dev = code >> bits
        here = (code >= 0) & (((dev & (n_table - 1)) >> y_bits) == z)
        return jnp.where(here, ((dev >> table_bits) << y_bits) + (dev & (n_y - 1)), -1)

    for k in range(N_Z):
        z = z_ref[0] ^ k
        codes = []
        for ref in (q_ref, r_ref):
            low = ref[...] & (QROWS_DEV - 1)
            codes += [in_plane(ref[...], LOG_QROWS, z), low >> 8, low & 255]
        codes += [in_plane(a_ref[...], LOG_ADM, z), a_ref[...] & (ADM_DEV - 1)]
        block = jnp.concatenate(codes, axis=0).astype(F32).astype(BF)
        if k < 2:
            (own_ref, near_ref)[k][...] = block
        else:
            far_ref[k - 2] = block


def cut_kernel(n_dp, x_ref, out_ref):
    piece = x_ref.shape[1] // (n_dp * N_Z)
    for z in range(N_Z):
        for d in range(n_dp):
            at = (d * N_Z + z) * piece
            out_ref[z, :, d * piece : (d + 1) * piece] = x_ref[:, at : at + piece]


def dpre_kernel(x_ref, w_ref, b_ref, g_ref, out_ref, acc_ref):
    step = pl.program_id(0)
    part = dot(x_ref[...], w_ref[...])

    @pl.when(step == 0)
    def _():
        acc_ref[...] = part

    @pl.when(step > 0)
    def _():
        acc_ref[...] += part

    @pl.when(step == pl.num_programs(0) - 1)
    def _():
        pre = acc_ref[...] + b_ref[...]
        sig = jax.nn.sigmoid(pre)
        out_ref[...] = (g_ref[...].astype(F32) * sig * (1.0 + pre * (1.0 - sig))).astype(BF)


def slots_kernel(n_dest, cap, own_ref, near_ref, far_ref, last_ref, slot_ref, down_ref):
    n_s = own_ref.shape[1]
    n_feat = own_ref.shape[0] // N_CODE
    sample = iota((n_s, n_s), 0)
    earlier = (sample < iota((n_s, n_s), 1)).astype(F32).astype(BF)
    ones = jnp.ones((n_s, n_s), BF)
    count = n_dest * n_feat
    feat_bits = n_feat.bit_length() - 1
    at_row, at_col = iota((count, count), 0), iota((count, count), 1)
    before = ((at_row >> feat_bits == at_col >> feat_bits) & (at_col < at_row)).astype(F32).astype(BF)
    half = n_dest // 2
    for z in range(N_Z):
        codes = (own_ref[...], near_ref[...], far_ref[0], last_ref[...])[z].astype(F32)
        plane = [codes[i * n_feat : (i + 1) * n_feat, :] for i in range(N_CODE)]
        for table in range(2):
            dest = plane[table * 3]
            hits = jnp.concatenate([jnp.where(dest == d, 1.0, 0.0) for d in range(n_dest)], axis=0)
            hits_bf = hits.astype(BF)
            rank = dot(hits_bf, earlier) + dot(before, dot(hits_bf, ones).astype(BF))
            rank = rank * hits
            total = rank[0:n_feat, :]
            for d in range(1, n_dest):
                total = total + rank[d * n_feat : (d + 1) * n_feat, :]
            slot = jnp.where(dest >= 0, dest * cap + total, -1.0)
            slot_ref[table, z, :, :] = slot.astype(jnp.int32)
        dest = plane[6]
        folded = jnp.where(dest >= half, dest - half, dest)
        slot_ref[2, z, :, :] = jnp.where(dest >= 0, folded * ADM_DEV + plane[7], -1.0).astype(jnp.int32)
        down_ref[z] = codes.T


def w_kernel(n_plane, z_ref, x_ref, d0_ref, d1_ref, d2_ref, d3_ref, out_ref):
    wide = x_ref.shape[2]
    share = wide // n_plane
    x = jnp.concatenate([x_ref[z_ref[0] ^ z, :, 0:wide] for z in range(N_Z)], axis=0)
    d = jnp.concatenate([ref[...] for ref in (d0_ref, d1_ref, d2_ref, d3_ref)], axis=0)
    res = dot(x, d, ((0,), (0,))).astype(BF)
    for p in range(n_plane):
        out_ref[p] = res[p * share : (p + 1) * share, :]


def lookup_kernel(n_src, *refs):
    sources, w_ref, so_far = refs[:n_src], refs[n_src], refs[n_src + 1 : -3]
    out_ref, bias_ref, d_ref = refs[-3:]
    n_s, depth = sources[0].shape
    for z, ref in enumerate(sources):
        d_ref[z * n_s : (z + 1) * n_s, :] = ref[...]
    for step in range(w_ref.shape[0] // (2 * E)):
        res = dot(d_ref[...], w_ref[step * 2 * E : (step + 1) * 2 * E, :], ((1,), (1,))).astype(BF)
        for z in range(n_src):
            for h in range(2):
                row = (step * 2 + h) * n_s
                out_ref[z, row : row + n_s, :] = res[z * n_s : (z + 1) * n_s, h * E : (h + 1) * E]
    bias = jnp.sum(d_ref[...].astype(F32), axis=0, keepdims=True)
    if not so_far:
        bias_ref[...] = bias
        return
    bias = bias + so_far[0][...]
    high = bias.astype(BF)
    low = (bias - high.astype(F32)).astype(BF)
    bias_ref[...] = jnp.concatenate(
        [part[:, i * E : (i + 1) * E].astype(F32) for part in (high, low) for i in range(depth // E)], axis=0
    ).astype(BF)


def bucket_kernel(n_dest, cap, first_ref, last_ref, slot_ref, down_ref, bias_ref, out_ref, mark_ref):
    n_feat, n_s = slot_ref.shape[2:]
    seg = N_Z * cap
    n_mark = -(-seg // E)
    half = n_dest // 2
    look = [first_ref.at[z] for z in range(N_Z - 1)] + [last_ref.at[0]]

    slots = n_dest * cap
    wanted = rows_from(slots)
    kind = iota((n_s, E), 1) & 3
    for z in range(N_Z):
        labels = []
        for f in range(n_feat):
            col = [down_ref[z, :, i * n_feat + f : i * n_feat + f + 1] for i in (1, 2, 4, 5)]
            one = jnp.where(kind < 2, jnp.where(kind == 0, col[0], col[1]), jnp.where(kind == 2, col[2], col[3]))
            labels.append(one.astype(BF))
        values = jnp.concatenate([look[z][...], jnp.concatenate(labels, axis=0)], axis=1)
        for which in range(2):
            hits = [one_hot(wanted, slot_ref[which, z, f : f + 1, :]) for f in range(n_feat)]
            o = dot(jnp.concatenate(hits, axis=1), values)
            for d in range(n_dest):
                rows = o[d * cap : (d + 1) * cap, :]
                out_ref[d, which * seg + z * cap : which * seg + (z + 1) * cap, :] = rows[:, 0:E].astype(BF)
                mark_ref[which, d, z * cap : (z + 1) * cap, :] = rows[:, E : 2 * E]

    tall = half * ADM_DEV
    wanted = rows_from(tall)
    o = jnp.zeros((tall, 2 * E), F32)
    for z in range(N_Z):
        hits = [one_hot(wanted, slot_ref[2, z, f : f + 1, :]) for f in range(n_feat)]
        sides = []
        for f in range(n_feat):
            upper = down_ref[z, :, 6 * n_feat + f : 6 * n_feat + f + 1] >= half
            v = look[z][f * n_s : (f + 1) * n_s, :].astype(F32)
            sides.append(jnp.concatenate([jnp.where(upper, 0.0, v), jnp.where(upper, v, 0.0)], axis=1).astype(BF))
        o = o + dot(jnp.concatenate(hits, axis=1), jnp.concatenate(sides, axis=0))
    for d in range(n_dest):
        at = d % half * ADM_DEV
        side = d // half * E
        out_ref[d, 2 * seg : 2 * seg + ADM_DEV, :] = o[at : at + ADM_DEV, side : side + E].astype(BF)

    at_mark = 2 * seg + ADM_DEV

    lane = iota((seg, E), 1) & 3
    rows = iota((16, E), 0) >> 2
    for d in range(n_dest):
        mixed = jnp.where(lane < 2, mark_ref[0, d], mark_ref[1, d])
        if seg % E:
            mixed = jnp.concatenate([mixed, jnp.zeros((n_mark * E - seg, E), F32)], axis=0)
        marks = jnp.zeros((16, E), F32)
        for j in range(n_mark):
            across = mixed[j * E : (j + 1) * E, :].T
            marks = jnp.where(rows == j, across[0:16, :], marks)
        out_ref[d, at_mark : at_mark + 16, :] = marks.astype(BF)
        out_ref[d, at_mark + 16 : at_mark + 16 + bias_ref.shape[0], :] = bias_ref[...]


def sums_kernel(n_src, seg, n_bias, table, in_ref, *outs):
    n_mark = -(-seg // E)
    at_mark = 2 * seg + ADM_DEV
    if table == 0:
        adm = jnp.zeros((ADM_DEV, E), F32)
        bias = jnp.zeros((2 * n_bias, E), F32)
        for s in range(n_src):
            adm = adm + in_ref[s, 2 * seg : at_mark, :].astype(F32)
            bias = bias + in_ref[s, at_mark + 16 : at_mark + 16 + 2 * n_bias, :].astype(F32)
        outs[1][...] = bias[0:n_bias, :] + bias[n_bias:, :]
        outs[2][...] = adm

    per_group = QROWS_DEV // GROUPS
    labels, sides = [], []
    for s in range(n_src):
        marks = in_ref[s, at_mark : at_mark + 16, :].astype(F32)
        down = jnp.concatenate([marks, jnp.zeros((E - 16, E), F32)], axis=0).T
        for j in range(n_mark):
            at = j * 4 + table * 2
            label = marks[at : at + 1, :] * 256.0 + marks[at + 1 : at + 2, :]
            label = label.astype(jnp.int32) & (per_group - 1)
            if (j + 1) * E > seg:
                label = jnp.where(iota((1, E), 1) + j * E < seg, label, -1)
            labels.append(label)
            group = down[:, at : at + 1].astype(jnp.int32) >> (LOG_GROUP - 8)
            rows = in_ref[s, table * seg + j * E : table * seg + (j + 1) * E, :].astype(F32)
            sides.append(
                jnp.concatenate([jnp.where(group == g, rows, 0.0) for g in range(GROUPS)], axis=1).astype(BF)
            )
    spread = jnp.concatenate(sides, axis=0)
    block = 512
    for b in range(per_group // block):
        wanted = rows_from(block, b * block)
        o = dot(jnp.concatenate([one_hot(wanted, label) for label in labels], axis=1), spread)
        for g in range(GROUPS):
            start = g * per_group + b * block
            outs[0][start : start + block, :] = o[:, g * E : (g + 1) * E]


def doubling(n):
    return [1 << i for i in range(n.bit_length() - 1)]


def swap(x, axis, k):
    n = lax.axis_size(axis)
    return lax.ppermute(x, axis, [(i, i ^ k) for i in range(n)])


def widen_kernel(n_y, share, places, at_ref, *refs):
    out_ref, held_ref, sems = refs[-3:]
    half = refs[0].shape[1]
    tall = N_Z * share
    copies = []
    for i, (key, side, flip) in enumerate(places):
        held_ref[i * tall : (i + 1) * tall, :] = refs[i][...].astype(F32)
        x, y = at_ref[0] ^ (key // n_y), at_ref[3] ^ (key % n_y)
        for b in range(N_Z):
            z = at_ref[2] ^ (((b & 1) << 1) | (b >> 1))
            row = (((x * 2 + (at_ref[1] ^ flip)) * N_Z + z) * n_y + y) * share
            copy = pltpu.make_async_copy(
                held_ref.at[i * tall + b * share : i * tall + (b + 1) * share, :],
                out_ref.at[pl.ds(pl.multiple_of(row, share), share), side * half : (side + 1) * half],
                sems.at[len(copies)],
            )
            copy.start()
            copies.append(copy)
    for copy in copies:
        copy.wait()


def widen(n_y, share, rows, at, parts, so_far):
    places, pieces = tuple(parts), list(parts.values())
    tall, half = pieces[0].shape
    array = pl.BlockSpec(memory_space=pltpu.VMEM)
    more = () if so_far is None else (so_far,)
    alias = {} if so_far is None else {"input_output_aliases": {1 + len(pieces): 0}}
    return call(
        functools.partial(widen_kernel, n_y, share, places),
        "widen",
        jax.ShapeDtypeStruct((rows, 2 * half), F32),
        len(pieces) * tall * half,
        len(pieces) * tall * half * 6,
        in_specs=[pl.BlockSpec(memory_space=pltpu.SMEM)]
        + [array] * len(pieces)
        + [pl.BlockSpec(memory_space=pltpu.HBM)] * len(more),
        out_specs=pl.BlockSpec(memory_space=pltpu.HBM),
        scratch_shapes=[
            pltpu.VMEM((len(pieces) * tall, half), F32),
            pltpu.SemaphoreType.DMA((len(pieces) * N_Z,)),
        ],
        **alias,
    )(at, *pieces, *more)


def after(x, *others):
    return lax.optimization_barrier((x,) + others)[0]


def local(
    features, w_first, b_first, grad_out, admit, owner, adm_row, q_shard, q_local, r_shard, r_local
):
    n_core = lax.axis_size("core")
    n_dp = lax.axis_size("x") * n_core
    n_y = lax.axis_size("ty")
    n_table = N_Z * n_y
    n_dev = n_dp * n_table
    n_plane = n_dp * n_y
    n_s, width = features.shape
    hidden = w_first.shape[1]
    n_feat = width // E
    count = n_s * n_feat
    cap = max(2, 3 * count // (2 * n_dev))
    seg = N_Z * cap
    n_bias = hidden // E
    share = width // n_dev
    wide = width // N_Z
    plane = ("x", "core", "ty")
    shape = jax.ShapeDtypeStruct
    my_z = lax.axis_index("tz").astype(jnp.int32).reshape(1)
    scalar = pl.BlockSpec(memory_space=pltpu.SMEM)
    array = pl.BlockSpec(memory_space=pltpu.VMEM)

    block = width // 4
    dpre = call(
        dpre_kernel,
        "dpre",
        shape((n_s, hidden), BF),
        2 * n_s * width * hidden,
        6 * 10**6,
        grid=(width // block,),
        in_specs=[
            pl.BlockSpec((n_s, block), lambda i: (0, i)),
            pl.BlockSpec((block, hidden), lambda i: (i, 0)),
            pl.BlockSpec((1, hidden), lambda i: (0, 0)),
            pl.BlockSpec((n_s, hidden), lambda i: (0, 0)),
        ],
        out_specs=pl.BlockSpec((n_s, hidden), lambda i: (0, 0)),
        scratch_shapes=[pltpu.VMEM((n_s, hidden), F32)],
        vmem=56,
    )(features, w_first, b_first.reshape(1, hidden), grad_out)

    far = swap(dpre, "tz", 2)
    near = swap(dpre, "tz", 1)
    admit, owner, adm_row, q_shard, q_local, r_shard, r_local = [
        a.reshape(n_s, n_feat).T for a in (admit, owner, adm_row, q_shard, q_local, r_shard, r_local)
    ]
    n_code = N_CODE * n_feat
    own_codes, near_codes, far_codes = call(
        functools.partial(codes_kernel, n_y, n_table),
        "codes",
        (shape((n_code, n_s), BF), shape((n_code, n_s), BF), shape((2, n_code, n_s), BF)),
        10**6,
        2 * 10**5,
        in_specs=[scalar] + [array] * 3,
    )(
        after(my_z, dpre),
        jnp.where(admit == 0, q_shard * QROWS_DEV + q_local, -1),
        jnp.where(admit == 0, r_shard * QROWS_DEV + r_local, -1),
        jnp.where(admit == 1, owner * (ADM_DEV * n_table) + adm_row, -1),
    )
    far_codes = swap(far_codes, "tz", 2)
    near_codes = swap(near_codes, "tz", 1)
    last_codes = swap(after(far_codes[1], near_codes), "tz", 1)

    slots, down = call(
        functools.partial(slots_kernel, n_plane, cap),
        "slots",
        (shape((3, N_Z, n_feat, n_s), jnp.int32), shape((N_Z, n_s, n_code), F32)),
        10**9,
        10**6,
        vmem=12,
    )(own_codes, near_codes, far_codes, last_codes)
    far = after(far, near)
    sources = [dpre, near, far, swap(far, "tz", 1)]

    cut = call(
        functools.partial(cut_kernel, n_dp), "cut", shape((N_Z, n_s, wide), BF), 10**6, 2 * 10**6, vmem=8
    )(after(features, dpre))
    feat_in = lax.all_to_all(after(cut, far, far_codes, near_codes), "tz", split_axis=0, concat_axis=0, tiled=True)

    def lookups(n_src, summed, *args):
        return call(
            functools.partial(lookup_kernel, n_src),
            "lookups",
            (shape((n_src, count, E), BF), summed),
            2 * n_src * n_s * width * hidden,
            7 * 10**6,
            scratch_shapes=[pltpu.VMEM((n_src * n_s, hidden), BF)],
            vmem=16,
        )(*args)

    look, sum_so_far = lookups(3, shape((1, hidden), F32), *sources[:3], w_first)
    sources[3] = after(sources[3], look)
    feat_in = after(feat_in, slots)

    w_part = call(
        functools.partial(w_kernel, n_plane),
        "w_part",
        shape((n_plane, share, hidden), BF),
        2 * N_Z * n_s * wide * hidden,
        3 * 10**6,
        in_specs=[scalar] + [array] * 5,
        vmem=12,
    )(my_z, feat_in, *sources)
    last_look, bias = lookups(1, shape((2 * n_bias, E), BF), after(sources[3], w_part), w_first, sum_so_far)
    w_part = lax.all_to_all(w_part, plane, split_axis=0, concat_axis=0, tiled=True)

    n_rows = 2 * seg + ADM_DEV + 16 + 2 * n_bias
    chunks = call(
        functools.partial(bucket_kernel, n_plane, cap),
        "buckets",
        shape((n_plane, n_rows, E), BF),
        15 * 10**9,
        4 * 10**7,
        scratch_shapes=[pltpu.VMEM((2, n_plane, seg, E), F32)],
        vmem=28,
    )(look, last_look, slots, down, bias)

    w_part = after(w_part, chunks)
    w_own = jnp.sum(w_part.astype(F32), axis=0).astype(BF)
    chunks = lax.all_to_all(chunks, plane, split_axis=0, concat_axis=0, tiled=True)

    w_far, w_near = swap(w_own, "tz", 2), swap(w_own, "tz", 1)
    w_four = jnp.concatenate([w_own, w_far, w_near, swap(w_far, "tz", 1)], axis=0)
    n_x = n_dp // n_core
    over_y = [("ty", 1, k) for k in doubling(n_y)]
    over_x = [("x", n_y, k) for k in doubling(n_x)]
    side = hidden // 2
    def sums(table, chunks):
        outs = (shape((QROWS_DEV, E), F32), shape((n_bias, E), F32), shape((ADM_DEV, E), F32))
        return call(
            functools.partial(sums_kernel, n_plane, seg, n_bias, table),
            ("q_sums", "r_sums")[table],
            outs if table == 0 else outs[:1],
            4 * 10**9,
            4 * 10**6,
            vmem=28,
        )(chunks)

    q_grad, b_grad, adm_grad = sums(0, after(chunks, w_four))
    late = n_x * n_y - 1
    (r_grad,) = sums(1, after(chunks, q_grad))
    early, mine, theirs = {}, {}, {}
    for h, steps in enumerate((over_y + over_x, over_x + over_y)):
        own = w_four[:, h * side : (h + 1) * side]
        pieces = {0: own}
        for axis, stride, k in steps:
            last = late ^ (k * stride)
            if last in pieces:
                pieces[last] = after(pieces[last], r_grad)
            pieces.update({key ^ (k * stride): swap(piece, axis, k) for key, piece in pieces.items()})
        mine[late, h, 0] = pieces.pop(late)
        pieces.update({key: after(piece, r_grad) for key, piece in pieces.items() if key > 0})
        early.update({(key, h, 0): piece for key, piece in pieces.items()})
        early.update({(key, h, 1): swap(piece, "core", 1) for key, piece in pieces.items()})
    at = jnp.stack([lax.axis_index(name) for name in ("x", "core", "tz", "ty")]).astype(jnp.int32)
    w_grad = widen(n_y, share, width, at, early, None)
    mine = {key: after(piece, w_grad) for key, piece in mine.items()}
    theirs = {(key, h, 1): swap(piece, "core", 1) for (key, h, _), piece in mine.items()}
    w_grad = widen(n_y, share, width, at, mine, w_grad)
    w_grad = widen(n_y, share, width, at, theirs, w_grad)
    return (w_grad, b_grad.reshape(hidden), adm_grad, q_grad, r_grad)


def solution(mesh):
    n_dp, n_table = mesh.devices.shape
    every = ("x", "core", "tz", "ty")
    fine = Mesh(mesh.devices.reshape(n_dp // 2, 2, N_Z, n_table // N_Z), every)
    two, three = P(every, None), P(every, None, None)
    in_specs = (two, P(), P(), two, two, three, two, three, two, three, two)
    out_specs = (P(), P(), two, two, two)
    return jax.shard_map(local, mesh=fine, in_specs=in_specs, out_specs=out_specs, check_vma=False)
```
